128 devices in a mesh: ty: 16 (over y, x), tx: 8 (over z, core).
Axes of the slice: x: 4, y: 4, z: 4, core: 2. Of those that a mesh axis runs over, the one named last changes fastest.
Arguments:
- object_field: float32 [2, 8192, 4096], P(None, 'ty', 'tx'), may hold values from -4 to 4
- probe: float32 [2, 256, 256], replicated, may hold values from -5 to 5
- moduli: float32 [1536, 256, 256], P(('ty', 'tx')), may hold values from 0.2 to 2
- positions: int32 [1536, 2], P(('ty', 'tx')), may hold values from 0 to 7936, as said below
- counts: int32 [128], replicated, may hold values from 1 to 12, as said below
Outputs:
- object_out: float32 [2, 8192, 4096], P(None, 'ty', 'tx')
- probe_out: float32 [2, 256, 256], replicated
The draws below stay inside these ranges and needn't reach their ends.
Inputs may be any that keep to these rules, and one draw needn't show every extreme that they name: `positions`: slots i * 12 to (i + 1) * 12 - 1 belong to device i (tile-row-major over the 16 x 4096 / 512 tiles); each holds the corner of a patch that starts inside that device's tile and lies wholly inside the object. `counts`: entry i is the number of leading slots of device i that are in use; some entry equals 12.
All inputs are finite; a program needn't handle non-finite values.
Results may differ from the reference program's by a relative error of at most 0.0001.
Values sent between devices are 32-bit elements; how exact they have to be, the bound alone decides.
A program may use at most 128 MiB of HBM per device.

```python
import math
import jax
import jax.numpy as jnp
from jax import lax

PATCH = 256
TILE = 512
CAP = 12
ITERS = 2
NY = 8192
NX = 4096
SLOTS = 1536
N_TY = 16
N_TX = 8


def draw_positions(key, part):
    key = jax.random.fold_in(key, 9)
    first_key, second_key = jax.random.split(key)
    slot_ids = jnp.arange(SLOTS, dtype=jnp.int32)
    device = slot_ids // CAP
    tile_row = device // N_TX
    tile_col = device % N_TX
    row_starts = jnp.minimum(tile_row * TILE + jax.random.randint(first_key, (SLOTS,), 0, TILE), NY - PATCH)
    col_starts = jnp.minimum(tile_col * TILE + jax.random.randint(second_key, (SLOTS,), 0, TILE), NX - PATCH)
    return jnp.stack([row_starts, col_starts], 1).astype(jnp.int32)


def draw_counts(key, part):
    key = jax.random.fold_in(key, 5)
    keys = jax.random.split(key, 4)
    total_devices = N_TY * N_TX
    device_ids = jnp.arange(total_devices, dtype=jnp.int32)
    tile_row = device_ids // N_TX
    band_shift = jax.random.randint(keys[0], (), 0, N_TY)
    in_band = (tile_row - band_shift) % N_TY < N_TY // 2
    coin_flip = jax.random.randint(keys[1], (total_devices,), 0, 10) < 7
    base_load = 1 + jax.random.randint(keys[2], (total_devices,), 0, CAP // 2)
    loads = base_load + jnp.where(in_band & coin_flip, CAP // 2, 0)
    chosen = jax.random.randint(keys[3], (), 0, total_devices)
    loads = jnp.where(device_ids == chosen, CAP, loads)
    return loads.astype(jnp.int32)


def levels(own_key, extent, shards, least, top_value):
    def one(position, shards_of):
        steps = jax.random.uniform(jax.random.fold_in(jax.random.fold_in(own_key, 6), position), (shards_of,), jnp.float32, least / len(shards), top_value / len(shards))
        return jnp.repeat(jnp.exp(steps), extent[position] // shards_of).reshape((-1,) + (1,) * (len(extent) - position - 1))

    loudness = one(*shards[0])
    for cut in shards[1:]:
        loudness = loudness * one(*cut)
    return loudness


def noise(key, dims, width, reach, shards=(), kind=jnp.bfloat16):
    level = levels(key, dims, shards, -0.22, 0.18) if shards else 1.0
    values = jax.random.normal(key, dims, jnp.float32) * width * level
    return jnp.minimum(jnp.maximum(values, -reach), reach).astype(kind)


def setup_inputs(seed: int = 0) -> dict:
    seeds = jax.random.split(jax.random.key(seed), 6)
    object_field = noise(seeds[0], (2, NY, NX), 0.7, 4.0, ((1, 16), (2, 8)), jnp.float32)
    probe = noise(seeds[1], (2, PATCH, PATCH), 1.0, 5.0, (), jnp.float32)
    moduli = jnp.clip(jnp.exp(math.log(2.0) - 2.3025851 * jax.random.uniform(seeds[2], (SLOTS, PATCH, PATCH), jnp.float32) ** levels(seeds[2], (SLOTS, PATCH, PATCH), ((0, 128),), -0.2, 0.2)), 0.2, 2.0)
    positions = draw_positions(jax.random.fold_in(seeds[5], 71), 0)
    counts = draw_counts(jax.random.fold_in(seeds[5], 71), 0)
    return dict(object_field=object_field, probe=probe, moduli=moduli, positions=positions, counts=counts)


step_object = 1.0
tiny_value = 1e-06
floor_sq = 0.0625

def correct_ref(patch_block, probe_now, modulus, weight):
    probe_c = lax.complex(probe_now[0], probe_now[1])
    patch_c = lax.complex(patch_block[0], patch_block[1])
    wave = jnp.fft.fft2(probe_c * patch_c, norm='ortho')
    scaling = modulus / jnp.sqrt(wave.real * wave.real + wave.imag * wave.imag + floor_sq) - 1.0
    delta = jnp.fft.ifft2(wave * scaling, norm='ortho')
    update = jnp.conj(probe_c) * delta * weight
    numer_term = jnp.conj(patch_c) * delta
    denom_term = patch_block[0] * patch_block[0] + patch_block[1] * patch_block[1]
    return (jnp.stack([update.real, update.imag]), jnp.stack([numer_term.real, numer_term.imag]), denom_term)

def reference(object_field, probe, moduli, positions, counts):
    slots_total = positions.shape[0]
    object_now = object_field
    probe_now = probe
    for iteration in range(ITERS):
        probe_peak = jnp.max(probe_now[0] * probe_now[0] + probe_now[1] * probe_now[1])
        weight = step_object / (probe_peak + tiny_value)

        def visit_slot(slot_id, totals):
            object_sums, probe_numer, probe_denom = totals
            row_start = positions[slot_id, 0].astype(jnp.int32)
            col_start = positions[slot_id, 1].astype(jnp.int32)
            in_use = (slot_id % CAP < counts[slot_id // CAP]).astype(object_now.dtype)
            corner_at = (jnp.int32(0), row_start, col_start)
            patch_block = lax.dynamic_slice(object_now, corner_at, (2, PATCH, PATCH))
            update, numer_term, denom_term = correct_ref(patch_block, probe_now, moduli[slot_id], weight)
            current = lax.dynamic_slice(object_sums, corner_at, (2, PATCH, PATCH))
            object_sums = lax.dynamic_update_slice(object_sums, current + in_use * update, corner_at)
            return (object_sums, probe_numer + in_use * numer_term, probe_denom + in_use * denom_term)
        start_totals = (jnp.zeros_like(object_now), jnp.zeros_like(probe_now), jnp.zeros(probe_now.shape[1:], probe_now.dtype))
        object_sums, probe_numer, probe_denom = lax.fori_loop(0, slots_total, visit_slot, start_totals)
        object_now = object_now + object_sums
        probe_now = probe_now + probe_numer / (probe_denom[None] + tiny_value)
    return (object_now, probe_now)
```

```python
import math

import jax
import jax.numpy as jnp
import ml_dtypes
import numpy as np
from jax import lax
from jax.experimental import pallas as pl
from jax.experimental.pallas import tpu as pltpu
from jax.sharding import PartitionSpec as P

F32 = jnp.float32
BF16 = jnp.bfloat16
MESH = pl.DeviceIdType.MESH

PATCH = 256
HALF = 128
TILE = 512
EXT = 768
CAP = 12
CHUNKS = 4
CHUNK = PATCH // CHUNKS
tiny_value = 1e-06
floor_sq = 0.0625

Z0 = slice(0, 256)
Z1 = slice(256, 512)
Z2 = slice(512, 768)


def dft_tables():
    rows = np.arange(HALF)[:, None]
    cols = np.arange(HALF)[None, :]
    parts = []
    for odd in (0, 1):
        wave = np.exp(-2j * math.pi * ((rows * (2 * cols + odd)) % PATCH) / PATCH) / 16.0
        table = np.block([[wave.real, wave.imag], [-wave.imag, wave.real]])
        for form in (table, table.T):
            high = form.astype(np.float32).astype(ml_dtypes.bfloat16)
            low = (form - high.astype(np.float64)).astype(ml_dtypes.bfloat16)
            parts += [high, low]
    return np.stack(parts)


def order_table():
    table = np.zeros((PATCH, PATCH), np.float32)
    for col in range(PATCH):
        table[2 * (col % HALF) + col // HALF, col] = 1.0
    return np.stack([table.T, table]).astype(ml_dtypes.bfloat16)


def dot(left, right):
    return jnp.dot(left, right, preferred_element_type=F32)


def split(value):
    high = value.astype(BF16)
    return high, (value - high.astype(F32)).astype(BF16)


def thirds(value):
    high = value.astype(BF16)
    rest = value - high.astype(F32)
    middle = rest.astype(BF16)
    return high, middle, (rest - middle.astype(F32)).astype(BF16)


def right_product(value, table, at):
    high, low = split(value)
    return dot(
        jnp.concatenate([high, low, high], 1),
        jnp.concatenate([table[at], table[at], table[at + 1]], 0),
    )


def left_product(table, at, value):
    high, low = split(value)
    return dot(
        jnp.concatenate([table[at], table[at + 1], table[at]], 1),
        jnp.concatenate([high, high, low], 0),
    )


def gather(ref, plane, row, col):
    sub_shift = row % 8
    lane_shift = col % 128
    row_at = pl.multiple_of(row - sub_shift, 8)
    col_at = pl.multiple_of(col - lane_shift, 128)
    lane = lax.broadcasted_iota(jnp.int32, (32, 8, 128), 2)
    sub = lax.broadcasted_iota(jnp.int32, (32, 8, 128), 1)
    cols = []
    for k in range(3):
        block = ref[plane, pl.ds(row_at, 264), pl.ds(col_at + 128 * k, 128)].reshape(33, 8, 128)
        block = pltpu.roll(block, (8 - sub_shift) % 8, 1)
        block = jnp.where(sub < 8 - sub_shift, block[:32], block[1:])
        cols.append(pltpu.roll(block, (128 - lane_shift) % 128, 2))
    parts = [
        jnp.where(lane < 128 - lane_shift, cols[k], cols[k + 1]).reshape(PATCH, 128)
        for k in range(2)
    ]
    return jnp.concatenate(parts, 1)


def scatter_add(ref, plane, row, col, update):
    sub_shift = row % 8
    lane_shift = col % 128
    row_at = pl.multiple_of(row - sub_shift, 8)
    col_at = pl.multiple_of(col - lane_shift, 128)
    lane = lax.broadcasted_iota(jnp.int32, (32, 8, 128), 2)
    sub = lax.broadcasted_iota(jnp.int32, (33, 8, 128), 1)
    first, second = [
        pltpu.roll(update[:, 128 * k : 128 * k + 128].reshape(32, 8, 128), lane_shift, 2)
        for k in range(2)
    ]
    zero = jnp.zeros((32, 8, 128), F32)
    row_of_zeros = jnp.zeros((1, 8, 128), F32)
    right = lane >= lane_shift
    cols = [
        jnp.where(right, first, zero),
        jnp.where(right, second, first),
        jnp.where(right, zero, second),
    ]
    for k in range(3):
        block = pltpu.roll(cols[k], sub_shift, 1)
        block = jnp.where(
            sub >= sub_shift,
            jnp.concatenate([block, row_of_zeros], 0),
            jnp.concatenate([row_of_zeros, block], 0),
        )
        ref[plane, pl.ds(row_at, 264), pl.ds(col_at + 128 * k, 128)] += block.reshape(264, 128)


def scaled(wave, modulus):
    real = wave[:HALF]
    imag = wave[HALF:]
    scale = modulus * lax.rsqrt(real * real + imag * imag + floor_sq) - 1.0
    return jnp.concatenate([real * scale, imag * scale], 0)


def visit(slot, offsets, extended, probe, weighted, moduli, table, sums, totals):
    row = offsets[slot, 0]
    col = offsets[slot, 1]
    patch_real = gather(extended, 0, row, col)
    patch_imag = gather(extended, 1, row, col)
    totals[2] += patch_real * patch_real + patch_imag * patch_imag
    exit_real = probe[0] * patch_real - probe[1] * patch_imag
    exit_imag = probe[0] * patch_imag + probe[1] * patch_real
    even = jnp.concatenate(
        [exit_real[:, :HALF] + exit_real[:, HALF:], exit_imag[:, :HALF] + exit_imag[:, HALF:]], 1
    )
    odd = jnp.concatenate(
        [exit_real[:, :HALF] - exit_real[:, HALF:], exit_imag[:, :HALF] - exit_imag[:, HALF:]], 1
    )
    even = right_product(even, table, 0)
    odd = right_product(odd, table, 4)
    real = jnp.concatenate([even[:, :HALF], odd[:, :HALF]], 1)
    imag = jnp.concatenate([even[:, HALF:], odd[:, HALF:]], 1)
    even = jnp.concatenate([real[:HALF] + real[HALF:], imag[:HALF] + imag[HALF:]], 0)
    odd = jnp.concatenate([real[:HALF] - real[HALF:], imag[:HALF] - imag[HALF:]], 0)
    even = scaled(left_product(table, 2, even), moduli[slot, :HALF])
    odd = scaled(left_product(table, 6, odd), moduli[slot, HALF:])
    even = left_product(table, 0, even)
    odd = left_product(table, 4, odd)
    real = jnp.concatenate([even[:HALF] + odd[:HALF], even[:HALF] - odd[:HALF]], 0)
    imag = jnp.concatenate([even[HALF:] + odd[HALF:], even[HALF:] - odd[HALF:]], 0)
    even = right_product(jnp.concatenate([real[:, :HALF], imag[:, :HALF]], 1), table, 2)
    odd = right_product(jnp.concatenate([real[:, HALF:], imag[:, HALF:]], 1), table, 6)
    delta_real = jnp.concatenate(
        [even[:, :HALF] + odd[:, :HALF], even[:, :HALF] - odd[:, :HALF]], 1
    )
    delta_imag = jnp.concatenate(
        [even[:, HALF:] + odd[:, HALF:], even[:, HALF:] - odd[:, HALF:]], 1
    )
    totals[0] += patch_real * delta_real + patch_imag * delta_imag
    totals[1] += patch_real * delta_imag - patch_imag * delta_real
    scatter_add(sums, 0, row, col, weighted[0] * delta_real + weighted[1] * delta_imag)
    scatter_add(sums, 1, row, col, weighted[0] * delta_imag - weighted[1] * delta_real)


def slots_kernel(count, offsets, extended, probe, moduli, table, sums, totals, weighted):
    peak = jnp.max(probe[0] * probe[0] + probe[1] * probe[1])
    weighted[...] = probe[...] * (1.0 / (peak + tiny_value))
    sums[...] = jnp.zeros_like(sums)
    totals[...] = jnp.zeros_like(totals)

    def step(slot, carry):
        visit(slot, offsets, extended, probe, weighted, moduli, table, sums, totals)
        return carry

    lax.fori_loop(0, count[0], step, 0)


VMEM = pl.BlockSpec(memory_space=pltpu.VMEM)
SMEM = pl.BlockSpec(memory_space=pltpu.SMEM)


def run_slots(count, offsets, extended, probe, moduli, table):
    return pl.pallas_call(
        slots_kernel,
        out_shape=(
            jax.ShapeDtypeStruct((2, EXT, EXT), F32),
            jax.ShapeDtypeStruct((3, PATCH, PATCH), F32),
        ),
        in_specs=[SMEM, SMEM, VMEM, VMEM, VMEM, VMEM],
        out_specs=(VMEM, VMEM),
        scratch_shapes=[pltpu.VMEM((2, PATCH, PATCH), F32)],
        compiler_params=pltpu.CompilerParams(vmem_limit_bytes=56 * 2**20),
        cost_estimate=pl.CostEstimate(
            flops=6 * 10**9, bytes_accessed=14 * 10**6, transcendentals=0
        ),
    )(count, offsets, extended, probe, moduli, table)


class Place:
    def __init__(self):
        ty = lax.axis_index("ty")
        tx = lax.axis_index("tx")
        self.ty, self.tx = ty, tx
        self.y, self.x = ty // 4, ty % 4
        self.z, self.core = tx // 2, tx % 2
        self.up = ((ty + 15) % 16, tx)
        self.down = ((ty + 1) % 16, tx)
        self.left = (ty, (tx + 7) % 8)
        self.right = (ty, (tx + 1) % 8)
        self.other = (ty, self.z * 2 + 1 - self.core)

    def along_y(self, step):
        return (((self.y + step) % 4) * 4 + self.x, self.tx)

    def along_x(self, step):
        return (self.y * 4 + (self.x + step) % 4, self.tx)

    def along_z(self, step):
        return (self.ty, ((self.z + step) % 4) * 2 + self.core)


def greet(devices):
    barrier = pltpu.get_barrier_semaphore()
    for device in devices:
        pl.semaphore_signal(barrier, inc=1, device_id=device, device_id_type=MESH)
    pl.semaphore_wait(barrier, len(devices))


class Copies:
    def __init__(self, send, receive):
        self.send, self.receive, self.used = send, receive, 0

    def start(self, source, target, device):
        copy = pltpu.make_async_remote_copy(
            src_ref=source,
            dst_ref=target,
            send_sem=self.send.at[self.used],
            recv_sem=self.receive.at[self.used],
            device_id=device,
            device_id_type=MESH,
        )
        self.used += 1
        copy.start()
        return copy


def rows_of(zone, chunk):
    return slice(zone.start + chunk * CHUNK, zone.start + (chunk + 1) * CHUNK)


def extend_kernel(tile, moduli, order, extended, ordered, send, receive):
    here = Place()
    copies = Copies(send, receive)
    greet([here.up, here.down, here.left, here.right])
    above = []
    for chunk in range(CHUNKS):
        above.append(
            copies.start(
                tile.at[:, rows_of(Z0, chunk), Z0], extended.at[:, rows_of(Z2, chunk), Z0], here.up
            )
        )
    beside = [copies.start(tile.at[:, :, Z0], extended.at[:, 0:TILE, Z2], here.left)]
    beside.append(copies.start(tile.at[:, Z0, Z1], extended.at[:, Z2, Z1], here.up))
    extended[:, 0:TILE, 0:TILE] = tile[...]

    def reorder(slot, carry):
        block = moduli[slot]
        block = sum(dot(order[0], part) for part in thirds(block))
        ordered[slot] = sum(dot(part, order[1]) for part in thirds(block))
        return carry

    lax.fori_loop(0, CAP, reorder, 0)
    for chunk in range(CHUNKS):
        above[chunk].wait_recv()
        beside.append(
            copies.start(
                extended.at[:, rows_of(Z2, chunk), Z0],
                extended.at[:, rows_of(Z2, chunk), Z2],
                here.left,
            )
        )
    for copy in above:
        copy.wait_send()
    for copy in beside:
        copy.wait()


def extend(tile, moduli, order):
    copies = 2 * CHUNKS + 2
    return pl.pallas_call(
        extend_kernel,
        out_shape=(
            jax.ShapeDtypeStruct((2, EXT, EXT), F32),
            jax.ShapeDtypeStruct((CAP, PATCH, PATCH), F32),
        ),
        in_specs=[VMEM] * 3,
        out_specs=(VMEM, VMEM),
        scratch_shapes=[pltpu.SemaphoreType.DMA((copies,)), pltpu.SemaphoreType.DMA((copies,))],
        compiler_params=pltpu.CompilerParams(
            vmem_limit_bytes=48 * 2**20, collective_id=0, has_side_effects=True
        ),
        cost_estimate=pl.CostEstimate(
            flops=10**9, bytes_accessed=14 * 10**6, transcendentals=0
        ),
    )(tile, moduli, order)


class Reduction:
    def __init__(self, here, copies, totals, probe, probe_out, landed, held):
        self.here, self.copies = here, copies
        self.totals, self.probe, self.probe_out = totals, probe, probe_out
        self.land_core, self.land_y, self.land_x, self.land_z = landed
        self.held_core, self.held_y, self.held_x = held
        self.in_flight = []
        self.sent = []

    def launch(self, source, target, device):
        self.in_flight.append(self.copies.start(source, target, device))

    def arrive(self):
        for copy in self.in_flight:
            copy.wait_recv()
        self.sent += self.in_flight
        self.in_flight = []

    def start(self):
        half = pl.ds(pl.multiple_of((1 - self.here.core) * HALF, HALF), HALF)
        self.launch(self.totals.at[:, half, :], self.land_core, self.here.other)

    def after_core(self):
        self.arrive()
        half = pl.ds(pl.multiple_of(self.here.core * HALF, HALF), HALF)
        self.held_core[...] = self.totals[:, half, :] + self.land_core[...]
        for step in range(1, 4):
            part = pl.ds(pl.multiple_of(((self.here.y + step) % 4) * 32, 32), 32)
            self.launch(
                self.held_core.at[:, part, :], self.land_y.at[step - 1], self.here.along_y(step)
            )

    def after_y(self):
        self.arrive()
        part = pl.ds(pl.multiple_of(self.here.y * 32, 32), 32)
        self.held_y[...] = (self.held_core[:, part, :] + self.land_y[0]) + (
            self.land_y[1] + self.land_y[2]
        )
        for step in range(1, 4):
            part = pl.ds(pl.multiple_of(((self.here.x + step) % 4) * 8, 8), 8)
            self.launch(
                self.held_y.at[:, part, :], self.land_x.at[step - 1], self.here.along_x(step)
            )

    def after_x(self):
        self.arrive()
        part = pl.ds(pl.multiple_of(self.here.x * 8, 8), 8)
        self.held_x[...] = (self.held_y[:, part, :] + self.land_x[0]) + (
            self.land_x[1] + self.land_x[2]
        )
        for step in range(1, 4):
            self.launch(self.held_x, self.land_z.at[self.here.z], self.here.along_z(step))
        self.land_z[self.here.z] = self.held_x[...]

    def share(self, rows):
        start = self.here.core * HALF
        if rows < 128:
            start = start + self.here.y * 32
        if rows < 32:
            start = start + self.here.x * 8
        part = pl.ds(pl.multiple_of(start, rows), rows)
        return self.probe_out.at[:, part, :]

    def after_z(self):
        self.arrive()
        total = (self.land_z[0] + self.land_z[1]) + (self.land_z[2] + self.land_z[3])
        start = self.here.core * HALF + self.here.y * 32 + self.here.x * 8
        part = pl.ds(pl.multiple_of(start, 8), 8)
        self.probe_out[:, part, :] = self.probe[:, part, :] + total[0:2] / (
            total[2:3] + tiny_value
        )
        for step in range(1, 4):
            self.launch(self.share(8), self.share(8), self.here.along_x(step))

    def gather_x(self):
        self.arrive()
        for step in range(1, 4):
            self.launch(self.share(32), self.share(32), self.here.along_y(step))

    def gather_y(self):
        self.arrive()
        self.launch(self.share(128), self.share(128), self.here.other)

    def finish(self):
        self.arrive()
        for copy in self.sent:
            copy.wait_send()


REDUCTION_COPIES = 1 + 3 + 3 + 3 + 3 + 3 + 1


def everyone(here):
    devices = [here.up, here.down, here.left, here.right, here.other]
    for step in range(1, 4):
        devices += [here.along_y(step), here.along_x(step), here.along_z(step)]
    return devices


def exchange_kernel(
    sums, extended, totals, probe, out, probe_out,
    from_left, from_up, from_down, from_right, top, bottom,
    land_core, land_y, land_x, land_z, held_core, held_y, held_x,
    send, receive,
):
    here = Place()
    copies = Copies(send, receive)
    reduction = Reduction(
        here, copies, totals, probe, probe_out,
        (land_core, land_y, land_x, land_z), (held_core, held_y, held_x),
    )
    greet(everyone(here))
    rest = []
    reduction.start()
    left_bottom, left_top = [], []
    for chunk in range(CHUNKS):
        for zone, kept in ((Z2, left_bottom), (Z0, left_top)):
            rows = rows_of(zone, chunk)
            kept.append(copies.start(sums.at[:, rows, Z2], from_left.at[:, rows, :], here.right))
    middle_down = copies.start(sums.at[:, Z2, Z1], from_up.at[:, :, Z1], here.down)
    middle_up = copies.start(sums.at[:, Z0, Z1], from_down.at[:, :, Z1], here.up)
    side_left = copies.start(sums.at[:, Z1, Z0], from_right, here.left)
    side_right = copies.start(sums.at[:, Z1, Z2], from_left.at[:, Z1, :], here.right)
    reduction.after_core()
    out[:, Z1, Z1] = extended[:, Z1, Z1] + sums[:, Z1, Z1]
    reduction.after_y()
    outer = []
    for chunk in range(CHUNKS):
        rows = rows_of(Z0, chunk)
        low = rows_of(Z2, chunk)
        left_bottom[chunk].wait_recv()
        bottom[:, rows, :] = sums[:, low, Z0] + from_left[:, low, :]
        down = copies.start(bottom.at[:, rows, :], from_up.at[:, rows, Z0], here.down)
        left_top[chunk].wait_recv()
        top[:, rows, :] = sums[:, rows, Z0] + from_left[:, rows, :]
        up = copies.start(top.at[:, rows, :], from_down.at[:, rows, Z0], here.up)
        outer.append((down, up))
    reduction.after_x()
    side_left.wait_recv()
    out[:, Z1, Z2] = extended[:, Z1, Z2] + (sums[:, Z1, Z2] + from_right[...])
    middle_down.wait_recv()
    out[:, Z0, Z1] = extended[:, Z0, Z1] + (sums[:, Z0, Z1] + from_up[:, :, Z1])
    middle_up.wait_recv()
    out[:, Z2, Z1] = extended[:, Z2, Z1] + (sums[:, Z2, Z1] + from_down[:, :, Z1])
    reduction.after_z()
    side_right.wait_recv()
    out[:, Z1, Z0] = extended[:, Z1, Z0] + (sums[:, Z1, Z0] + from_left[:, Z1, :])
    reduction.gather_x()
    last = []
    for chunk in range(CHUNKS):
        rows = rows_of(Z0, chunk)
        low = rows_of(Z2, chunk)
        down, up = outer[chunk]
        down.wait_recv()
        out[:, rows, Z0] = extended[:, rows, Z0] + (top[:, rows, :] + from_up[:, rows, Z0])
        last.append(copies.start(out.at[:, rows, Z0], out.at[:, rows, Z2], here.left))
        up.wait_recv()
        out[:, low, Z0] = extended[:, low, Z0] + (bottom[:, rows, :] + from_down[:, rows, Z0])
        last.append(copies.start(out.at[:, low, Z0], out.at[:, low, Z2], here.left))
        if chunk == 1:
            reduction.gather_y()
    reduction.finish()
    for copy in left_bottom + left_top + [middle_down, middle_up, side_left, side_right]:
        copy.wait_send()
    for down, up in outer:
        down.wait_send()
        up.wait_send()
    for copy in last:
        copy.wait()


def reduction_scratch():
    return [
        pltpu.VMEM((3, 128, PATCH), F32),
        pltpu.VMEM((3, 3, 32, PATCH), F32),
        pltpu.VMEM((3, 3, 8, PATCH), F32),
        pltpu.VMEM((4, 3, 8, PATCH), F32),
        pltpu.VMEM((3, 128, PATCH), F32),
        pltpu.VMEM((3, 32, PATCH), F32),
        pltpu.VMEM((3, 8, PATCH), F32),
    ]


def exchange(sums, extended, totals, probe):
    copies = REDUCTION_COPIES + 6 * CHUNKS + 4
    return pl.pallas_call(
        exchange_kernel,
        out_shape=(
            jax.ShapeDtypeStruct((2, EXT, EXT), F32),
            jax.ShapeDtypeStruct((2, PATCH, PATCH), F32),
        ),
        in_specs=[VMEM] * 4,
        out_specs=(VMEM, VMEM),
        scratch_shapes=[
            pltpu.VMEM((2, EXT, PATCH), F32),
            pltpu.VMEM((2, PATCH, TILE), F32),
            pltpu.VMEM((2, PATCH, TILE), F32),
            pltpu.VMEM((2, PATCH, PATCH), F32),
            pltpu.VMEM((2, PATCH, PATCH), F32),
            pltpu.VMEM((2, PATCH, PATCH), F32),
            *reduction_scratch(),
            pltpu.SemaphoreType.DMA((copies,)),
            pltpu.SemaphoreType.DMA((copies,)),
        ],
        compiler_params=pltpu.CompilerParams(
            vmem_limit_bytes=48 * 2**20, collective_id=1, has_side_effects=True
        ),
        cost_estimate=pl.CostEstimate(
            flops=10**9, bytes_accessed=14 * 10**6, transcendentals=0
        ),
    )(sums, extended, totals, probe)


def fold_kernel(
    sums, extended, totals, probe, out, probe_out,
    from_left, from_up, bottom,
    land_core, land_y, land_x, land_z, held_core, held_y, held_x,
    send, receive,
):
    here = Place()
    copies = Copies(send, receive)
    reduction = Reduction(
        here, copies, totals, probe, probe_out,
        (land_core, land_y, land_x, land_z), (held_core, held_y, held_x),
    )
    greet(everyone(here))
    reduction.start()
    corner = []
    for chunk in range(CHUNKS):
        rows = rows_of(Z2, chunk)
        corner.append(copies.start(sums.at[:, rows, Z2], from_left.at[:, rows, :], here.right))
    middle = copies.start(sums.at[:, Z2, Z1], from_up.at[:, :, Z1], here.down)
    side = copies.start(sums.at[:, 0:TILE, Z2], from_left.at[:, 0:TILE, :], here.right)
    reduction.after_core()
    out[:, Z1, Z1] = extended[:, Z1, Z1] + sums[:, Z1, Z1]
    reduction.after_y()
    outer = []
    for chunk in range(CHUNKS):
        rows = rows_of(Z0, chunk)
        low = rows_of(Z2, chunk)
        corner[chunk].wait_recv()
        bottom[:, rows, :] = sums[:, low, Z0] + from_left[:, low, :]
        outer.append(copies.start(bottom.at[:, rows, :], from_up.at[:, rows, Z0], here.down))
    reduction.after_x()
    reduction.after_z()
    side.wait_recv()
    out[:, Z1, Z0] = extended[:, Z1, Z0] + (sums[:, Z1, Z0] + from_left[:, Z1, :])
    reduction.gather_x()
    middle.wait_recv()
    out[:, Z0, Z1] = extended[:, Z0, Z1] + (sums[:, Z0, Z1] + from_up[:, :, Z1])
    reduction.gather_y()
    for chunk in range(CHUNKS):
        rows = rows_of(Z0, chunk)
        outer[chunk].wait_recv()
        out[:, rows, Z0] = extended[:, rows, Z0] + (
            (sums[:, rows, Z0] + from_left[:, rows, :]) + from_up[:, rows, Z0]
        )
    reduction.finish()
    for copy in corner + [middle, side] + outer:
        copy.wait_send()


def fold(sums, extended, totals, probe):
    copies = REDUCTION_COPIES + 2 * CHUNKS + 2
    return pl.pallas_call(
        fold_kernel,
        out_shape=(
            jax.ShapeDtypeStruct((2, TILE, TILE), F32),
            jax.ShapeDtypeStruct((2, PATCH, PATCH), F32),
        ),
        in_specs=[VMEM] * 4,
        out_specs=(VMEM, VMEM),
        scratch_shapes=[
            pltpu.VMEM((2, EXT, PATCH), F32),
            pltpu.VMEM((2, PATCH, TILE), F32),
            pltpu.VMEM((2, PATCH, PATCH), F32),
            *reduction_scratch(),
            pltpu.SemaphoreType.DMA((copies,)),
            pltpu.SemaphoreType.DMA((copies,)),
        ],
        compiler_params=pltpu.CompilerParams(
            vmem_limit_bytes=48 * 2**20, collective_id=2, has_side_effects=True
        ),
        cost_estimate=pl.CostEstimate(
            flops=10**9, bytes_accessed=14 * 10**6, transcendentals=0
        ),
    )(sums, extended, totals, probe)


def shards(object_field, probe, moduli, positions, counts):
    row = lax.axis_index("ty")
    col = lax.axis_index("tx")
    anchor = jnp.stack([row * TILE, col * TILE])
    offsets = positions - anchor[None, :]
    count = lax.dynamic_slice(counts, (row * lax.axis_size("tx") + col,), (1,))
    table = jnp.asarray(dft_tables())
    extended, ordered = extend(object_field, moduli, jnp.asarray(order_table()))
    sums, totals = run_slots(count, offsets, extended, probe, ordered, table)
    extended, probe = exchange(sums, extended, totals, probe)
    sums, totals = run_slots(count, offsets, extended, probe, ordered, table)
    return fold(sums, extended, totals, probe)


def solution(mesh):
    return jax.shard_map(
        shards,
        mesh=mesh,
        in_specs=(
            P(None, "ty", "tx"),
            P(),
            P(("ty", "tx"), None, None),
            P(("ty", "tx"), None),
            P(),
        ),
        out_specs=(P(None, "ty", "tx"), P()),
        check_vma=False,
    )
```

```python
import math

import jax
import jax.numpy as jnp
from jax import lax
from jax.experimental import pallas as pl
from jax.experimental.pallas import tpu as pltpu
from jax.sharding import PartitionSpec as P

F32 = jnp.float32
BF16 = jnp.bfloat16
MESH = pl.DeviceIdType.MESH

PATCH = 256
HALF = 128
TILE = 512
EXT = 768
CAP = 12
CHUNKS = 4
CHUNK = PATCH // CHUNKS
tiny_value = 1e-06
floor_sq = 0.0625

Z0 = slice(0, 256)
Z1 = slice(256, 512)
Z2 = slice(512, 768)


def write_tables(table):
    first = lax.broadcasted_iota(jnp.int32, (HALF, HALF), 0)
    second = lax.broadcasted_iota(jnp.int32, (HALF, HALF), 1)
    for odd in range(2):
        forms = ((first * (2 * second + odd), 1.0), (second * (2 * first + odd), -1.0))
        for k, (step, sign) in enumerate(forms):
            angle = (step % PATCH).astype(F32) * (2.0 * math.pi / PATCH)
            real = jnp.cos(angle) / 16.0
            imag = jnp.sin(angle) * (-sign / 16.0)
            form = jnp.concatenate(
                [jnp.concatenate([real, imag], 1), jnp.concatenate([-imag, real], 1)], 0
            )
            at = 4 * odd + 2 * k
            table[at], table[at + 1] = split(form)


def dot(left, right):
    return jnp.dot(left, right, preferred_element_type=F32)


def split(value):
    high = value.astype(BF16)
    return high, (value - high.astype(F32)).astype(BF16)


def thirds(value):
    high = value.astype(BF16)
    rest = value - high.astype(F32)
    middle = rest.astype(BF16)
    return high, middle, (rest - middle.astype(F32)).astype(BF16)


def right_product(value, table, at):
    high, low = split(value)
    both = dot(jnp.concatenate([high, low], 0), table[at])
    return both[:PATCH] + (both[PATCH:] + dot(high, table[at + 1]))


def left_product(table, at, value):
    high, low = split(value)
    both = dot(jnp.concatenate([table[at], table[at + 1]], 0), high)
    return both[:PATCH] + (both[PATCH:] + dot(table[at], low))


def window(row, col):
    sub_shift = row % 8
    lane_shift = col % 128
    row_at = pl.multiple_of(row - sub_shift, 8)
    col_at = pl.multiple_of(col - lane_shift, 128)
    sub = lax.broadcasted_iota(jnp.int32, (33, 8, 128), 1)
    lane = lax.broadcasted_iota(jnp.int32, (33, 8, 128), 2)
    return row_at, col_at, sub_shift, lane_shift, sub, lane


def gather(ref, plane, row, col):
    row_at, col_at, sub_shift, lane_shift, sub, lane = window(row, col)
    cols = []
    for k in range(3):
        block = ref[plane, pl.ds(row_at, 264), pl.ds(col_at + 128 * k, 128)]
        cols.append(pltpu.roll(block.reshape(33, 8, 128), (128 - lane_shift) % 128, 2))
    parts = []
    for k in range(2):
        block = jnp.where(lane < 128 - lane_shift, cols[k], cols[k + 1])
        block = pltpu.roll(block, (8 - sub_shift) % 8, 1)
        block = jnp.where(sub[:32] < 8 - sub_shift, block[:32], block[1:])
        parts.append(block.reshape(PATCH, 128))
    return jnp.concatenate(parts, 1)


def scatter_add(ref, plane, row, col, update):
    row_at, col_at, sub_shift, lane_shift, sub, lane = window(row, col)
    zeros = jnp.zeros((1, 8, 128), F32)
    parts = []
    for k in range(2):
        block = pltpu.roll(update[:, 128 * k : 128 * k + 128].reshape(32, 8, 128), sub_shift, 1)
        block = jnp.where(
            sub >= sub_shift,
            jnp.concatenate([block, zeros], 0),
            jnp.concatenate([zeros, block], 0),
        )
        parts.append(pltpu.roll(block, lane_shift, 2))
    right = lane >= lane_shift
    cols = [
        jnp.where(right, parts[0], 0.0),
        jnp.where(right, parts[1], parts[0]),
        jnp.where(right, 0.0, parts[1]),
    ]
    for k in range(3):
        place = (plane, pl.ds(row_at, 264), pl.ds(col_at + 128 * k, 128))
        ref[place] += cols[k].reshape(264, 128)


def scaled(wave, modulus):
    real = wave[:HALF]
    imag = wave[HALF:]
    scale = modulus * lax.rsqrt(real * real + imag * imag + floor_sq) - 1.0
    return jnp.concatenate([real * scale, imag * scale], 0)


def visit(slot, corner, extended, probe, weighted, moduli, table, sums, totals):
    row, col = corner(slot)
    patch_real = gather(extended, 0, row, col)
    patch_imag = gather(extended, 1, row, col)
    totals[2] += patch_real * patch_real + patch_imag * patch_imag
    exit_real = probe[0] * patch_real - probe[1] * patch_imag
    exit_imag = probe[0] * patch_imag + probe[1] * patch_real
    even = jnp.concatenate(
        [exit_real[:, :HALF] + exit_real[:, HALF:], exit_imag[:, :HALF] + exit_imag[:, HALF:]], 1
    )
    odd = jnp.concatenate(
        [exit_real[:, :HALF] - exit_real[:, HALF:], exit_imag[:, :HALF] - exit_imag[:, HALF:]], 1
    )
    yield
    even = right_product(even, table, 0)
    odd = right_product(odd, table, 4)
    yield
    real = jnp.concatenate([even[:, :HALF], odd[:, :HALF]], 1)
    imag = jnp.concatenate([even[:, HALF:], odd[:, HALF:]], 1)
    even = jnp.concatenate([real[:HALF] + real[HALF:], imag[:HALF] + imag[HALF:]], 0)
    odd = jnp.concatenate([real[:HALF] - real[HALF:], imag[:HALF] - imag[HALF:]], 0)
    yield
    even = left_product(table, 2, even)
    odd = left_product(table, 6, odd)
    yield
    even = scaled(even, moduli[slot, :HALF])
    odd = scaled(odd, moduli[slot, HALF:])
    yield
    even = left_product(table, 0, even)
    odd = left_product(table, 4, odd)
    yield
    real = jnp.concatenate([even[:HALF] + odd[:HALF], even[:HALF] - odd[:HALF]], 0)
    imag = jnp.concatenate([even[HALF:] + odd[HALF:], even[HALF:] - odd[HALF:]], 0)
    even = jnp.concatenate([real[:, :HALF], imag[:, :HALF]], 1)
    odd = jnp.concatenate([real[:, HALF:], imag[:, HALF:]], 1)
    yield
    even = right_product(even, table, 2)
    odd = right_product(odd, table, 6)
    yield
    delta_real = jnp.concatenate(
        [even[:, :HALF] + odd[:, :HALF], even[:, :HALF] - odd[:, :HALF]], 1
    )
    delta_imag = jnp.concatenate(
        [even[:, HALF:] + odd[:, HALF:], even[:, HALF:] - odd[:, HALF:]], 1
    )
    totals[0] += patch_real * delta_real + patch_imag * delta_imag
    totals[1] += patch_real * delta_imag - patch_imag * delta_real
    yield
    scatter_add(sums, 0, row, col, weighted[0] * delta_real + weighted[1] * delta_imag)
    scatter_add(sums, 1, row, col, weighted[0] * delta_imag - weighted[1] * delta_real)


def visit_together(slots, *refs):
    turns = [visit(slot, *refs) for slot in slots]
    while turns:
        turns = [turn for turn in turns if next(turn, "end") != "end"]


def slots_kernel(
    counts, positions, extended, probe, moduli, table, sums, totals, weighted
):
    ty = lax.axis_index("ty")
    tx = lax.axis_index("tx")
    count = counts[ty * lax.axis_size("tx") + tx]
    peak = jnp.max(probe[0] * probe[0] + probe[1] * probe[1])
    weighted[...] = probe[...] * (1.0 / (peak + tiny_value))
    sums[...] = jnp.zeros_like(sums)
    totals[...] = jnp.zeros_like(totals)

    def corner(slot):
        return positions[0, slot] - ty * TILE, positions[1, slot] - tx * TILE

    refs = (corner, extended, probe, weighted, moduli, table, sums, totals)

    def two(pair, carry):
        visit_together([2 * pair, 2 * pair + 1], *refs)
        return carry

    def one(slot, carry):
        visit_together([slot], *refs)
        return carry

    lax.fori_loop(0, count // 2, two, 0)
    lax.fori_loop(2 * (count // 2), count, one, 0)


VMEM = pl.BlockSpec(memory_space=pltpu.VMEM)
SMEM = pl.BlockSpec(memory_space=pltpu.SMEM)
HBM = pl.BlockSpec(memory_space=pltpu.HBM)


def run_slots(counts, positions, extended, probe, moduli, table):
    return pl.pallas_call(
        slots_kernel,
        out_shape=(
            jax.ShapeDtypeStruct((2, EXT, EXT), F32),
            jax.ShapeDtypeStruct((3, PATCH, PATCH), F32),
        ),
        in_specs=[SMEM, SMEM, VMEM, VMEM, VMEM, VMEM],
        out_specs=(VMEM, VMEM),
        scratch_shapes=[
            pltpu.VMEM((2, PATCH, PATCH), F32),
        ],
        compiler_params=pltpu.CompilerParams(vmem_limit_bytes=24 * 2**20),
        cost_estimate=pl.CostEstimate(
            flops=6 * 10**9, bytes_accessed=14 * 10**6, transcendentals=0
        ),
    )(counts, positions, extended, probe, moduli, table)


class Place:
    def __init__(self):
        ty = lax.axis_index("ty")
        tx = lax.axis_index("tx")
        self.ty, self.tx = ty, tx
        self.y, self.x = ty // 4, ty % 4
        self.z, self.core = tx // 2, tx % 2
        self.up = ((ty + 15) % 16, tx)
        self.down = ((ty + 1) % 16, tx)
        self.left = (ty, (tx + 7) % 8)
        self.right = (ty, (tx + 1) % 8)
        self.other = (ty, self.z * 2 + 1 - self.core)

    def along_y(self, step):
        return (((self.y + step) % 4) * 4 + self.x, self.tx)

    def along_x(self, step):
        return (self.y * 4 + (self.x + step) % 4, self.tx)

    def along_z(self, step):
        return (self.ty, ((self.z + step) % 4) * 2 + self.core)


def greet(devices):
    barrier = pltpu.get_barrier_semaphore()
    for device in devices:
        pl.semaphore_signal(barrier, inc=1, device_id=device, device_id_type=MESH)
    pl.semaphore_wait(barrier, len(devices))


class Copies:
    def __init__(self, send, receive):
        self.send, self.receive, self.used = send, receive, 0

    def start(self, source, target, device):
        copy = pltpu.make_async_remote_copy(
            src_ref=source,
            dst_ref=target,
            send_sem=self.send.at[self.used],
            recv_sem=self.receive.at[self.used],
            device_id=device,
            device_id_type=MESH,
        )
        self.used += 1
        copy.start()
        return copy


def rows_of(zone, chunk):
    return slice(zone.start + chunk * CHUNK, zone.start + (chunk + 1) * CHUNK)


def extend_kernel(tile, moduli_far, extended, ordered, table, moduli, send, receive, arrived):
    here = Place()
    copies = Copies(send, receive)
    moduli_copy = pltpu.make_async_copy(moduli_far, moduli, arrived.at[0])
    moduli_copy.start()
    tile_copy = pltpu.make_async_copy(tile, extended.at[:, 0:TILE, 0:TILE], arrived.at[1])
    tile_copy.start()
    greet([here.up, here.down, here.left, here.right])
    above = []
    for chunk in range(CHUNKS):
        above.append(
            copies.start(
                tile.at[:, rows_of(Z0, chunk), Z0], extended.at[:, rows_of(Z2, chunk), Z0], here.up
            )
        )
    beside = [copies.start(tile.at[:, :, Z0], extended.at[:, 0:TILE, Z2], here.left)]
    beside.append(copies.start(tile.at[:, Z0, Z1], extended.at[:, Z2, Z1], here.up))

    first = lax.broadcasted_iota(jnp.int32, (PATCH, PATCH), 0)
    second = lax.broadcasted_iota(jnp.int32, (PATCH, PATCH), 1)
    rows_order = (second == 2 * (first % HALF) + first // HALF).astype(F32).astype(BF16)
    cols_order = (first == 2 * (second % HALF) + second // HALF).astype(F32).astype(BF16)

    def reorder(slot, carry):
        block = moduli[slot]
        block = sum(dot(rows_order, part) for part in thirds(block))
        ordered[slot] = sum(dot(part, cols_order) for part in thirds(block))
        return carry

    write_tables(table)
    moduli_copy.wait()
    lax.fori_loop(0, CAP, reorder, 0)
    for chunk in range(CHUNKS):
        above[chunk].wait_recv()
        beside.append(
            copies.start(
                extended.at[:, rows_of(Z2, chunk), Z0],
                extended.at[:, rows_of(Z2, chunk), Z2],
                here.left,
            )
        )
    tile_copy.wait()
    for copy in above:
        copy.wait_send()
    for copy in beside:
        copy.wait()


def extend(tile, moduli):
    copies = 2 * CHUNKS + 2
    return pl.pallas_call(
        extend_kernel,
        out_shape=(
            jax.ShapeDtypeStruct((2, EXT, EXT), F32),
            jax.ShapeDtypeStruct((CAP, PATCH, PATCH), F32),
            jax.ShapeDtypeStruct((8, PATCH, PATCH), BF16),
        ),
        in_specs=[HBM, HBM],
        out_specs=(VMEM, VMEM, VMEM),
        scratch_shapes=[
            pltpu.VMEM((CAP, PATCH, PATCH), F32),
            pltpu.SemaphoreType.DMA((copies,)),
            pltpu.SemaphoreType.DMA((copies,)),
            pltpu.SemaphoreType.DMA((2,)),
        ],
        compiler_params=pltpu.CompilerParams(
            vmem_limit_bytes=20 * 2**20, collective_id=0, has_side_effects=True
        ),
        cost_estimate=pl.CostEstimate(
            flops=10**9, bytes_accessed=14 * 10**6, transcendentals=0
        ),
    )(tile, moduli)


class Reduction:
    def __init__(self, here, copies, totals, probe, probe_out, landed, held):
        self.here, self.copies = here, copies
        self.totals, self.probe, self.probe_out = totals, probe, probe_out
        self.land_core, self.land_z, self.land_x, self.land_y = landed
        self.held_core, self.held_z, self.held_x = held
        self.in_flight = []
        self.sent = []

    def launch(self, source, target, device):
        self.in_flight.append(self.copies.start(source, target, device))

    def arrive(self):
        for copy in self.in_flight:
            copy.wait_recv()
        self.sent += self.in_flight
        self.in_flight = []

    def start(self):
        half = pl.ds(pl.multiple_of((1 - self.here.core) * HALF, HALF), HALF)
        self.launch(self.totals.at[:, half, :], self.land_core, self.here.other)

    def after_core(self):
        self.arrive()
        half = pl.ds(pl.multiple_of(self.here.core * HALF, HALF), HALF)
        self.held_core[...] = self.totals[:, half, :] + self.land_core[...]
        for step in (2, 1, 3):
            part = pl.ds(pl.multiple_of(((self.here.z + step) % 4) * 32, 32), 32)
            self.launch(
                self.held_core.at[:, part, :], self.land_z.at[step - 1], self.here.along_z(step)
            )

    def after_z(self):
        self.arrive()
        part = pl.ds(pl.multiple_of(self.here.z * 32, 32), 32)
        self.held_z[...] = (self.held_core[:, part, :] + self.land_z[0]) + (
            self.land_z[1] + self.land_z[2]
        )
        for step in (2, 1, 3):
            part = pl.ds(pl.multiple_of(((self.here.x + step) % 4) * 8, 8), 8)
            self.launch(
                self.held_z.at[:, part, :], self.land_x.at[step - 1], self.here.along_x(step)
            )

    def after_x(self):
        self.arrive()
        part = pl.ds(pl.multiple_of(self.here.x * 8, 8), 8)
        self.held_x[...] = (self.held_z[:, part, :] + self.land_x[0]) + (
            self.land_x[1] + self.land_x[2]
        )
        for step in (2, 1, 3):
            self.launch(self.held_x, self.land_y.at[self.here.y], self.here.along_y(step))
        self.land_y[self.here.y] = self.held_x[...]

    def share(self, rows):
        start = self.here.core * HALF
        if rows < 128:
            start = start + self.here.z * 32
        if rows < 32:
            start = start + self.here.x * 8
        return pl.ds(pl.multiple_of(start, rows), rows)

    def spread(self, rows, device):
        part = self.probe_out.at[:, self.share(rows), :]
        self.launch(part, part, device)

    def after_y(self):
        self.arrive()
        total = (self.land_y[0] + self.land_y[1]) + (self.land_y[2] + self.land_y[3])
        part = self.share(8)
        self.probe_out[:, part, :] = self.probe[:, part, :] + total[0:2] / (
            total[2:3] + tiny_value
        )
        for step in (2, 1, 3):
            self.spread(8, self.here.along_x(step))

    def gather_x(self):
        self.arrive()
        for step in (2, 1, 3):
            self.spread(32, self.here.along_z(step))

    def gather_z(self):
        self.arrive()
        self.spread(128, self.here.other)

    def finish(self):
        self.arrive()
        for copy in self.sent:
            copy.wait_send()


REDUCTION_COPIES = 1 + 3 + 3 + 3 + 3 + 3 + 1


def everyone(here):
    devices = [here.up, here.down, here.left, here.right, here.other]
    for step in range(1, 4):
        devices += [here.along_y(step), here.along_x(step), here.along_z(step)]
    return devices


def exchange_kernel(
    sums, extended, totals, probe, out, probe_out,
    from_left, from_up, from_down, from_right, top, bottom,
    land_core, land_z, land_x, land_y, held_core, held_z, held_x,
    send, receive,
):
    here = Place()
    copies = Copies(send, receive)
    reduction = Reduction(
        here, copies, totals, probe, probe_out,
        (land_core, land_z, land_x, land_y), (held_core, held_z, held_x),
    )
    greet(everyone(here))
    corners, outer, last = [], [], []

    def send_corner(chunk):
        pair = []
        for zone in (Z2, Z0):
            rows = rows_of(zone, chunk)
            pair.append(copies.start(sums.at[:, rows, Z2], from_left.at[:, rows, :], here.right))
        corners.append(pair)

    def take_corner(chunk):
        rows, low = rows_of(Z0, chunk), rows_of(Z2, chunk)
        for copy in corners[chunk]:
            copy.wait_recv()
        bottom[:, rows, :] = sums[:, low, Z0] + from_left[:, low, :]
        top[:, rows, :] = sums[:, rows, Z0] + from_left[:, rows, :]

    def send_outer(chunk):
        rows = rows_of(Z0, chunk)
        down = copies.start(bottom.at[:, rows, :], from_up.at[:, rows, Z0], here.down)
        up = copies.start(top.at[:, rows, :], from_down.at[:, rows, Z0], here.up)
        outer.append((down, up))

    def take_outer(chunk):
        rows, low = rows_of(Z0, chunk), rows_of(Z2, chunk)
        down, up = outer[chunk]
        down.wait_recv()
        out[:, rows, Z0] = extended[:, rows, Z0] + (top[:, rows, :] + from_up[:, rows, Z0])
        last.append(copies.start(out.at[:, rows, Z0], out.at[:, rows, Z2], here.left))
        up.wait_recv()
        out[:, low, Z0] = extended[:, low, Z0] + (bottom[:, rows, :] + from_down[:, rows, Z0])
        last.append(copies.start(out.at[:, low, Z0], out.at[:, low, Z2], here.left))

    reduction.start()
    send_corner(0)
    middle_down = copies.start(sums.at[:, Z2, Z1], from_up.at[:, :, Z1], here.down)
    middle_up = copies.start(sums.at[:, Z0, Z1], from_down.at[:, :, Z1], here.up)
    reduction.after_core()
    for chunk in range(1, CHUNKS):
        send_corner(chunk)
    side_left = copies.start(sums.at[:, Z1, Z0], from_right, here.left)
    side_right = copies.start(sums.at[:, Z1, Z2], from_left.at[:, Z1, :], here.right)
    out[:, Z1, Z1] = extended[:, Z1, Z1] + sums[:, Z1, Z1]
    reduction.after_z()
    take_corner(0)
    send_outer(0)
    middle_down.wait_recv()
    out[:, Z0, Z1] = extended[:, Z0, Z1] + (sums[:, Z0, Z1] + from_up[:, :, Z1])
    middle_up.wait_recv()
    out[:, Z2, Z1] = extended[:, Z2, Z1] + (sums[:, Z2, Z1] + from_down[:, :, Z1])
    reduction.after_x()
    for chunk in range(1, CHUNKS):
        take_corner(chunk)
    reduction.after_y()
    for chunk in range(1, CHUNKS):
        send_outer(chunk)
    side_left.wait_recv()
    out[:, Z1, Z2] = extended[:, Z1, Z2] + (sums[:, Z1, Z2] + from_right[...])
    take_outer(0)
    reduction.gather_x()
    side_right.wait_recv()
    out[:, Z1, Z0] = extended[:, Z1, Z0] + (sums[:, Z1, Z0] + from_left[:, Z1, :])
    take_outer(1)
    reduction.gather_z()
    for chunk in range(2, CHUNKS):
        take_outer(chunk)
    reduction.finish()
    for pair in corners + outer:
        for copy in pair:
            copy.wait_send()
    for copy in [middle_down, middle_up, side_left, side_right]:
        copy.wait_send()
    for copy in last:
        copy.wait()


def reduction_scratch():
    return [
        pltpu.VMEM((3, 128, PATCH), F32),
        pltpu.VMEM((3, 3, 32, PATCH), F32),
        pltpu.VMEM((3, 3, 8, PATCH), F32),
        pltpu.VMEM((4, 3, 8, PATCH), F32),
        pltpu.VMEM((3, 128, PATCH), F32),
        pltpu.VMEM((3, 32, PATCH), F32),
        pltpu.VMEM((3, 8, PATCH), F32),
    ]


def exchange(sums, extended, totals, probe):
    copies = REDUCTION_COPIES + 6 * CHUNKS + 4
    return pl.pallas_call(
        exchange_kernel,
        out_shape=(
            jax.ShapeDtypeStruct((2, EXT, EXT), F32),
            jax.ShapeDtypeStruct((2, PATCH, PATCH), F32),
        ),
        in_specs=[VMEM] * 4,
        out_specs=(VMEM, VMEM),
        scratch_shapes=[
            pltpu.VMEM((2, EXT, PATCH), F32),
            pltpu.VMEM((2, PATCH, TILE), F32),
            pltpu.VMEM((2, PATCH, TILE), F32),
            pltpu.VMEM((2, PATCH, PATCH), F32),
            pltpu.VMEM((2, PATCH, PATCH), F32),
            pltpu.VMEM((2, PATCH, PATCH), F32),
            *reduction_scratch(),
            pltpu.SemaphoreType.DMA((copies,)),
            pltpu.SemaphoreType.DMA((copies,)),
        ],
        compiler_params=pltpu.CompilerParams(
            vmem_limit_bytes=28 * 2**20, collective_id=1, has_side_effects=True
        ),
        cost_estimate=pl.CostEstimate(
            flops=10**9, bytes_accessed=14 * 10**6, transcendentals=0
        ),
    )(sums, extended, totals, probe)


def fold_kernel(
    sums, extended, totals, probe, out, probe_out,
    from_left, from_up, bottom,
    land_core, land_z, land_x, land_y, held_core, held_z, held_x,
    send, receive,
):
    here = Place()
    copies = Copies(send, receive)
    reduction = Reduction(
        here, copies, totals, probe, probe_out,
        (land_core, land_z, land_x, land_y), (held_core, held_z, held_x),
    )
    greet(everyone(here))
    corners, outer = [], []

    def send_corner(chunk):
        rows = rows_of(Z2, chunk)
        corners.append(copies.start(sums.at[:, rows, Z2], from_left.at[:, rows, :], here.right))

    def take_corner(chunk):
        rows, low = rows_of(Z0, chunk), rows_of(Z2, chunk)
        corners[chunk].wait_recv()
        bottom[:, rows, :] = sums[:, low, Z0] + from_left[:, low, :]

    def send_outer(chunk):
        rows = rows_of(Z0, chunk)
        outer.append(copies.start(bottom.at[:, rows, :], from_up.at[:, rows, Z0], here.down))

    reduction.start()
    send_corner(0)
    middle = copies.start(sums.at[:, Z2, Z1], from_up.at[:, :, Z1], here.down)
    reduction.after_core()
    for chunk in range(1, CHUNKS):
        send_corner(chunk)
    side = copies.start(sums.at[:, 0:TILE, Z2], from_left.at[:, 0:TILE, :], here.right)
    out[:, Z1, Z1] = extended[:, Z1, Z1] + sums[:, Z1, Z1]
    reduction.after_z()
    take_corner(0)
    send_outer(0)
    middle.wait_recv()
    out[:, Z0, Z1] = extended[:, Z0, Z1] + (sums[:, Z0, Z1] + from_up[:, :, Z1])
    reduction.after_x()
    for chunk in range(1, CHUNKS):
        take_corner(chunk)
    reduction.after_y()
    for chunk in range(1, CHUNKS):
        send_outer(chunk)
    side.wait_recv()
    out[:, Z1, Z0] = extended[:, Z1, Z0] + (sums[:, Z1, Z0] + from_left[:, Z1, :])
    reduction.gather_x()
    reduction.gather_z()
    for chunk in range(CHUNKS):
        rows = rows_of(Z0, chunk)
        outer[chunk].wait_recv()
        out[:, rows, Z0] = extended[:, rows, Z0] + (
            (sums[:, rows, Z0] + from_left[:, rows, :]) + from_up[:, rows, Z0]
        )
    reduction.finish()
    for copy in corners + outer + [middle, side]:
        copy.wait_send()


def fold(sums, extended, totals, probe):
    copies = REDUCTION_COPIES + 2 * CHUNKS + 2
    return pl.pallas_call(
        fold_kernel,
        out_shape=(
            jax.ShapeDtypeStruct((2, TILE, TILE), F32),
            jax.ShapeDtypeStruct((2, PATCH, PATCH), F32),
        ),
        in_specs=[VMEM] * 4,
        out_specs=(VMEM, VMEM),
        scratch_shapes=[
            pltpu.VMEM((2, EXT, PATCH), F32),
            pltpu.VMEM((2, PATCH, TILE), F32),
            pltpu.VMEM((2, PATCH, PATCH), F32),
            *reduction_scratch(),
            pltpu.SemaphoreType.DMA((copies,)),
            pltpu.SemaphoreType.DMA((copies,)),
        ],
        compiler_params=pltpu.CompilerParams(
            vmem_limit_bytes=22 * 2**20, collective_id=2, has_side_effects=True
        ),
        cost_estimate=pl.CostEstimate(
            flops=10**9, bytes_accessed=14 * 10**6, transcendentals=0
        ),
    )(sums, extended, totals, probe)


def shards(object_field, probe, moduli, positions, counts):
    positions = positions.T
    extended, ordered, table = extend(
        pltpu.with_memory_space_constraint(object_field, pltpu.HBM),
        pltpu.with_memory_space_constraint(moduli, pltpu.HBM),
    )
    sums, totals = run_slots(counts, positions, extended, probe, ordered, table)
    extended, probe = exchange(sums, extended, totals, probe)
    sums, totals = run_slots(counts, positions, extended, probe, ordered, table)
    return fold(sums, extended, totals, probe)


def solution(mesh):
    return jax.shard_map(
        shards,
        mesh=mesh,
        in_specs=(
            P(None, "ty", "tx"),
            P(),
            P(("ty", "tx"), None, None),
            P(("ty", "tx"), None),
            P(),
        ),
        out_specs=(P(None, "ty", "tx"), P()),
        check_vma=False,
    )
```

```python
import math

import jax
import jax.numpy as jnp
from jax import lax
from jax.experimental import pallas as pl
from jax.experimental.pallas import tpu as pltpu
from jax.sharding import PartitionSpec as P

F32 = jnp.float32
BF16 = jnp.bfloat16
MESH = pl.DeviceIdType.MESH

PATCH = 256
HALF = 128
TILE = 512
EXT = 768
CAP = 12
NEAR = 4
EARLY = 8
CHUNKS = 4
CHUNK = PATCH // CHUNKS
tiny_value = 1e-06
floor_sq = 0.0625

Z0 = slice(0, 256)
Z1 = slice(256, 512)
Z2 = slice(512, 768)


def write_tables(table):
    first = lax.broadcasted_iota(jnp.int32, (HALF, HALF), 0)
    second = lax.broadcasted_iota(jnp.int32, (HALF, HALF), 1)
    for odd in range(2):
        forms = ((first * (2 * second + odd), 1.0), (second * (2 * first + odd), -1.0))
        for k, (step, sign) in enumerate(forms):
            angle = (step % PATCH).astype(F32) * (2.0 * math.pi / PATCH)
            real = jnp.cos(angle) / 16.0
            imag = jnp.sin(angle) * (-sign / 16.0)
            form = jnp.concatenate(
                [jnp.concatenate([real, imag], 1), jnp.concatenate([-imag, real], 1)], 0
            )
            at = 4 * odd + 2 * k
            table[at], table[at + 1] = split(form)


def dot(left, right):
    return jnp.dot(left, right, preferred_element_type=F32)


def split(value):
    high = value.astype(BF16)
    return high, (value - high.astype(F32)).astype(BF16)


def thirds(value):
    high = value.astype(BF16)
    rest = value - high.astype(F32)
    middle = rest.astype(BF16)
    return high, middle, (rest - middle.astype(F32)).astype(BF16)


def right_product(value, table, at):
    high, low = split(value)
    both = dot(jnp.concatenate([high, low], 0), table[at])
    return both[:PATCH] + (both[PATCH:] + dot(high, table[at + 1]))


def left_product(table, at, value):
    high, low = split(value)
    both = dot(jnp.concatenate([table[at], table[at + 1]], 0), high)
    return both[:PATCH] + (both[PATCH:] + dot(table[at], low))


def window(row, col):
    row_at = lax.shift_right_logical(row, 3) * 8
    col_at = lax.shift_right_logical(col, 7) * 128
    sub_shift = row - row_at
    lane_shift = col - col_at
    sub = lax.broadcasted_iota(jnp.int32, (33, 8, 128), 1)
    lane = lax.broadcasted_iota(jnp.int32, (33, 8, 128), 2)
    return row_at, col_at, sub_shift, lane_shift, sub, lane


def gather(ref, plane, row, col):
    row_at, col_at, sub_shift, lane_shift, sub, lane = window(row, col)
    cols = []
    for k in range(3):
        block = ref[plane, pl.ds(row_at, 264), pl.ds(col_at + 128 * k, 128)]
        cols.append(pltpu.roll(block.reshape(33, 8, 128), (128 - lane_shift) & 127, 2))
    parts = []
    for k in range(2):
        block = jnp.where(lane < 128 - lane_shift, cols[k], cols[k + 1])
        block = pltpu.roll(block, (8 - sub_shift) & 7, 1)
        block = jnp.where(sub[:32] < 8 - sub_shift, block[:32], block[1:])
        parts.append(block.reshape(PATCH, 128))
    return jnp.concatenate(parts, 1)


def scatter_add(ref, plane, row, col, update):
    row_at, col_at, sub_shift, lane_shift, sub, lane = window(row, col)
    zeros = jnp.zeros((1, 8, 128), F32)
    parts = []
    for k in range(2):
        block = pltpu.roll(update[:, 128 * k : 128 * k + 128].reshape(32, 8, 128), sub_shift, 1)
        block = jnp.where(
            sub >= sub_shift,
            jnp.concatenate([block, zeros], 0),
            jnp.concatenate([zeros, block], 0),
        )
        parts.append(pltpu.roll(block, lane_shift, 2))
    right = lane >= lane_shift
    cols = [
        jnp.where(right, parts[0], 0.0),
        jnp.where(right, parts[1], parts[0]),
        jnp.where(right, 0.0, parts[1]),
    ]
    for k in range(3):
        place = (plane, pl.ds(row_at, 264), pl.ds(col_at + 128 * k, 128))
        ref[place] += cols[k].reshape(264, 128)


def scaled(wave, modulus):
    real = wave[:HALF]
    imag = wave[HALF:]
    scale = modulus * lax.rsqrt(real * real + imag * imag + floor_sq) - 1.0
    return jnp.concatenate([real * scale, imag * scale], 0)


def visit(slot, row, col, keep, source, probe, weighted, moduli, table, totals, deliver):
    patch_real = gather(source, 0, row, col)
    patch_imag = gather(source, 1, row, col)
    kept_real, kept_imag = patch_real, patch_imag
    if keep is not None:
        kept_real, kept_imag = patch_real * keep, patch_imag * keep
    totals[2] += patch_real * kept_real + patch_imag * kept_imag
    exit_real = probe[0] * patch_real - probe[1] * patch_imag
    exit_imag = probe[0] * patch_imag + probe[1] * patch_real
    even = jnp.concatenate(
        [exit_real[:, :HALF] + exit_real[:, HALF:], exit_imag[:, :HALF] + exit_imag[:, HALF:]], 1
    )
    odd = jnp.concatenate(
        [exit_real[:, :HALF] - exit_real[:, HALF:], exit_imag[:, :HALF] - exit_imag[:, HALF:]], 1
    )
    yield
    even = right_product(even, table, 0)
    odd = right_product(odd, table, 4)
    yield
    real = jnp.concatenate([even[:, :HALF], odd[:, :HALF]], 1)
    imag = jnp.concatenate([even[:, HALF:], odd[:, HALF:]], 1)
    even = jnp.concatenate([real[:HALF] + real[HALF:], imag[:HALF] + imag[HALF:]], 0)
    odd = jnp.concatenate([real[:HALF] - real[HALF:], imag[:HALF] - imag[HALF:]], 0)
    yield
    even = left_product(table, 2, even)
    odd = left_product(table, 6, odd)
    yield
    even = scaled(even, moduli[slot, :HALF])
    odd = scaled(odd, moduli[slot, HALF:])
    yield
    even = left_product(table, 0, even)
    odd = left_product(table, 4, odd)
    yield
    real = jnp.concatenate([even[:HALF] + odd[:HALF], even[:HALF] - odd[:HALF]], 0)
    imag = jnp.concatenate([even[HALF:] + odd[HALF:], even[HALF:] - odd[HALF:]], 0)
    even = jnp.concatenate([real[:, :HALF], imag[:, :HALF]], 1)
    odd = jnp.concatenate([real[:, HALF:], imag[:, HALF:]], 1)
    yield
    even = right_product(even, table, 2)
    odd = right_product(odd, table, 6)
    yield
    delta_real = jnp.concatenate(
        [even[:, :HALF] + odd[:, :HALF], even[:, :HALF] - odd[:, :HALF]], 1
    )
    delta_imag = jnp.concatenate(
        [even[:, HALF:] + odd[:, HALF:], even[:, HALF:] - odd[:, HALF:]], 1
    )
    totals[0] += kept_real * delta_real + kept_imag * delta_imag
    totals[1] += kept_real * delta_imag - kept_imag * delta_real
    yield
    deliver(0, weighted[0] * delta_real + weighted[1] * delta_imag)
    deliver(1, weighted[0] * delta_imag - weighted[1] * delta_real)


def together(turns):
    while turns:
        turns = [turn for turn in turns if next(turn, "end") != "end"]


class Slots:
    def __init__(self, counts, positions):
        self.positions = positions
        self.ty = lax.axis_index("ty")
        self.tx = lax.axis_index("tx")
        self.count = counts[self.ty * lax.axis_size("tx") + self.tx]
        self.place = []
        near, far = jnp.int32(0), jnp.int32(NEAR)
        for slot in range(CAP):
            used = slot < self.count
            takes_near = used & (self.row(slot) <= TILE - PATCH) & (near < NEAR)
            takes_far = used & (self.row(slot) <= TILE - HALF) & (far < EARLY)
            place = jnp.where(takes_near, near, jnp.where(takes_far, far, -1))
            near = near + takes_near.astype(jnp.int32)
            far = far + jnp.where(takes_near, 0, takes_far.astype(jnp.int32))
            self.place.append(place)

    def row(self, slot):
        return self.positions[0, slot] - self.ty * TILE

    def col(self, slot):
        return self.positions[1, slot] - self.tx * TILE

    def at(self, place):
        found, present = jnp.int32(0), jnp.int32(0)
        for slot in range(CAP):
            chosen = self.place[slot] == place
            found = jnp.where(chosen, slot, found)
            present = jnp.where(chosen, 1, present)
        return found, present


def write_weighted(weighted, probe):
    peak = jnp.max(probe[0] * probe[0] + probe[1] * probe[1])
    weighted[...] = probe[...] * (1.0 / (peak + tiny_value))


def slots_kernel(
    first, counts, positions, extended, probe, moduli, table, updates, totals_in,
    sums, totals, weighted, queue,
):
    slots = Slots(counts, positions)
    write_weighted(weighted, probe)
    sums[...] = jnp.zeros_like(sums)

    def turn(slot):
        row, col = slots.row(slot), slots.col(slot)

        def deliver(plane, update):
            scatter_add(sums, plane, row, col, update)

        return visit(
            slot, row, col, None, extended, probe, weighted, moduli, table, totals, deliver
        )

    left = jnp.int32(0)
    if first:
        totals[...] = totals_in[...]

        def add_early(index, carry):
            slot, present = slots.at(index)

            @pl.when(present == 1)
            def _():
                for plane in range(2):
                    update = updates[index, plane]
                    scatter_add(sums, plane, slots.row(slot), slots.col(slot), update)

            return carry

        lax.fori_loop(0, EARLY, add_early, 0)
        for slot in range(CAP):
            queue[left] = slot
            late = (slot < slots.count) & (slots.place[slot] < 0)
            left = left + late.astype(jnp.int32)
        pick = lambda index: queue[index]
    else:
        totals[...] = jnp.zeros_like(totals)
        left = slots.count
        pick = lambda index: index

    def two(pair, carry):
        together([turn(pick(2 * pair)), turn(pick(2 * pair + 1))])
        return carry

    def one(index, carry):
        together([turn(pick(index))])
        return carry

    lax.fori_loop(0, left // 2, two, 0)
    lax.fori_loop(2 * (left // 2), left, one, 0)


VMEM = pl.BlockSpec(memory_space=pltpu.VMEM)
SMEM = pl.BlockSpec(memory_space=pltpu.SMEM)
HBM = pl.BlockSpec(memory_space=pltpu.HBM)


def run_slots(counts, positions, extended, probe, moduli, table, updates=None, totals=None):
    first = updates is not None

    def kernel(*refs):
        refs = list(refs)
        if not first:
            refs[6:6] = [None, None]
        slots_kernel(first, *refs)

    operands = [counts, positions, extended, probe, moduli, table]
    if first:
        operands += [updates, totals]
    return pl.pallas_call(
        kernel,
        out_shape=(
            jax.ShapeDtypeStruct((2, EXT, EXT), F32),
            jax.ShapeDtypeStruct((3, PATCH, PATCH), F32),
        ),
        in_specs=[SMEM, SMEM] + [VMEM] * (len(operands) - 2),
        out_specs=(VMEM, VMEM),
        scratch_shapes=[pltpu.VMEM((2, PATCH, PATCH), F32), pltpu.SMEM((CAP,), jnp.int32)],
        compiler_params=pltpu.CompilerParams(vmem_limit_bytes=24 * 2**20),
        cost_estimate=pl.CostEstimate(
            flops=6 * 10**9, bytes_accessed=14 * 10**6, transcendentals=0
        ),
    )(*operands)


class Place:
    def __init__(self):
        ty = lax.axis_index("ty")
        tx = lax.axis_index("tx")
        self.ty, self.tx = ty, tx
        self.y, self.x = ty // 4, ty % 4
        self.z, self.core = tx // 2, tx % 2
        self.up = ((ty + 15) % 16, tx)
        self.down = ((ty + 1) % 16, tx)
        self.left = (ty, (tx + 7) % 8)
        self.right = (ty, (tx + 1) % 8)
        self.other = (ty, self.z * 2 + 1 - self.core)

    def along_y(self, step):
        return (((self.y + step) % 4) * 4 + self.x, self.tx)

    def along_x(self, step):
        return (self.y * 4 + (self.x + step) % 4, self.tx)

    def along_z(self, step):
        return (self.ty, ((self.z + step) % 4) * 2 + self.core)


def greet(devices):
    barrier = pltpu.get_barrier_semaphore()
    for device in devices:
        pl.semaphore_signal(barrier, inc=1, device_id=device, device_id_type=MESH)
    pl.semaphore_wait(barrier, len(devices))


class Copies:
    def __init__(self, send, receive):
        self.send, self.receive, self.used = send, receive, 0

    def start(self, source, target, device):
        copy = pltpu.make_async_remote_copy(
            src_ref=source,
            dst_ref=target,
            send_sem=self.send.at[self.used],
            recv_sem=self.receive.at[self.used],
            device_id=device,
            device_id_type=MESH,
        )
        self.used += 1
        copy.start()
        return copy


def rows_of(zone, chunk):
    return slice(zone.start + chunk * CHUNK, zone.start + (chunk + 1) * CHUNK)


def extend_kernel(
    counts, positions, probe, tile, moduli_far,
    extended, ordered, table, updates, totals,
    moduli, near, weighted, send, receive, arrived,
):
    here = Place()
    copies = Copies(send, receive)
    moduli_copy = pltpu.make_async_copy(moduli_far, moduli, arrived.at[0])
    moduli_copy.start()
    tile_copy = pltpu.make_async_copy(tile, extended.at[:, 0:TILE, 0:TILE], arrived.at[1])
    tile_copy.start()
    near_copy = pltpu.make_async_copy(tile, near.at[:, 0:TILE, 0:TILE], arrived.at[2])
    near_copy.start()
    greet([here.up, here.down, here.left, here.right])
    above, middle = [], []
    for chunk in range(CHUNKS):
        above.append(
            copies.start(
                tile.at[:, rows_of(Z0, chunk), Z0], extended.at[:, rows_of(Z2, chunk), Z0], here.up
            )
        )
    side = copies.start(tile.at[:, :, Z0], near.at[:, 0:TILE, Z2], here.left)
    for half in range(2):
        rows = slice(half * HALF, (half + 1) * HALF)
        low = slice(TILE + half * HALF, TILE + (half + 1) * HALF)
        middle.append(copies.start(tile.at[:, rows, Z1], extended.at[:, low, Z1], here.up))

    first = lax.broadcasted_iota(jnp.int32, (PATCH, PATCH), 0)
    second = lax.broadcasted_iota(jnp.int32, (PATCH, PATCH), 1)
    rows_order = (second == 2 * (first % HALF) + first // HALF).astype(F32).astype(BF16)
    cols_order = (first == 2 * (second % HALF) + second // HALF).astype(F32).astype(BF16)

    def reorder(slot, carry):
        block = moduli[slot]
        block = sum(dot(rows_order, part) for part in thirds(block))
        ordered[slot] = sum(dot(part, cols_order) for part in thirds(block))
        return carry

    write_tables(table)
    write_weighted(weighted, probe)
    totals[...] = jnp.zeros_like(totals)
    near[:, TILE:, :] = jnp.zeros((2, HALF + 8, EXT), F32)
    moduli_copy.wait()
    lax.fori_loop(0, CAP, reorder, 0)
    corners = []
    for chunk in range(CHUNKS):
        above[chunk].wait_recv()
        corners.append(
            copies.start(
                extended.at[:, rows_of(Z2, chunk), Z0],
                extended.at[:, rows_of(Z2, chunk), Z2],
                here.left,
            )
        )
    near_copy.wait()
    side.wait_recv()
    extended[:, 0:TILE, Z2] = near[:, 0:TILE, Z2]

    slots = Slots(counts, positions)

    def turn(index):
        slot, present = slots.at(index)
        row = jnp.clip(slots.row(slot), 0, TILE - HALF)
        col = jnp.clip(slots.col(slot), 0, TILE - 1)
        keep = present.astype(F32)

        def deliver(plane, update):
            updates[index, plane] = update

        return visit(
            slot, row, col, keep, near, probe, weighted, ordered, table, totals, deliver
        )

    def two(pair, carry):
        @pl.when(pair == NEAR // 2)
        def _():
            middle[0].wait_recv()
            for copy in corners[: CHUNKS // 2]:
                copy.wait_recv()
            near[:, TILE : TILE + HALF, :] = extended[:, TILE : TILE + HALF, :]

        together([turn(2 * pair), turn(2 * pair + 1)])
        return carry

    lax.fori_loop(0, EARLY // 2, two, 0)
    tile_copy.wait()
    middle[1].wait_recv()
    for copy in corners[CHUNKS // 2 :]:
        copy.wait_recv()
    for copy in above + middle + corners + [side]:
        copy.wait_send()


def extend(counts, positions, probe, tile, moduli):
    copies = 2 * CHUNKS + 3
    return pl.pallas_call(
        extend_kernel,
        out_shape=(
            jax.ShapeDtypeStruct((2, EXT, EXT), F32),
            jax.ShapeDtypeStruct((CAP, PATCH, PATCH), F32),
            jax.ShapeDtypeStruct((8, PATCH, PATCH), BF16),
            jax.ShapeDtypeStruct((EARLY, 2, PATCH, PATCH), F32),
            jax.ShapeDtypeStruct((3, PATCH, PATCH), F32),
        ),
        in_specs=[SMEM, SMEM, VMEM, HBM, HBM],
        out_specs=(VMEM,) * 5,
        scratch_shapes=[
            pltpu.VMEM((CAP, PATCH, PATCH), F32),
            pltpu.VMEM((2, TILE + HALF + 8, EXT), F32),
            pltpu.VMEM((2, PATCH, PATCH), F32),
            pltpu.SemaphoreType.DMA((copies,)),
            pltpu.SemaphoreType.DMA((copies,)),
            pltpu.SemaphoreType.DMA((3,)),
        ],
        compiler_params=pltpu.CompilerParams(
            vmem_limit_bytes=30 * 2**20, collective_id=0, has_side_effects=True
        ),
        cost_estimate=pl.CostEstimate(
            flops=10**9, bytes_accessed=14 * 10**6, transcendentals=0
        ),
    )(counts, positions, probe, tile, moduli)


class Reduction:
    def __init__(self, here, copies, totals, probe, probe_out, landed, held):
        self.here, self.copies = here, copies
        self.totals, self.probe, self.probe_out = totals, probe, probe_out
        self.land_core, self.land_z, self.land_x, self.land_y = landed
        self.held_core, self.held_z, self.held_x = held
        self.in_flight = []
        self.sent = []

    def launch(self, source, target, device):
        self.in_flight.append(self.copies.start(source, target, device))

    def arrive(self):
        for copy in self.in_flight:
            copy.wait_recv()
        self.sent += self.in_flight
        self.in_flight = []

    def start(self):
        half = pl.ds(pl.multiple_of((1 - self.here.core) * HALF, HALF), HALF)
        self.launch(self.totals.at[:, half, :], self.land_core, self.here.other)

    def after_core(self):
        self.arrive()
        half = pl.ds(pl.multiple_of(self.here.core * HALF, HALF), HALF)
        self.held_core[...] = self.totals[:, half, :] + self.land_core[...]
        for step in (2, 1, 3):
            part = pl.ds(pl.multiple_of(((self.here.z + step) % 4) * 32, 32), 32)
            self.launch(
                self.held_core.at[:, part, :], self.land_z.at[step - 1], self.here.along_z(step)
            )

    def after_z(self):
        self.arrive()
        part = pl.ds(pl.multiple_of(self.here.z * 32, 32), 32)
        self.held_z[...] = (self.held_core[:, part, :] + self.land_z[0]) + (
            self.land_z[1] + self.land_z[2]
        )
        for step in (2, 1, 3):
            part = pl.ds(pl.multiple_of(((self.here.x + step) % 4) * 8, 8), 8)
            self.launch(
                self.held_z.at[:, part, :], self.land_x.at[step - 1], self.here.along_x(step)
            )

    def after_x(self):
        self.arrive()
        part = pl.ds(pl.multiple_of(self.here.x * 8, 8), 8)
        self.held_x[...] = (self.held_z[:, part, :] + self.land_x[0]) + (
            self.land_x[1] + self.land_x[2]
        )
        for step in (2, 1, 3):
            self.launch(self.held_x, self.land_y.at[self.here.y], self.here.along_y(step))
        self.land_y[self.here.y] = self.held_x[...]

    def share(self, rows):
        start = self.here.core * HALF
        if rows < 128:
            start = start + self.here.z * 32
        if rows < 32:
            start = start + self.here.x * 8
        return pl.ds(pl.multiple_of(start, rows), rows)

    def spread(self, rows, device):
        part = self.probe_out.at[:, self.share(rows), :]
        self.launch(part, part, device)

    def after_y(self):
        self.arrive()
        total = (self.land_y[0] + self.land_y[1]) + (self.land_y[2] + self.land_y[3])
        part = self.share(8)
        self.probe_out[:, part, :] = self.probe[:, part, :] + total[0:2] / (
            total[2:3] + tiny_value
        )
        for step in (2, 1, 3):
            self.spread(8, self.here.along_x(step))

    def gather_x(self):
        self.arrive()
        for step in (2, 1, 3):
            self.spread(32, self.here.along_z(step))

    def gather_z(self):
        self.arrive()
        self.spread(128, self.here.other)

    def finish(self):
        self.arrive()
        for copy in self.sent:
            copy.wait_send()


REDUCTION_COPIES = 1 + 3 + 3 + 3 + 3 + 3 + 1


def everyone(here):
    devices = [here.up, here.down, here.left, here.right, here.other]
    for step in range(1, 4):
        devices += [here.along_y(step), here.along_x(step), here.along_z(step)]
    return devices


def exchange_kernel(
    sums, extended, totals, probe, out, probe_out,
    from_left, from_up, from_down, from_right, top, bottom,
    land_core, land_z, land_x, land_y, held_core, held_z, held_x,
    send, receive,
):
    here = Place()
    copies = Copies(send, receive)
    reduction = Reduction(
        here, copies, totals, probe, probe_out,
        (land_core, land_z, land_x, land_y), (held_core, held_z, held_x),
    )
    greet(everyone(here))
    corners, outer, last = [], [], []

    def send_corner(chunk):
        pair = []
        for zone in (Z2, Z0):
            rows = rows_of(zone, chunk)
            pair.append(copies.start(sums.at[:, rows, Z2], from_left.at[:, rows, :], here.right))
        corners.append(pair)

    def take_corner(chunk):
        rows, low = rows_of(Z0, chunk), rows_of(Z2, chunk)
        for copy in corners[chunk]:
            copy.wait_recv()
        bottom[:, rows, :] = sums[:, low, Z0] + from_left[:, low, :]
        top[:, rows, :] = sums[:, rows, Z0] + from_left[:, rows, :]

    def send_outer(chunk):
        rows = rows_of(Z0, chunk)
        down = copies.start(bottom.at[:, rows, :], from_up.at[:, rows, Z0], here.down)
        up = copies.start(top.at[:, rows, :], from_down.at[:, rows, Z0], here.up)
        outer.append((down, up))

    def take_outer(chunk):
        rows, low = rows_of(Z0, chunk), rows_of(Z2, chunk)
        down, up = outer[chunk]
        down.wait_recv()
        out[:, rows, Z0] = extended[:, rows, Z0] + (top[:, rows, :] + from_up[:, rows, Z0])
        last.append(copies.start(out.at[:, rows, Z0], out.at[:, rows, Z2], here.left))
        up.wait_recv()
        out[:, low, Z0] = extended[:, low, Z0] + (bottom[:, rows, :] + from_down[:, rows, Z0])
        last.append(copies.start(out.at[:, low, Z0], out.at[:, low, Z2], here.left))

    reduction.start()
    send_corner(0)
    middle_down = copies.start(sums.at[:, Z2, Z1], from_up.at[:, :, Z1], here.down)
    middle_up = copies.start(sums.at[:, Z0, Z1], from_down.at[:, :, Z1], here.up)
    reduction.after_core()
    for chunk in range(1, CHUNKS):
        send_corner(chunk)
    side_left = copies.start(sums.at[:, Z1, Z0], from_right, here.left)
    side_right = copies.start(sums.at[:, Z1, Z2], from_left.at[:, Z1, :], here.right)
    out[:, Z1, Z1] = extended[:, Z1, Z1] + sums[:, Z1, Z1]
    reduction.after_z()
    take_corner(0)
    send_outer(0)
    middle_down.wait_recv()
    out[:, Z0, Z1] = extended[:, Z0, Z1] + (sums[:, Z0, Z1] + from_up[:, :, Z1])
    middle_up.wait_recv()
    out[:, Z2, Z1] = extended[:, Z2, Z1] + (sums[:, Z2, Z1] + from_down[:, :, Z1])
    reduction.after_x()
    for chunk in range(1, CHUNKS):
        take_corner(chunk)
    reduction.after_y()
    for chunk in range(1, CHUNKS):
        send_outer(chunk)
    side_left.wait_recv()
    out[:, Z1, Z2] = extended[:, Z1, Z2] + (sums[:, Z1, Z2] + from_right[...])
    take_outer(0)
    reduction.gather_x()
    side_right.wait_recv()
    out[:, Z1, Z0] = extended[:, Z1, Z0] + (sums[:, Z1, Z0] + from_left[:, Z1, :])
    take_outer(1)
    reduction.gather_z()
    for chunk in range(2, CHUNKS):
        take_outer(chunk)
    reduction.finish()
    for pair in corners + outer:
        for copy in pair:
            copy.wait_send()
    for copy in [middle_down, middle_up, side_left, side_right]:
        copy.wait_send()
    for copy in last:
        copy.wait()


def reduction_scratch():
    return [
        pltpu.VMEM((3, 128, PATCH), F32),
        pltpu.VMEM((3, 3, 32, PATCH), F32),
        pltpu.VMEM((3, 3, 8, PATCH), F32),
        pltpu.VMEM((4, 3, 8, PATCH), F32),
        pltpu.VMEM((3, 128, PATCH), F32),
        pltpu.VMEM((3, 32, PATCH), F32),
        pltpu.VMEM((3, 8, PATCH), F32),
    ]


def exchange(sums, extended, totals, probe):
    copies = REDUCTION_COPIES + 6 * CHUNKS + 4
    return pl.pallas_call(
        exchange_kernel,
        out_shape=(
            jax.ShapeDtypeStruct((2, EXT, EXT), F32),
            jax.ShapeDtypeStruct((2, PATCH, PATCH), F32),
        ),
        in_specs=[VMEM] * 4,
        out_specs=(VMEM, VMEM),
        scratch_shapes=[
            pltpu.VMEM((2, EXT, PATCH), F32),
            pltpu.VMEM((2, PATCH, TILE), F32),
            pltpu.VMEM((2, PATCH, TILE), F32),
            pltpu.VMEM((2, PATCH, PATCH), F32),
            pltpu.VMEM((2, PATCH, PATCH), F32),
            pltpu.VMEM((2, PATCH, PATCH), F32),
            *reduction_scratch(),
            pltpu.SemaphoreType.DMA((copies,)),
            pltpu.SemaphoreType.DMA((copies,)),
        ],
        compiler_params=pltpu.CompilerParams(
            vmem_limit_bytes=28 * 2**20, collective_id=1, has_side_effects=True
        ),
        cost_estimate=pl.CostEstimate(
            flops=10**9, bytes_accessed=14 * 10**6, transcendentals=0
        ),
    )(sums, extended, totals, probe)


def fold_kernel(
    sums, extended, totals, probe, out, probe_out,
    from_left, from_up, bottom,
    land_core, land_z, land_x, land_y, held_core, held_z, held_x,
    send, receive,
):
    here = Place()
    copies = Copies(send, receive)
    reduction = Reduction(
        here, copies, totals, probe, probe_out,
        (land_core, land_z, land_x, land_y), (held_core, held_z, held_x),
    )
    greet(everyone(here))
    corners, outer = [], []

    def send_corner(chunk):
        rows = rows_of(Z2, chunk)
        corners.append(copies.start(sums.at[:, rows, Z2], from_left.at[:, rows, :], here.right))

    def take_corner(chunk):
        rows, low = rows_of(Z0, chunk), rows_of(Z2, chunk)
        corners[chunk].wait_recv()
        bottom[:, rows, :] = sums[:, low, Z0] + from_left[:, low, :]

    def send_outer(chunk):
        rows = rows_of(Z0, chunk)
        outer.append(copies.start(bottom.at[:, rows, :], from_up.at[:, rows, Z0], here.down))

    reduction.start()
    send_corner(0)
    middle = copies.start(sums.at[:, Z2, Z1], from_up.at[:, :, Z1], here.down)
    reduction.after_core()
    for chunk in range(1, CHUNKS):
        send_corner(chunk)
    side = copies.start(sums.at[:, 0:TILE, Z2], from_left.at[:, 0:TILE, :], here.right)
    out[:, Z1, Z1] = extended[:, Z1, Z1] + sums[:, Z1, Z1]
    reduction.after_z()
    take_corner(0)
    send_outer(0)
    middle.wait_recv()
    out[:, Z0, Z1] = extended[:, Z0, Z1] + (sums[:, Z0, Z1] + from_up[:, :, Z1])
    reduction.after_x()
    for chunk in range(1, CHUNKS):
        take_corner(chunk)
    reduction.after_y()
    for chunk in range(1, CHUNKS):
        send_outer(chunk)
    side.wait_recv()
    out[:, Z1, Z0] = extended[:, Z1, Z0] + (sums[:, Z1, Z0] + from_left[:, Z1, :])
    reduction.gather_x()
    reduction.gather_z()
    for chunk in range(CHUNKS):
        rows = rows_of(Z0, chunk)
        outer[chunk].wait_recv()
        out[:, rows, Z0] = extended[:, rows, Z0] + (
            (sums[:, rows, Z0] + from_left[:, rows, :]) + from_up[:, rows, Z0]
        )
    reduction.finish()
    for copy in corners + outer + [middle, side]:
        copy.wait_send()


def fold(sums, extended, totals, probe):
    copies = REDUCTION_COPIES + 2 * CHUNKS + 2
    return pl.pallas_call(
        fold_kernel,
        out_shape=(
            jax.ShapeDtypeStruct((2, TILE, TILE), F32),
            jax.ShapeDtypeStruct((2, PATCH, PATCH), F32),
        ),
        in_specs=[VMEM] * 4,
        out_specs=(VMEM, VMEM),
        scratch_shapes=[
            pltpu.VMEM((2, EXT, PATCH), F32),
            pltpu.VMEM((2, PATCH, TILE), F32),
            pltpu.VMEM((2, PATCH, PATCH), F32),
            *reduction_scratch(),
            pltpu.SemaphoreType.DMA((copies,)),
            pltpu.SemaphoreType.DMA((copies,)),
        ],
        compiler_params=pltpu.CompilerParams(
            vmem_limit_bytes=22 * 2**20, collective_id=2, has_side_effects=True
        ),
        cost_estimate=pl.CostEstimate(
            flops=10**9, bytes_accessed=14 * 10**6, transcendentals=0
        ),
    )(sums, extended, totals, probe)


def shards(object_field, probe, moduli, positions, counts):
    positions = positions.T
    extended, ordered, table, updates, totals = extend(
        counts,
        positions,
        probe,
        pltpu.with_memory_space_constraint(object_field, pltpu.HBM),
        pltpu.with_memory_space_constraint(moduli, pltpu.HBM),
    )
    sums, totals = run_slots(
        counts, positions, extended, probe, ordered, table, updates, totals
    )
    extended, probe = exchange(sums, extended, totals, probe)
    sums, totals = run_slots(counts, positions, extended, probe, ordered, table)
    return fold(sums, extended, totals, probe)


def solution(mesh):
    return jax.shard_map(
        shards,
        mesh=mesh,
        in_specs=(
            P(None, "ty", "tx"),
            P(),
            P(("ty", "tx"), None, None),
            P(("ty", "tx"), None),
            P(),
        ),
        out_specs=(P(None, "ty", "tx"), P()),
        check_vma=False,
    )
```

```python
import math

import jax
import jax.numpy as jnp
from jax import lax
from jax.experimental import pallas as pl
from jax.experimental.pallas import tpu as pltpu
from jax.sharding import PartitionSpec as P

F32 = jnp.float32
BF16 = jnp.bfloat16
MESH = pl.DeviceIdType.MESH

PATCH = 256
HALF = 128
TILE = 512
EXT = 768
CAP = 12
NEAR = 4
EARLY = 8
CHUNKS = 4
CHUNK = PATCH // CHUNKS
tiny_value = 1e-06
floor_sq = 0.0625

Z0 = slice(0, 256)
Z1 = slice(256, 512)
Z2 = slice(512, 768)


def write_tables(table):
    first = lax.broadcasted_iota(jnp.int32, (HALF, HALF), 0)
    second = lax.broadcasted_iota(jnp.int32, (HALF, HALF), 1)
    for odd in range(2):
        forms = ((first * (2 * second + odd), 1.0), (second * (2 * first + odd), -1.0))
        for k, (step, sign) in enumerate(forms):
            angle = (step % PATCH).astype(F32) * (2.0 * math.pi / PATCH)
            real = jnp.cos(angle) / 16.0
            imag = jnp.sin(angle) * (-sign / 16.0)
            form = jnp.concatenate(
                [jnp.concatenate([real, imag], 1), jnp.concatenate([-imag, real], 1)], 0
            )
            at = 4 * odd + 2 * k
            table[at], table[at + 1] = split(form)


def dot(left, right):
    return jnp.dot(left, right, preferred_element_type=F32)


def split(value):
    high = value.astype(BF16)
    return high, (value - high.astype(F32)).astype(BF16)


def thirds(value):
    high = value.astype(BF16)
    rest = value - high.astype(F32)
    middle = rest.astype(BF16)
    return high, middle, (rest - middle.astype(F32)).astype(BF16)


def right_product(value, table, at):
    high, low = split(value)
    both = dot(jnp.concatenate([high, low], 0), table[at])
    return both[:PATCH] + (both[PATCH:] + dot(high, table[at + 1]))


def left_product(table, at, value):
    high, low = split(value)
    both = dot(jnp.concatenate([table[at], table[at + 1]], 0), high)
    return both[:PATCH] + (both[PATCH:] + dot(table[at], low))


def window(row, col):
    row_at = lax.shift_right_logical(row, 3) * 8
    col_at = lax.shift_right_logical(col, 7) * 128
    sub_shift = row - row_at
    lane_shift = col - col_at
    sub = lax.broadcasted_iota(jnp.int32, (33, 8, 128), 1)
    lane = lax.broadcasted_iota(jnp.int32, (33, 8, 128), 2)
    return row_at, col_at, sub_shift, lane_shift, sub, lane


def gather(ref, plane, row, col):
    row_at, col_at, sub_shift, lane_shift, sub, lane = window(row, col)
    cols = []
    for k in range(3):
        block = ref[plane, pl.ds(row_at, 264), pl.ds(col_at + 128 * k, 128)]
        cols.append(pltpu.roll(block.reshape(33, 8, 128), (128 - lane_shift) & 127, 2))
    parts = []
    for k in range(2):
        block = jnp.where(lane < 128 - lane_shift, cols[k], cols[k + 1])
        block = pltpu.roll(block, (8 - sub_shift) & 7, 1)
        block = jnp.where(sub[:32] < 8 - sub_shift, block[:32], block[1:])
        parts.append(block.reshape(PATCH, 128))
    return jnp.concatenate(parts, 1)


def scatter_add(ref, plane, row, col, update):
    row_at, col_at, sub_shift, lane_shift, sub, lane = window(row, col)
    zeros = jnp.zeros((1, 8, 128), F32)
    parts = []
    for k in range(2):
        block = pltpu.roll(update[:, 128 * k : 128 * k + 128].reshape(32, 8, 128), sub_shift, 1)
        block = jnp.where(
            sub >= sub_shift,
            jnp.concatenate([block, zeros], 0),
            jnp.concatenate([zeros, block], 0),
        )
        parts.append(pltpu.roll(block, lane_shift, 2))
    right = lane >= lane_shift
    cols = [
        jnp.where(right, parts[0], 0.0),
        jnp.where(right, parts[1], parts[0]),
        jnp.where(right, 0.0, parts[1]),
    ]
    for k in range(3):
        place = (plane, pl.ds(row_at, 264), pl.ds(col_at + 128 * k, 128))
        ref[place] += cols[k].reshape(264, 128)


def scaled(wave, modulus):
    real = wave[:HALF]
    imag = wave[HALF:]
    scale = modulus * lax.rsqrt(real * real + imag * imag + floor_sq) - 1.0
    return jnp.concatenate([real * scale, imag * scale], 0)


def visit(slot, row, col, keep, source, probe, weighted, moduli, table, totals, deliver):
    patch_real = gather(source, 0, row, col)
    patch_imag = gather(source, 1, row, col)
    kept_real, kept_imag = patch_real, patch_imag
    if keep is not None:
        kept_real, kept_imag = patch_real * keep, patch_imag * keep
    totals[2] += patch_real * kept_real + patch_imag * kept_imag
    exit_real = probe[0] * patch_real - probe[1] * patch_imag
    exit_imag = probe[0] * patch_imag + probe[1] * patch_real
    even = jnp.concatenate(
        [exit_real[:, :HALF] + exit_real[:, HALF:], exit_imag[:, :HALF] + exit_imag[:, HALF:]], 1
    )
    odd = jnp.concatenate(
        [exit_real[:, :HALF] - exit_real[:, HALF:], exit_imag[:, :HALF] - exit_imag[:, HALF:]], 1
    )
    yield
    even = right_product(even, table, 0)
    odd = right_product(odd, table, 4)
    yield
    real = jnp.concatenate([even[:, :HALF], odd[:, :HALF]], 1)
    imag = jnp.concatenate([even[:, HALF:], odd[:, HALF:]], 1)
    even = jnp.concatenate([real[:HALF] + real[HALF:], imag[:HALF] + imag[HALF:]], 0)
    odd = jnp.concatenate([real[:HALF] - real[HALF:], imag[:HALF] - imag[HALF:]], 0)
    yield
    even = left_product(table, 2, even)
    odd = left_product(table, 6, odd)
    yield
    even = scaled(even, moduli[slot, :HALF])
    odd = scaled(odd, moduli[slot, HALF:])
    yield
    even = left_product(table, 0, even)
    odd = left_product(table, 4, odd)
    yield
    real = jnp.concatenate([even[:HALF] + odd[:HALF], even[:HALF] - odd[:HALF]], 0)
    imag = jnp.concatenate([even[HALF:] + odd[HALF:], even[HALF:] - odd[HALF:]], 0)
    even = jnp.concatenate([real[:, :HALF], imag[:, :HALF]], 1)
    odd = jnp.concatenate([real[:, HALF:], imag[:, HALF:]], 1)
    yield
    even = right_product(even, table, 2)
    odd = right_product(odd, table, 6)
    yield
    delta_real = jnp.concatenate(
        [even[:, :HALF] + odd[:, :HALF], even[:, :HALF] - odd[:, :HALF]], 1
    )
    delta_imag = jnp.concatenate(
        [even[:, HALF:] + odd[:, HALF:], even[:, HALF:] - odd[:, HALF:]], 1
    )
    totals[0] += kept_real * delta_real + kept_imag * delta_imag
    totals[1] += kept_real * delta_imag - kept_imag * delta_real
    yield
    deliver(0, weighted[0] * delta_real + weighted[1] * delta_imag)
    deliver(1, weighted[0] * delta_imag - weighted[1] * delta_real)


def together(turns):
    while turns:
        turns = [turn for turn in turns if next(turn, "end") != "end"]


class Slots:
    def __init__(self, counts, positions):
        self.positions = positions
        self.ty = lax.axis_index("ty")
        self.tx = lax.axis_index("tx")
        self.count = counts[self.ty * lax.axis_size("tx") + self.tx]
        self.place = []
        near, far = jnp.int32(0), jnp.int32(NEAR)
        for slot in range(CAP):
            used = slot < self.count
            takes_near = used & (self.row(slot) <= TILE - PATCH) & (near < NEAR)
            takes_far = used & (self.row(slot) <= TILE - HALF) & (far < EARLY)
            place = jnp.where(takes_near, near, jnp.where(takes_far, far, -1))
            near = near + takes_near.astype(jnp.int32)
            far = far + jnp.where(takes_near, 0, takes_far.astype(jnp.int32))
            self.place.append(place)

    def row(self, slot):
        return self.positions[0, slot] - self.ty * TILE

    def col(self, slot):
        return self.positions[1, slot] - self.tx * TILE

    def at(self, place):
        found, present = jnp.int32(0), jnp.int32(0)
        for slot in range(CAP):
            chosen = self.place[slot] == place
            found = jnp.where(chosen, slot, found)
            present = jnp.where(chosen, 1, present)
        return found, present


def write_weighted(weighted, probe):
    peak = jnp.max(probe[0] * probe[0] + probe[1] * probe[1])
    weighted[...] = probe[...] * (1.0 / (peak + tiny_value))


def slots_kernel(
    first, counts, positions, extended, probe, moduli, table, updates, totals_in,
    sums, totals, weighted, queue,
):
    slots = Slots(counts, positions)
    write_weighted(weighted, probe)
    sums[...] = jnp.zeros_like(sums)

    def turn(slot):
        row, col = slots.row(slot), slots.col(slot)

        def deliver(plane, update):
            scatter_add(sums, plane, row, col, update)

        return visit(
            slot, row, col, None, extended, probe, weighted, moduli, table, totals, deliver
        )

    left = jnp.int32(0)
    if first:
        totals[...] = totals_in[...]

        def add_early(index, carry):
            slot, present = slots.at(index)

            @pl.when(present == 1)
            def _():
                for plane in range(2):
                    update = updates[index, plane]
                    scatter_add(sums, plane, slots.row(slot), slots.col(slot), update)

            return carry

        lax.fori_loop(0, EARLY, add_early, 0)
        for slot in range(CAP):
            queue[left] = slot
            late = (slot < slots.count) & (slots.place[slot] < 0)
            left = left + late.astype(jnp.int32)
        pick = lambda index: queue[index]
    else:
        totals[...] = jnp.zeros_like(totals)
        left = slots.count
        pick = lambda index: index

    def two(pair, carry):
        together([turn(pick(2 * pair)), turn(pick(2 * pair + 1))])
        return carry

    def one(index, carry):
        together([turn(pick(index))])
        return carry

    lax.fori_loop(0, left // 2, two, 0)
    lax.fori_loop(2 * (left // 2), left, one, 0)


VMEM = pl.BlockSpec(memory_space=pltpu.VMEM)
SMEM = pl.BlockSpec(memory_space=pltpu.SMEM)
HBM = pl.BlockSpec(memory_space=pltpu.HBM)


def run_slots(counts, positions, extended, probe, moduli, table, updates=None, totals=None):
    first = updates is not None

    def kernel(*refs):
        refs = list(refs)
        if not first:
            refs[6:6] = [None, None]
        slots_kernel(first, *refs)

    operands = [counts, positions, extended, probe, moduli, table]
    if first:
        operands += [updates, totals]
    return pl.pallas_call(
        kernel,
        out_shape=(
            jax.ShapeDtypeStruct((2, EXT, EXT), F32),
            jax.ShapeDtypeStruct((3, PATCH, PATCH), F32),
        ),
        in_specs=[SMEM, SMEM] + [VMEM] * (len(operands) - 2),
        out_specs=(VMEM, VMEM),
        scratch_shapes=[pltpu.VMEM((2, PATCH, PATCH), F32), pltpu.SMEM((CAP,), jnp.int32)],
        compiler_params=pltpu.CompilerParams(vmem_limit_bytes=24 * 2**20),
        cost_estimate=pl.CostEstimate(
            flops=6 * 10**9, bytes_accessed=14 * 10**6, transcendentals=0
        ),
    )(*operands)


class Place:
    def __init__(self):
        ty = lax.axis_index("ty")
        tx = lax.axis_index("tx")
        self.ty, self.tx = ty, tx
        self.y, self.x = ty // 4, ty % 4
        self.z, self.core = tx // 2, tx % 2
        self.up = ((ty + 15) % 16, tx)
        self.down = ((ty + 1) % 16, tx)
        self.left = (ty, (tx + 7) % 8)
        self.right = (ty, (tx + 1) % 8)
        self.other = (ty, self.z * 2 + 1 - self.core)

    def along_y(self, step):
        return (((self.y + step) % 4) * 4 + self.x, self.tx)

    def along_x(self, step):
        return (self.y * 4 + (self.x + step) % 4, self.tx)

    def along_z(self, step):
        return (self.ty, ((self.z + step) % 4) * 2 + self.core)


def greet(devices):
    barrier = pltpu.get_barrier_semaphore()
    for device in devices:
        pl.semaphore_signal(barrier, inc=1, device_id=device, device_id_type=MESH)
    pl.semaphore_wait(barrier, len(devices))


class Copies:
    def __init__(self, send, receive):
        self.send, self.receive, self.used = send, receive, 0

    def make(self, source, target, device):
        copy = pltpu.make_async_remote_copy(
            src_ref=source,
            dst_ref=target,
            send_sem=self.send.at[self.used],
            recv_sem=self.receive.at[self.used],
            device_id=device,
            device_id_type=MESH,
        )
        self.used += 1
        return copy

    def start(self, source, target, device):
        copy = self.make(source, target, device)
        copy.start()
        return copy


def rows_of(zone, chunk):
    return slice(zone.start + chunk * CHUNK, zone.start + (chunk + 1) * CHUNK)


def extend_kernel(
    counts, positions, probe_far, tile, moduli_far,
    extended, ordered, table, updates, totals,
    moduli, near, probe, weighted, send, receive, arrived,
):
    here = Place()
    copies = Copies(send, receive)
    moduli_copy = pltpu.make_async_copy(moduli_far, moduli, arrived.at[0])
    moduli_copy.start()
    tile_copy = pltpu.make_async_copy(tile, extended.at[:, 0:TILE, 0:TILE], arrived.at[1])
    tile_copy.start()
    near_copy = pltpu.make_async_copy(tile, near.at[:, 0:TILE, 0:TILE], arrived.at[2])
    near_copy.start()
    probe_copy = pltpu.make_async_copy(probe_far, probe, arrived.at[3])
    probe_copy.start()
    greet([here.up, here.down, here.left, here.right])
    above, middle = [], []
    for chunk in range(CHUNKS):
        above.append(
            copies.start(
                tile.at[:, rows_of(Z0, chunk), Z0], extended.at[:, rows_of(Z2, chunk), Z0], here.up
            )
        )
    side = copies.start(tile.at[:, :, Z0], near.at[:, 0:TILE, Z2], here.left)
    for half in range(2):
        rows = slice(half * HALF, (half + 1) * HALF)
        low = slice(TILE + half * HALF, TILE + (half + 1) * HALF)
        middle.append(copies.start(tile.at[:, rows, Z1], extended.at[:, low, Z1], here.up))

    first = lax.broadcasted_iota(jnp.int32, (PATCH, PATCH), 0)
    second = lax.broadcasted_iota(jnp.int32, (PATCH, PATCH), 1)
    rows_order = (second == 2 * (first % HALF) + first // HALF).astype(F32).astype(BF16)
    cols_order = (first == 2 * (second % HALF) + second // HALF).astype(F32).astype(BF16)

    def reorder(slot, carry):
        block = moduli[slot]
        block = sum(dot(rows_order, part) for part in thirds(block))
        ordered[slot] = sum(dot(part, cols_order) for part in thirds(block))
        return carry

    write_tables(table)
    probe_copy.wait()
    write_weighted(weighted, probe)
    totals[...] = jnp.zeros_like(totals)
    near[:, TILE:, :] = jnp.zeros((2, HALF + 8, EXT), F32)
    moduli_copy.wait()
    lax.fori_loop(0, CAP, reorder, 0)
    corners = []
    for chunk in range(CHUNKS):
        above[chunk].wait_recv()
        corners.append(
            copies.start(
                extended.at[:, rows_of(Z2, chunk), Z0],
                extended.at[:, rows_of(Z2, chunk), Z2],
                here.left,
            )
        )
    near_copy.wait()
    side.wait_recv()
    extended[:, 0:TILE, Z2] = near[:, 0:TILE, Z2]

    slots = Slots(counts, positions)

    def turn(index):
        slot, present = slots.at(index)
        row = jnp.clip(slots.row(slot), 0, TILE - HALF)
        col = jnp.clip(slots.col(slot), 0, TILE - 1)
        keep = present.astype(F32)

        def deliver(plane, update):
            updates[index, plane] = update

        return visit(
            slot, row, col, keep, near, probe, weighted, ordered, table, totals, deliver
        )

    def two(pair, carry):
        @pl.when(pair == NEAR // 2)
        def _():
            middle[0].wait_recv()
            for copy in corners[: CHUNKS // 2]:
                copy.wait_recv()
            near[:, TILE : TILE + HALF, :] = extended[:, TILE : TILE + HALF, :]

        together([turn(2 * pair), turn(2 * pair + 1)])
        return carry

    lax.fori_loop(0, EARLY // 2, two, 0)
    tile_copy.wait()
    middle[1].wait_recv()
    for copy in corners[CHUNKS // 2 :]:
        copy.wait_recv()
    for copy in above + middle + corners + [side]:
        copy.wait_send()


def extend(counts, positions, probe, tile, moduli):
    copies = 2 * CHUNKS + 3
    return pl.pallas_call(
        extend_kernel,
        out_shape=(
            jax.ShapeDtypeStruct((2, EXT, EXT), F32),
            jax.ShapeDtypeStruct((CAP, PATCH, PATCH), F32),
            jax.ShapeDtypeStruct((8, PATCH, PATCH), BF16),
            jax.ShapeDtypeStruct((EARLY, 2, PATCH, PATCH), F32),
            jax.ShapeDtypeStruct((3, PATCH, PATCH), F32),
        ),
        in_specs=[SMEM, SMEM, HBM, HBM, HBM],
        out_specs=(VMEM,) * 5,
        scratch_shapes=[
            pltpu.VMEM((CAP, PATCH, PATCH), F32),
            pltpu.VMEM((2, TILE + HALF + 8, EXT), F32),
            pltpu.VMEM((2, PATCH, PATCH), F32),
            pltpu.VMEM((2, PATCH, PATCH), F32),
            pltpu.SemaphoreType.DMA((copies,)),
            pltpu.SemaphoreType.DMA((copies,)),
            pltpu.SemaphoreType.DMA((4,)),
        ],
        compiler_params=pltpu.CompilerParams(
            vmem_limit_bytes=30 * 2**20, collective_id=0, has_side_effects=True
        ),
        cost_estimate=pl.CostEstimate(
            flops=10**9, bytes_accessed=14 * 10**6, transcendentals=0
        ),
    )(counts, positions, probe, tile, moduli)


def is_inner(x):
    return (x == 1) | (x == 2)


class Reduction:
    def __init__(self, here, copies, totals, probe, probe_out, landed, held):
        self.here, self.copies = here, copies
        self.totals, self.probe, self.probe_out = totals, probe, probe_out
        self.land_core, self.land_z, self.land_x, self.land_y = landed
        self.held_core, self.held_z, self.held_x = held
        self.in_flight = []
        self.sent = []

    def launch(self, source, target, device):
        self.in_flight.append(self.copies.start(source, target, device))

    def arrive(self):
        for copy in self.in_flight:
            copy.wait_recv()
        self.sent += self.in_flight
        self.in_flight = []

    def start(self):
        half = pl.ds(pl.multiple_of((1 - self.here.core) * HALF, HALF), HALF)
        self.launch(self.totals.at[:, half, :], self.land_core, self.here.other)

    def after_core(self):
        self.arrive()
        half = pl.ds(pl.multiple_of(self.here.core * HALF, HALF), HALF)
        self.held_core[...] = self.totals[:, half, :] + self.land_core[...]
        for step in (2, 1, 3):
            part = pl.ds(pl.multiple_of(((self.here.z + step) % 4) * 32, 32), 32)
            self.launch(
                self.held_core.at[:, part, :], self.land_z.at[step - 1], self.here.along_z(step)
            )

    def after_z(self):
        self.arrive()
        part = pl.ds(pl.multiple_of(self.here.z * 32, 32), 32)
        self.held_z[...] = (self.held_core[:, part, :] + self.land_z[0]) + (
            self.land_z[1] + self.land_z[2]
        )
        self.to_inner = []
        for step in (2, 1, 3):
            target = (self.here.x + step) % 4
            copy = self.copies.make(
                self.held_z.at[:, self.inner_rows(0, target), :],
                self.land_x.at[step - 1],
                self.here.along_x(step),
            )
            self.to_inner.append((copy, is_inner(target)))
            pl.when(is_inner(target))(copy.start)

    def inner_rows(self, start, x):
        rows = start + (x // 2) * 16
        return pl.ds(pl.multiple_of(rows, 16), 16)

    def after_x(self):
        self.across = [
            self.copies.make(
                self.held_x, self.land_y.at[self.here.y], self.here.along_y(step)
            )
            for step in (2, 1, 3)
        ]

        @pl.when(is_inner(self.here.x))
        def _():
            for copy, _ in self.to_inner:
                copy.wait_recv()
            part = self.inner_rows(0, self.here.x)
            self.held_x[...] = (self.held_z[:, part, :] + self.land_x[0]) + (
                self.land_x[1] + self.land_x[2]
            )
            for copy in self.across:
                copy.start()
            self.land_y[self.here.y] = self.held_x[...]

    def share(self, rows):
        start = self.here.core * HALF
        if rows < 128:
            start = start + self.here.z * 32
        return pl.ds(pl.multiple_of(start, rows), rows)

    def spread(self, rows, device):
        part = self.probe_out.at[:, self.share(rows), :]
        self.launch(part, part, device)

    def after_y(self):
        part = self.inner_rows(self.here.core * HALF + self.here.z * 32, self.here.x)
        updated = self.probe_out.at[:, part, :]
        self.from_inner = [
            self.copies.make(updated, updated, self.here.along_x(step)) for step in (2, 1, 3)
        ]

        @pl.when(is_inner(self.here.x))
        def _():
            for copy in self.across:
                copy.wait_recv()
            total = (self.land_y[0] + self.land_y[1]) + (self.land_y[2] + self.land_y[3])
            self.probe_out[:, part, :] = self.probe[:, part, :] + total[0:2] / (
                total[2:3] + tiny_value
            )
            for copy in self.from_inner:
                copy.start()

    def gather_x(self):
        for copy, step in zip(self.from_inner, (2, 1, 3)):
            sender = (self.here.x + 4 - step) % 4
            pl.when(is_inner(sender))(copy.wait_recv)
        for step in (2, 1, 3):
            self.spread(32, self.here.along_z(step))

    def gather_z(self):
        self.arrive()
        self.spread(128, self.here.other)

    def finish(self):
        self.arrive()
        for copy in self.sent:
            copy.wait_send()
        for copy, started in self.to_inner:
            pl.when(started)(copy.wait_send)

        @pl.when(is_inner(self.here.x))
        def _():
            for copy in self.across + self.from_inner:
                copy.wait_send()


REDUCTION_COPIES = 1 + 3 + 3 + 3 + 3 + 3 + 1


def everyone(here):
    devices = [here.up, here.down, here.left, here.right, here.other]
    for step in range(1, 4):
        devices += [here.along_y(step), here.along_x(step), here.along_z(step)]
    return devices


def exchange_kernel(
    sums, extended, totals, probe, out, probe_out,
    from_left, from_up, from_down, from_right, top, bottom,
    land_core, land_z, land_x, land_y, held_core, held_z, held_x,
    send, receive,
):
    here = Place()
    copies = Copies(send, receive)
    reduction = Reduction(
        here, copies, totals, probe, probe_out,
        (land_core, land_z, land_x, land_y), (held_core, held_z, held_x),
    )
    greet(everyone(here))
    corners, outer, middle, last = [], [], [], []

    def send_corner(chunk):
        pair = []
        for zone in (Z2, Z0):
            rows = rows_of(zone, chunk)
            pair.append(copies.start(sums.at[:, rows, Z2], from_left.at[:, rows, :], here.right))
        corners.append(pair)

    def take_corner(chunk):
        rows, low = rows_of(Z0, chunk), rows_of(Z2, chunk)
        for copy in corners[chunk]:
            copy.wait_recv()
        bottom[:, rows, :] = sums[:, low, Z0] + from_left[:, low, :]
        top[:, rows, :] = sums[:, rows, Z0] + from_left[:, rows, :]

    def send_outer(chunk):
        rows = rows_of(Z0, chunk)
        down = copies.start(bottom.at[:, rows, :], from_up.at[:, rows, Z0], here.down)
        up = copies.start(top.at[:, rows, :], from_down.at[:, rows, Z0], here.up)
        outer.append((down, up))

    def take_outer(chunk):
        rows, low = rows_of(Z0, chunk), rows_of(Z2, chunk)
        down, up = outer[chunk]
        down.wait_recv()
        out[:, rows, Z0] = extended[:, rows, Z0] + (top[:, rows, :] + from_up[:, rows, Z0])
        last.append(copies.start(out.at[:, rows, Z0], out.at[:, rows, Z2], here.left))
        up.wait_recv()
        out[:, low, Z0] = extended[:, low, Z0] + (bottom[:, rows, :] + from_down[:, rows, Z0])
        last.append(copies.start(out.at[:, low, Z0], out.at[:, low, Z2], here.left))

    def send_middle(chunk):
        rows, low = rows_of(Z0, chunk), rows_of(Z2, chunk)
        down = copies.start(sums.at[:, low, Z1], from_up.at[:, rows, Z1], here.down)
        up = copies.start(sums.at[:, rows, Z1], from_down.at[:, rows, Z1], here.up)
        middle.append((down, up))

    def take_middle(chunk):
        rows, low = rows_of(Z0, chunk), rows_of(Z2, chunk)
        down, up = middle[chunk]
        down.wait_recv()
        out[:, rows, Z1] = extended[:, rows, Z1] + (sums[:, rows, Z1] + from_up[:, rows, Z1])
        up.wait_recv()
        out[:, low, Z1] = extended[:, low, Z1] + (sums[:, low, Z1] + from_down[:, rows, Z1])

    reduction.start()
    send_corner(0)
    for chunk in range(3):
        send_middle(chunk)
    reduction.after_core()
    for chunk in range(1, CHUNKS):
        send_corner(chunk)
    side_left = copies.start(sums.at[:, Z1, Z0], from_right, here.left)
    side_right = copies.start(sums.at[:, Z1, Z2], from_left.at[:, Z1, :], here.right)
    out[:, Z1, Z1] = extended[:, Z1, Z1] + sums[:, Z1, Z1]
    take_corner(0)
    send_outer(0)
    reduction.after_z()
    take_corner(1)
    send_outer(1)
    reduction.after_x()
    take_outer(0)
    take_corner(2)
    reduction.after_y()
    send_outer(2)
    take_corner(3)
    send_outer(3)
    send_middle(3)
    take_outer(1)
    side_left.wait_recv()
    out[:, Z1, Z2] = extended[:, Z1, Z2] + (sums[:, Z1, Z2] + from_right[...])
    reduction.gather_x()
    for chunk in range(3):
        take_middle(chunk)
    take_outer(2)
    side_right.wait_recv()
    out[:, Z1, Z0] = extended[:, Z1, Z0] + (sums[:, Z1, Z0] + from_left[:, Z1, :])
    reduction.gather_z()
    take_outer(3)
    take_middle(3)
    reduction.finish()
    for pair in corners + outer + middle:
        for copy in pair:
            copy.wait_send()
    for copy in [side_left, side_right]:
        copy.wait_send()
    for copy in last:
        copy.wait()


def reduction_scratch():
    return [
        pltpu.VMEM((3, 128, PATCH), F32),
        pltpu.VMEM((3, 3, 32, PATCH), F32),
        pltpu.VMEM((3, 3, 16, PATCH), F32),
        pltpu.VMEM((4, 3, 16, PATCH), F32),
        pltpu.VMEM((3, 128, PATCH), F32),
        pltpu.VMEM((3, 32, PATCH), F32),
        pltpu.VMEM((3, 16, PATCH), F32),
    ]


def exchange(sums, extended, totals, probe):
    copies = REDUCTION_COPIES + 8 * CHUNKS + 2
    return pl.pallas_call(
        exchange_kernel,
        out_shape=(
            jax.ShapeDtypeStruct((2, EXT, EXT), F32),
            jax.ShapeDtypeStruct((2, PATCH, PATCH), F32),
        ),
        in_specs=[VMEM] * 4,
        out_specs=(VMEM, VMEM),
        scratch_shapes=[
            pltpu.VMEM((2, EXT, PATCH), F32),
            pltpu.VMEM((2, PATCH, TILE), F32),
            pltpu.VMEM((2, PATCH, TILE), F32),
            pltpu.VMEM((2, PATCH, PATCH), F32),
            pltpu.VMEM((2, PATCH, PATCH), F32),
            pltpu.VMEM((2, PATCH, PATCH), F32),
            *reduction_scratch(),
            pltpu.SemaphoreType.DMA((copies,)),
            pltpu.SemaphoreType.DMA((copies,)),
        ],
        compiler_params=pltpu.CompilerParams(
            vmem_limit_bytes=28 * 2**20, collective_id=1, has_side_effects=True
        ),
        cost_estimate=pl.CostEstimate(
            flops=10**9, bytes_accessed=14 * 10**6, transcendentals=0
        ),
    )(sums, extended, totals, probe)


def fold_kernel(
    sums, extended, totals, probe, out, probe_out,
    from_left, from_up, bottom,
    land_core, land_z, land_x, land_y, held_core, held_z, held_x,
    send, receive,
):
    here = Place()
    copies = Copies(send, receive)
    reduction = Reduction(
        here, copies, totals, probe, probe_out,
        (land_core, land_z, land_x, land_y), (held_core, held_z, held_x),
    )
    greet(everyone(here))
    corners, outer = [], []

    def send_corner(chunk):
        rows = rows_of(Z2, chunk)
        corners.append(copies.start(sums.at[:, rows, Z2], from_left.at[:, rows, :], here.right))

    def take_corner(chunk):
        rows, low = rows_of(Z0, chunk), rows_of(Z2, chunk)
        corners[chunk].wait_recv()
        bottom[:, rows, :] = sums[:, low, Z0] + from_left[:, low, :]

    def send_outer(chunk):
        rows = rows_of(Z0, chunk)
        outer.append(copies.start(bottom.at[:, rows, :], from_up.at[:, rows, Z0], here.down))

    reduction.start()
    send_corner(0)
    middle = copies.start(sums.at[:, Z2, Z1], from_up.at[:, :, Z1], here.down)
    reduction.after_core()
    for chunk in range(1, CHUNKS):
        send_corner(chunk)
    side = copies.start(sums.at[:, 0:TILE, Z2], from_left.at[:, 0:TILE, :], here.right)
    out[:, Z1, Z1] = extended[:, Z1, Z1] + sums[:, Z1, Z1]
    reduction.after_z()
    for chunk in range(2):
        take_corner(chunk)
        send_outer(chunk)
    middle.wait_recv()
    out[:, Z0, Z1] = extended[:, Z0, Z1] + (sums[:, Z0, Z1] + from_up[:, :, Z1])
    reduction.after_x()
    for chunk in range(2, CHUNKS):
        take_corner(chunk)
    reduction.after_y()
    for chunk in range(2, CHUNKS):
        send_outer(chunk)
    side.wait_recv()
    out[:, Z1, Z0] = extended[:, Z1, Z0] + (sums[:, Z1, Z0] + from_left[:, Z1, :])
    reduction.gather_x()
    reduction.gather_z()
    for chunk in range(CHUNKS):
        rows = rows_of(Z0, chunk)
        outer[chunk].wait_recv()
        out[:, rows, Z0] = extended[:, rows, Z0] + (
            (sums[:, rows, Z0] + from_left[:, rows, :]) + from_up[:, rows, Z0]
        )
    reduction.finish()
    for copy in corners + outer + [middle, side]:
        copy.wait_send()


def fold(sums, extended, totals, probe):
    copies = REDUCTION_COPIES + 2 * CHUNKS + 2
    return pl.pallas_call(
        fold_kernel,
        out_shape=(
            jax.ShapeDtypeStruct((2, TILE, TILE), F32),
            jax.ShapeDtypeStruct((2, PATCH, PATCH), F32),
        ),
        in_specs=[VMEM] * 4,
        out_specs=(VMEM, VMEM),
        scratch_shapes=[
            pltpu.VMEM((2, EXT, PATCH), F32),
            pltpu.VMEM((2, PATCH, TILE), F32),
            pltpu.VMEM((2, PATCH, PATCH), F32),
            *reduction_scratch(),
            pltpu.SemaphoreType.DMA((copies,)),
            pltpu.SemaphoreType.DMA((copies,)),
        ],
        compiler_params=pltpu.CompilerParams(
            vmem_limit_bytes=22 * 2**20, collective_id=2, has_side_effects=True
        ),
        cost_estimate=pl.CostEstimate(
            flops=10**9, bytes_accessed=14 * 10**6, transcendentals=0
        ),
    )(sums, extended, totals, probe)


def publish_kernel(tile, probe, tile_out, probe_out, done):
    copies = [
        pltpu.make_async_copy(tile, tile_out, done.at[0]),
        pltpu.make_async_copy(probe, probe_out, done.at[1]),
    ]
    for copy in copies:
        copy.start()
    for copy in copies:
        copy.wait()


def publish(tile, probe):
    return pl.pallas_call(
        publish_kernel,
        out_shape=(
            jax.ShapeDtypeStruct(tile.shape, tile.dtype),
            jax.ShapeDtypeStruct(probe.shape, probe.dtype),
        ),
        in_specs=[VMEM, VMEM],
        out_specs=(HBM, HBM),
        scratch_shapes=[pltpu.SemaphoreType.DMA((2,))],
        compiler_params=pltpu.CompilerParams(vmem_limit_bytes=8 * 2**20),
    )(tile, probe)


def shards(object_field, probe, moduli, positions, counts):
    positions = positions.T
    extended, ordered, table, updates, totals = extend(
        counts,
        positions,
        pltpu.with_memory_space_constraint(probe, pltpu.HBM),
        pltpu.with_memory_space_constraint(object_field, pltpu.HBM),
        pltpu.with_memory_space_constraint(moduli, pltpu.HBM),
    )
    sums, totals = run_slots(
        counts, positions, extended, probe, ordered, table, updates, totals
    )
    extended, probe = exchange(sums, extended, totals, probe)
    sums, totals = run_slots(counts, positions, extended, probe, ordered, table)
    return publish(*fold(sums, extended, totals, probe))


def solution(mesh):
    return jax.shard_map(
        shards,
        mesh=mesh,
        in_specs=(
            P(None, "ty", "tx"),
            P(),
            P(("ty", "tx"), None, None),
            P(("ty", "tx"), None),
            P(),
        ),
        out_specs=(P(None, "ty", "tx"), P()),
        check_vma=False,
    )
```

```python
import math

import jax
import jax.numpy as jnp
from jax import lax
from jax.experimental import pallas as pl
from jax.experimental.pallas import tpu as pltpu
from jax.sharding import PartitionSpec as P

F32 = jnp.float32
BF16 = jnp.bfloat16
MESH = pl.DeviceIdType.MESH

PATCH = 256
HALF = 128
QUARTER = 64
TILE = 512
EXT = 768
CAP = 12
NEAR = 4
EARLY = 8
CHUNKS = 4
CHUNK = PATCH // CHUNKS
tiny_value = 1e-06
floor_sq = 0.0625

Z0 = slice(0, 256)
Z1 = slice(256, 512)
Z2 = slice(512, 768)


def write_tables(table):
    first = lax.broadcasted_iota(jnp.int32, (HALF, HALF), 0)
    second = lax.broadcasted_iota(jnp.int32, (HALF, HALF), 1)
    for odd in range(2):
        forms = ((first * (2 * second + odd), 1.0), (second * (2 * first + odd), -1.0))
        for k, (step, sign) in enumerate(forms):
            angle = (step % PATCH).astype(F32) * (2.0 * math.pi / PATCH)
            real = jnp.cos(angle) / 16.0
            imag = jnp.sin(angle) * (-sign / 16.0)
            form = jnp.concatenate(
                [jnp.concatenate([real, imag], 1), jnp.concatenate([-imag, real], 1)], 0
            )
            at = 4 * odd + 2 * k
            table[at], table[at + 1] = split(form)
    for part in range(4):
        for k, (point, wave) in enumerate(((second, first), (first, second))):
            step = (point % QUARTER) * (4 * (wave % QUARTER) + part)
            step = step + QUARTER * (wave // QUARTER - point // QUARTER)
            angle = ((step + 2 * PATCH) % PATCH).astype(F32) * (2.0 * math.pi / PATCH)
            high, low = split(jnp.cos(angle) / 16.0)
            table[8 + 4 * k + part] = jnp.concatenate(
                [jnp.concatenate([high, high], 1), jnp.concatenate([low, low], 1)], 0
            )


def dot(left, right):
    return jnp.dot(left, right, preferred_element_type=F32)


def split(value):
    high = value.astype(BF16)
    return high, (value - high.astype(F32)).astype(BF16)


def thirds(value):
    high = value.astype(BF16)
    rest = value - high.astype(F32)
    middle = rest.astype(BF16)
    return high, middle, (rest - middle.astype(F32)).astype(BF16)


def right_product(value, table, at):
    high, low = split(value)
    both = dot(jnp.concatenate([high, low], 0), table[at])
    return both[:PATCH] + (both[PATCH:] + dot(high, table[at + 1]))


def left_product(table, real, imag):
    high, low = split(jnp.concatenate([real, imag], 0))
    both = dot(table, jnp.concatenate([high, low], 0))
    both = both[:HALF] + both[HALF:]
    return both[:QUARTER], both[QUARTER:]


def window(row, col):
    row_at = lax.shift_right_logical(row, 3) * 8
    col_at = lax.shift_right_logical(col, 7) * 128
    sub_shift = row - row_at
    lane_shift = col - col_at
    sub = lax.broadcasted_iota(jnp.int32, (33, 8, 128), 1)
    lane = lax.broadcasted_iota(jnp.int32, (33, 8, 128), 2)
    return row_at, col_at, sub_shift, lane_shift, sub, lane


def gather(ref, plane, row, col):
    row_at, col_at, sub_shift, lane_shift, sub, lane = window(row, col)
    cols = []
    for k in range(3):
        block = ref[plane, pl.ds(row_at, 264), pl.ds(col_at + 128 * k, 128)]
        cols.append(pltpu.roll(block.reshape(33, 8, 128), (128 - lane_shift) & 127, 2))
    parts = []
    for k in range(2):
        block = jnp.where(lane < 128 - lane_shift, cols[k], cols[k + 1])
        block = pltpu.roll(block, (8 - sub_shift) & 7, 1)
        block = jnp.where(sub[:32] < 8 - sub_shift, block[:32], block[1:])
        parts.append(block.reshape(PATCH, 128))
    return jnp.concatenate(parts, 1)


def scatter_add(ref, plane, row, col, update):
    row_at, col_at, sub_shift, lane_shift, sub, lane = window(row, col)
    zeros = jnp.zeros((1, 8, 128), F32)
    parts = []
    for k in range(2):
        block = pltpu.roll(update[:, 128 * k : 128 * k + 128].reshape(32, 8, 128), sub_shift, 1)
        block = jnp.where(
            sub >= sub_shift,
            jnp.concatenate([block, zeros], 0),
            jnp.concatenate([zeros, block], 0),
        )
        parts.append(pltpu.roll(block, lane_shift, 2))
    right = lane >= lane_shift
    cols = [
        jnp.where(right, parts[0], 0.0),
        jnp.where(right, parts[1], parts[0]),
        jnp.where(right, 0.0, parts[1]),
    ]
    for k in range(3):
        place = (plane, pl.ds(row_at, 264), pl.ds(col_at + 128 * k, 128))
        ref[place] += cols[k].reshape(264, 128)


def scaled(real, imag, modulus):
    scale = modulus * lax.rsqrt(real * real + imag * imag + floor_sq) - 1.0
    return real * scale, imag * scale


def butterfly(real, imag):
    return (
        (real[0] + real[2], imag[0] + imag[2]),
        (real[0] - real[2], imag[0] - imag[2]),
        (real[1] + real[3], imag[1] + imag[3]),
        (real[1] - real[3], imag[1] - imag[3]),
    )


def visit(slot, row, col, keep, source, probe, weighted, moduli, table, totals, deliver):
    patch_real = gather(source, 0, row, col)
    patch_imag = gather(source, 1, row, col)
    kept_real, kept_imag = patch_real, patch_imag
    if keep is not None:
        kept_real, kept_imag = patch_real * keep, patch_imag * keep
    totals[2] += patch_real * kept_real + patch_imag * kept_imag
    exit_real = probe[0] * patch_real - probe[1] * patch_imag
    exit_imag = probe[0] * patch_imag + probe[1] * patch_real
    even = jnp.concatenate(
        [exit_real[:, :HALF] + exit_real[:, HALF:], exit_imag[:, :HALF] + exit_imag[:, HALF:]], 1
    )
    odd = jnp.concatenate(
        [exit_real[:, :HALF] - exit_real[:, HALF:], exit_imag[:, :HALF] - exit_imag[:, HALF:]], 1
    )
    yield
    even = right_product(even, table, 0)
    odd = right_product(odd, table, 4)
    yield
    real = jnp.concatenate([even[:, :HALF], odd[:, :HALF]], 1)
    imag = jnp.concatenate([even[:, HALF:], odd[:, HALF:]], 1)
    rows = [slice(QUARTER * k, QUARTER * (k + 1)) for k in range(4)]
    (ar, ai), (br, bi), (cr, ci), (dr, di) = butterfly(
        [real[at] for at in rows], [imag[at] for at in rows]
    )
    parts = [(ar + cr, ai + ci), (br + di, bi - dr), (ar - cr, ai - ci), (br - di, bi + dr)]
    yield
    parts = [left_product(table[8 + k], *part) for k, part in enumerate(parts)]
    yield
    parts = [scaled(*part, moduli[slot, rows[k]]) for k, part in enumerate(parts)]
    yield
    parts = [left_product(table[12 + k], *part) for k, part in enumerate(parts)]
    yield
    (ar, ai), (br, bi), (cr, ci), (dr, di) = butterfly(
        [part[0] for part in parts], [part[1] for part in parts]
    )
    real = jnp.concatenate([ar + cr, br - di, ar - cr, br + di], 0)
    imag = jnp.concatenate([ai + ci, bi + dr, ai - ci, bi - dr], 0)
    even = jnp.concatenate([real[:, :HALF], imag[:, :HALF]], 1)
    odd = jnp.concatenate([real[:, HALF:], imag[:, HALF:]], 1)
    yield
    even = right_product(even, table, 2)
    odd = right_product(odd, table, 6)
    yield
    delta_real = jnp.concatenate(
        [even[:, :HALF] + odd[:, :HALF], even[:, :HALF] - odd[:, :HALF]], 1
    )
    delta_imag = jnp.concatenate(
        [even[:, HALF:] + odd[:, HALF:], even[:, HALF:] - odd[:, HALF:]], 1
    )
    totals[0] += kept_real * delta_real + kept_imag * delta_imag
    totals[1] += kept_real * delta_imag - kept_imag * delta_real
    yield
    deliver(0, weighted[0] * delta_real + weighted[1] * delta_imag)
    deliver(1, weighted[0] * delta_imag - weighted[1] * delta_real)


def together(turns):
    while turns:
        turns = [turn for turn in turns if next(turn, "end") != "end"]


class Slots:
    def __init__(self, counts, positions):
        self.positions = positions
        self.ty = lax.axis_index("ty")
        self.tx = lax.axis_index("tx")
        self.count = counts[self.ty * lax.axis_size("tx") + self.tx]
        self.place = []
        near, far = jnp.int32(0), jnp.int32(NEAR)
        for slot in range(CAP):
            used = slot < self.count
            takes_near = used & (self.row(slot) <= TILE - PATCH) & (near < NEAR)
            takes_far = used & (self.row(slot) <= TILE - HALF) & (far < EARLY)
            place = jnp.where(takes_near, near, jnp.where(takes_far, far, -1))
            near = near + takes_near.astype(jnp.int32)
            far = far + jnp.where(takes_near, 0, takes_far.astype(jnp.int32))
            self.place.append(place)

    def row(self, slot):
        return self.positions[0, slot] - self.ty * TILE

    def col(self, slot):
        return self.positions[1, slot] - self.tx * TILE

    def at(self, place):
        found, present = jnp.int32(0), jnp.int32(0)
        for slot in range(CAP):
            chosen = self.place[slot] == place
            found = jnp.where(chosen, slot, found)
            present = jnp.where(chosen, 1, present)
        return found, present


def write_weighted(weighted, probe):
    peak = jnp.max(probe[0] * probe[0] + probe[1] * probe[1])
    weighted[...] = probe[...] * (1.0 / (peak + tiny_value))


def slots_kernel(
    first, counts, positions, extended, probe, moduli, table, updates, totals_in,
    sums, totals, weighted, queue,
):
    slots = Slots(counts, positions)
    write_weighted(weighted, probe)
    sums[...] = jnp.zeros_like(sums)

    def turn(slot):
        row, col = slots.row(slot), slots.col(slot)

        def deliver(plane, update):
            scatter_add(sums, plane, row, col, update)

        return visit(
            slot, row, col, None, extended, probe, weighted, moduli, table, totals, deliver
        )

    left = jnp.int32(0)
    if first:
        totals[...] = totals_in[...]

        def add_early(index, carry):
            slot, present = slots.at(index)

            @pl.when(present == 1)
            def _():
                for plane in range(2):
                    update = updates[index, plane]
                    scatter_add(sums, plane, slots.row(slot), slots.col(slot), update)

            return carry

        lax.fori_loop(0, EARLY, add_early, 0)
        for slot in range(CAP):
            queue[left] = slot
            late = (slot < slots.count) & (slots.place[slot] < 0)
            left = left + late.astype(jnp.int32)
        pick = lambda index: queue[index]
    else:
        totals[...] = jnp.zeros_like(totals)
        left = slots.count
        pick = lambda index: index

    def two(pair, carry):
        together([turn(pick(2 * pair)), turn(pick(2 * pair + 1))])
        return carry

    def one(index, carry):
        together([turn(pick(index))])
        return carry

    lax.fori_loop(0, left // 2, two, 0)
    lax.fori_loop(2 * (left // 2), left, one, 0)


VMEM = pl.BlockSpec(memory_space=pltpu.VMEM)
SMEM = pl.BlockSpec(memory_space=pltpu.SMEM)
HBM = pl.BlockSpec(memory_space=pltpu.HBM)


def run_slots(counts, positions, extended, probe, moduli, table, updates=None, totals=None):
    first = updates is not None

    def kernel(*refs):
        refs = list(refs)
        if not first:
            refs[6:6] = [None, None]
        slots_kernel(first, *refs)

    operands = [counts, positions, extended, probe, moduli, table]
    if first:
        operands += [updates, totals]
    return pl.pallas_call(
        kernel,
        out_shape=(
            jax.ShapeDtypeStruct((2, EXT, EXT), F32),
            jax.ShapeDtypeStruct((3, PATCH, PATCH), F32),
        ),
        in_specs=[SMEM, SMEM] + [VMEM] * (len(operands) - 2),
        out_specs=(VMEM, VMEM),
        scratch_shapes=[pltpu.VMEM((2, PATCH, PATCH), F32), pltpu.SMEM((CAP,), jnp.int32)],
        compiler_params=pltpu.CompilerParams(vmem_limit_bytes=24 * 2**20),
        cost_estimate=pl.CostEstimate(
            flops=6 * 10**9, bytes_accessed=14 * 10**6, transcendentals=0
        ),
    )(*operands)


class Place:
    def __init__(self):
        ty = lax.axis_index("ty")
        tx = lax.axis_index("tx")
        self.ty, self.tx = ty, tx
        self.y, self.x = ty // 4, ty % 4
        self.z, self.core = tx // 2, tx % 2
        self.up = ((ty + 15) % 16, tx)
        self.down = ((ty + 1) % 16, tx)
        self.left = (ty, (tx + 7) % 8)
        self.right = (ty, (tx + 1) % 8)
        self.other = (ty, self.z * 2 + 1 - self.core)

    def along_y(self, step):
        return (((self.y + step) % 4) * 4 + self.x, self.tx)

    def along_x(self, step):
        return (self.y * 4 + (self.x + step) % 4, self.tx)

    def along_z(self, step):
        return (self.ty, ((self.z + step) % 4) * 2 + self.core)


def greet(devices):
    barrier = pltpu.get_barrier_semaphore()
    for device in devices:
        pl.semaphore_signal(barrier, inc=1, device_id=device, device_id_type=MESH)
    pl.semaphore_wait(barrier, len(devices))


class Copies:
    def __init__(self, send, receive):
        self.send, self.receive, self.used = send, receive, 0

    def make(self, source, target, device):
        copy = pltpu.make_async_remote_copy(
            src_ref=source,
            dst_ref=target,
            send_sem=self.send.at[self.used],
            recv_sem=self.receive.at[self.used],
            device_id=device,
            device_id_type=MESH,
        )
        self.used += 1
        return copy

    def start(self, source, target, device):
        copy = self.make(source, target, device)
        copy.start()
        return copy


def rows_of(zone, chunk):
    return slice(zone.start + chunk * CHUNK, zone.start + (chunk + 1) * CHUNK)


def extend_kernel(
    counts, positions, probe_far, tile, moduli_far,
    extended, ordered, table, updates, totals,
    moduli, near, probe, weighted, send, receive, arrived,
):
    here = Place()
    copies = Copies(send, receive)
    moduli_copy = pltpu.make_async_copy(moduli_far, moduli, arrived.at[0])
    moduli_copy.start()
    tile_copy = pltpu.make_async_copy(tile, extended.at[:, 0:TILE, 0:TILE], arrived.at[1])
    tile_copy.start()
    near_copy = pltpu.make_async_copy(tile, near.at[:, 0:TILE, 0:TILE], arrived.at[2])
    near_copy.start()
    probe_copy = pltpu.make_async_copy(probe_far, probe, arrived.at[3])
    probe_copy.start()
    greet([here.up, here.down, here.left, here.right])
    above, middle = [], []
    for chunk in range(CHUNKS):
        above.append(
            copies.start(
                tile.at[:, rows_of(Z0, chunk), Z0], extended.at[:, rows_of(Z2, chunk), Z0], here.up
            )
        )
    side = copies.start(tile.at[:, :, Z0], near.at[:, 0:TILE, Z2], here.left)
    for half in range(2):
        rows = slice(half * HALF, (half + 1) * HALF)
        low = slice(TILE + half * HALF, TILE + (half + 1) * HALF)
        middle.append(copies.start(tile.at[:, rows, Z1], extended.at[:, low, Z1], here.up))

    first = lax.broadcasted_iota(jnp.int32, (PATCH, PATCH), 0)
    second = lax.broadcasted_iota(jnp.int32, (PATCH, PATCH), 1)
    rows_order = (second == 4 * (first % QUARTER) + first // QUARTER).astype(F32).astype(BF16)
    cols_order = (first == 2 * (second % HALF) + second // HALF).astype(F32).astype(BF16)

    def reorder(slot, carry):
        block = moduli[slot]
        block = sum(dot(rows_order, part) for part in thirds(block))
        ordered[slot] = sum(dot(part, cols_order) for part in thirds(block))
        return carry

    write_tables(table)
    probe_copy.wait()
    write_weighted(weighted, probe)
    totals[...] = jnp.zeros_like(totals)
    near[:, TILE:, :] = jnp.zeros((2, HALF + 8, EXT), F32)
    moduli_copy.wait()
    lax.fori_loop(0, CAP, reorder, 0)
    corners = []
    for chunk in range(CHUNKS):
        above[chunk].wait_recv()
        corners.append(
            copies.start(
                extended.at[:, rows_of(Z2, chunk), Z0],
                extended.at[:, rows_of(Z2, chunk), Z2],
                here.left,
            )
        )
    near_copy.wait()
    side.wait_recv()
    extended[:, 0:TILE, Z2] = near[:, 0:TILE, Z2]

    slots = Slots(counts, positions)

    def turn(index):
        slot, present = slots.at(index)
        row = jnp.clip(slots.row(slot), 0, TILE - HALF)
        col = jnp.clip(slots.col(slot), 0, TILE - 1)
        keep = present.astype(F32)

        def deliver(plane, update):
            updates[index, plane] = update

        return visit(
            slot, row, col, keep, near, probe, weighted, ordered, table, totals, deliver
        )

    def two(pair, carry):
        @pl.when(pair == NEAR // 2)
        def _():
            middle[0].wait_recv()
            for copy in corners[: CHUNKS // 2]:
                copy.wait_recv()
            near[:, TILE : TILE + HALF, :] = extended[:, TILE : TILE + HALF, :]

        together([turn(2 * pair), turn(2 * pair + 1)])
        return carry

    lax.fori_loop(0, EARLY // 2, two, 0)
    tile_copy.wait()
    middle[1].wait_recv()
    for copy in corners[CHUNKS // 2 :]:
        copy.wait_recv()
    for copy in above + middle + corners + [side]:
        copy.wait_send()


def extend(counts, positions, probe, tile, moduli):
    copies = 2 * CHUNKS + 3
    return pl.pallas_call(
        extend_kernel,
        out_shape=(
            jax.ShapeDtypeStruct((2, EXT, EXT), F32),
            jax.ShapeDtypeStruct((CAP, PATCH, PATCH), F32),
            jax.ShapeDtypeStruct((16, PATCH, PATCH), BF16),
            jax.ShapeDtypeStruct((EARLY, 2, PATCH, PATCH), F32),
            jax.ShapeDtypeStruct((3, PATCH, PATCH), F32),
        ),
        in_specs=[SMEM, SMEM, HBM, HBM, HBM],
        out_specs=(VMEM,) * 5,
        scratch_shapes=[
            pltpu.VMEM((CAP, PATCH, PATCH), F32),
            pltpu.VMEM((2, TILE + HALF + 8, EXT), F32),
            pltpu.VMEM((2, PATCH, PATCH), F32),
            pltpu.VMEM((2, PATCH, PATCH), F32),
            pltpu.SemaphoreType.DMA((copies,)),
            pltpu.SemaphoreType.DMA((copies,)),
            pltpu.SemaphoreType.DMA((4,)),
        ],
        compiler_params=pltpu.CompilerParams(
            vmem_limit_bytes=30 * 2**20, collective_id=0, has_side_effects=True
        ),
        cost_estimate=pl.CostEstimate(
            flops=10**9, bytes_accessed=14 * 10**6, transcendentals=0
        ),
    )(counts, positions, probe, tile, moduli)


def is_inner(x):
    return (x == 1) | (x == 2)


class Reduction:
    def __init__(self, here, copies, totals, probe, probe_out, landed, held):
        self.here, self.copies = here, copies
        self.totals, self.probe, self.probe_out = totals, probe, probe_out
        self.land_core, self.land_z, self.land_x, self.land_y = landed
        self.held_core, self.held_z, self.held_x = held
        self.in_flight = []
        self.sent = []

    def launch(self, source, target, device):
        self.in_flight.append(self.copies.start(source, target, device))

    def arrive(self):
        for copy in self.in_flight:
            copy.wait_recv()
        self.sent += self.in_flight
        self.in_flight = []

    def start(self):
        half = pl.ds(pl.multiple_of((1 - self.here.core) * HALF, HALF), HALF)
        self.launch(self.totals.at[:, half, :], self.land_core, self.here.other)

    def after_core(self):
        self.arrive()
        half = pl.ds(pl.multiple_of(self.here.core * HALF, HALF), HALF)
        self.held_core[...] = self.totals[:, half, :] + self.land_core[...]
        for step in (2, 1, 3):
            part = pl.ds(pl.multiple_of(((self.here.z + step) % 4) * 32, 32), 32)
            self.launch(
                self.held_core.at[:, part, :], self.land_z.at[step - 1], self.here.along_z(step)
            )

    def after_z(self):
        self.arrive()
        part = pl.ds(pl.multiple_of(self.here.z * 32, 32), 32)
        self.held_z[...] = (self.held_core[:, part, :] + self.land_z[0]) + (
            self.land_z[1] + self.land_z[2]
        )
        self.to_inner = []
        for step in (2, 1, 3):
            target = (self.here.x + step) % 4
            copy = self.copies.make(
                self.held_z.at[:, self.inner_rows(0, target), :],
                self.land_x.at[step - 1],
                self.here.along_x(step),
            )
            self.to_inner.append((copy, is_inner(target)))
            pl.when(is_inner(target))(copy.start)

    def inner_rows(self, start, x):
        rows = start + (x // 2) * 16
        return pl.ds(pl.multiple_of(rows, 16), 16)

    def after_x(self):
        self.across = [
            self.copies.make(
                self.held_x, self.land_y.at[self.here.y], self.here.along_y(step)
            )
            for step in (2, 1, 3)
        ]

        @pl.when(is_inner(self.here.x))
        def _():
            for copy, _ in self.to_inner:
                copy.wait_recv()
            part = self.inner_rows(0, self.here.x)
            self.held_x[...] = (self.held_z[:, part, :] + self.land_x[0]) + (
                self.land_x[1] + self.land_x[2]
            )
            for copy in self.across:
                copy.start()
            self.land_y[self.here.y] = self.held_x[...]

    def share(self, rows):
        start = self.here.core * HALF
        if rows < 128:
            start = start + self.here.z * 32
        return pl.ds(pl.multiple_of(start, rows), rows)

    def spread(self, rows, device):
        part = self.probe_out.at[:, self.share(rows), :]
        self.launch(part, part, device)

    def after_y(self):
        part = self.inner_rows(self.here.core * HALF + self.here.z * 32, self.here.x)
        updated = self.probe_out.at[:, part, :]
        self.from_inner = [
            self.copies.make(updated, updated, self.here.along_x(step)) for step in (2, 1, 3)
        ]

        @pl.when(is_inner(self.here.x))
        def _():
            for copy in self.across:
                copy.wait_recv()
            total = (self.land_y[0] + self.land_y[1]) + (self.land_y[2] + self.land_y[3])
            self.probe_out[:, part, :] = self.probe[:, part, :] + total[0:2] / (
                total[2:3] + tiny_value
            )
            for copy in self.from_inner:
                copy.start()

    def gather_x(self):
        for copy, step in zip(self.from_inner, (2, 1, 3)):
            sender = (self.here.x + 4 - step) % 4
            pl.when(is_inner(sender))(copy.wait_recv)
        for step in (2, 1, 3):
            self.spread(32, self.here.along_z(step))

    def gather_z(self):
        self.arrive()
        self.spread(128, self.here.other)

    def finish(self):
        self.arrive()
        for copy in self.sent:
            copy.wait_send()
        for copy, started in self.to_inner:
            pl.when(started)(copy.wait_send)

        @pl.when(is_inner(self.here.x))
        def _():
            for copy in self.across + self.from_inner:
                copy.wait_send()


REDUCTION_COPIES = 1 + 3 + 3 + 3 + 3 + 3 + 1


def everyone(here):
    devices = [here.up, here.down, here.left, here.right, here.other]
    for step in range(1, 4):
        devices += [here.along_y(step), here.along_x(step), here.along_z(step)]
    return devices


def exchange_kernel(
    sums, extended, totals, probe, out, probe_out,
    from_left, from_up, from_down, from_right, top, bottom,
    land_core, land_z, land_x, land_y, held_core, held_z, held_x,
    send, receive,
):
    here = Place()
    copies = Copies(send, receive)
    reduction = Reduction(
        here, copies, totals, probe, probe_out,
        (land_core, land_z, land_x, land_y), (held_core, held_z, held_x),
    )
    greet(everyone(here))
    corners, outer, middle, last = [], [], [], []

    def send_corner(chunk):
        pair = []
        for zone in (Z2, Z0):
            rows = rows_of(zone, chunk)
            pair.append(copies.start(sums.at[:, rows, Z2], from_left.at[:, rows, :], here.right))
        corners.append(pair)

    def take_corner(chunk):
        rows, low = rows_of(Z0, chunk), rows_of(Z2, chunk)
        for copy in corners[chunk]:
            copy.wait_recv()
        bottom[:, rows, :] = sums[:, low, Z0] + from_left[:, low, :]
        top[:, rows, :] = sums[:, rows, Z0] + from_left[:, rows, :]

    def send_outer(chunk):
        rows = rows_of(Z0, chunk)
        down = copies.start(bottom.at[:, rows, :], from_up.at[:, rows, Z0], here.down)
        up = copies.start(top.at[:, rows, :], from_down.at[:, rows, Z0], here.up)
        outer.append((down, up))

    def take_outer(chunk):
        rows, low = rows_of(Z0, chunk), rows_of(Z2, chunk)
        down, up = outer[chunk]
        down.wait_recv()
        out[:, rows, Z0] = extended[:, rows, Z0] + (top[:, rows, :] + from_up[:, rows, Z0])
        last.append(copies.start(out.at[:, rows, Z0], out.at[:, rows, Z2], here.left))
        up.wait_recv()
        out[:, low, Z0] = extended[:, low, Z0] + (bottom[:, rows, :] + from_down[:, rows, Z0])
        last.append(copies.start(out.at[:, low, Z0], out.at[:, low, Z2], here.left))

    def send_middle(chunk):
        rows, low = rows_of(Z0, chunk), rows_of(Z2, chunk)
        down = copies.start(sums.at[:, low, Z1], from_up.at[:, rows, Z1], here.down)
        up = copies.start(sums.at[:, rows, Z1], from_down.at[:, rows, Z1], here.up)
        middle.append((down, up))

    def take_middle(chunk):
        rows, low = rows_of(Z0, chunk), rows_of(Z2, chunk)
        down, up = middle[chunk]
        down.wait_recv()
        out[:, rows, Z1] = extended[:, rows, Z1] + (sums[:, rows, Z1] + from_up[:, rows, Z1])
        up.wait_recv()
        out[:, low, Z1] = extended[:, low, Z1] + (sums[:, low, Z1] + from_down[:, rows, Z1])

    reduction.start()
    send_corner(0)
    for chunk in range(3):
        send_middle(chunk)
    reduction.after_core()
    for chunk in range(1, CHUNKS):
        send_corner(chunk)
    side_left = copies.start(sums.at[:, Z1, Z0], from_right, here.left)
    side_right = copies.start(sums.at[:, Z1, Z2], from_left.at[:, Z1, :], here.right)
    out[:, Z1, Z1] = extended[:, Z1, Z1] + sums[:, Z1, Z1]
    take_corner(0)
    send_outer(0)
    reduction.after_z()
    take_corner(1)
    send_outer(1)
    reduction.after_x()
    take_outer(0)
    take_corner(2)
    reduction.after_y()
    send_outer(2)
    take_corner(3)
    send_outer(3)
    send_middle(3)
    take_outer(1)
    side_left.wait_recv()
    out[:, Z1, Z2] = extended[:, Z1, Z2] + (sums[:, Z1, Z2] + from_right[...])
    reduction.gather_x()
    for chunk in range(3):
        take_middle(chunk)
    take_outer(2)
    side_right.wait_recv()
    out[:, Z1, Z0] = extended[:, Z1, Z0] + (sums[:, Z1, Z0] + from_left[:, Z1, :])
    reduction.gather_z()
    take_outer(3)
    take_middle(3)
    reduction.finish()
    for pair in corners + outer + middle:
        for copy in pair:
            copy.wait_send()
    for copy in [side_left, side_right]:
        copy.wait_send()
    for copy in last:
        copy.wait()


def reduction_scratch():
    return [
        pltpu.VMEM((3, 128, PATCH), F32),
        pltpu.VMEM((3, 3, 32, PATCH), F32),
        pltpu.VMEM((3, 3, 16, PATCH), F32),
        pltpu.VMEM((4, 3, 16, PATCH), F32),
        pltpu.VMEM((3, 128, PATCH), F32),
        pltpu.VMEM((3, 32, PATCH), F32),
        pltpu.VMEM((3, 16, PATCH), F32),
    ]


def exchange(sums, extended, totals, probe):
    copies = REDUCTION_COPIES + 8 * CHUNKS + 2
    return pl.pallas_call(
        exchange_kernel,
        out_shape=(
            jax.ShapeDtypeStruct((2, EXT, EXT), F32),
            jax.ShapeDtypeStruct((2, PATCH, PATCH), F32),
        ),
        in_specs=[VMEM] * 4,
        out_specs=(VMEM, VMEM),
        scratch_shapes=[
            pltpu.VMEM((2, EXT, PATCH), F32),
            pltpu.VMEM((2, PATCH, TILE), F32),
            pltpu.VMEM((2, PATCH, TILE), F32),
            pltpu.VMEM((2, PATCH, PATCH), F32),
            pltpu.VMEM((2, PATCH, PATCH), F32),
            pltpu.VMEM((2, PATCH, PATCH), F32),
            *reduction_scratch(),
            pltpu.SemaphoreType.DMA((copies,)),
            pltpu.SemaphoreType.DMA((copies,)),
        ],
        compiler_params=pltpu.CompilerParams(
            vmem_limit_bytes=28 * 2**20, collective_id=1, has_side_effects=True
        ),
        cost_estimate=pl.CostEstimate(
            flops=10**9, bytes_accessed=14 * 10**6, transcendentals=0
        ),
    )(sums, extended, totals, probe)


def fold_kernel(
    sums, extended, totals, probe, out, probe_out,
    from_left, from_up, bottom,
    land_core, land_z, land_x, land_y, held_core, held_z, held_x,
    send, receive,
):
    here = Place()
    copies = Copies(send, receive)
    reduction = Reduction(
        here, copies, totals, probe, probe_out,
        (land_core, land_z, land_x, land_y), (held_core, held_z, held_x),
    )
    greet(everyone(here))
    corners, outer = [], []

    def send_corner(chunk):
        rows = rows_of(Z2, chunk)
        corners.append(copies.start(sums.at[:, rows, Z2], from_left.at[:, rows, :], here.right))

    def take_corner(chunk):
        rows, low = rows_of(Z0, chunk), rows_of(Z2, chunk)
        corners[chunk].wait_recv()
        bottom[:, rows, :] = sums[:, low, Z0] + from_left[:, low, :]

    def send_outer(chunk):
        rows = rows_of(Z0, chunk)
        outer.append(copies.start(bottom.at[:, rows, :], from_up.at[:, rows, Z0], here.down))

    reduction.start()
    send_corner(0)
    middle = copies.start(sums.at[:, Z2, Z1], from_up.at[:, :, Z1], here.down)
    reduction.after_core()
    for chunk in range(1, CHUNKS):
        send_corner(chunk)
    side = copies.start(sums.at[:, 0:TILE, Z2], from_left.at[:, 0:TILE, :], here.right)
    out[:, Z1, Z1] = extended[:, Z1, Z1] + sums[:, Z1, Z1]
    reduction.after_z()
    for chunk in range(2):
        take_corner(chunk)
        send_outer(chunk)
    middle.wait_recv()
    out[:, Z0, Z1] = extended[:, Z0, Z1] + (sums[:, Z0, Z1] + from_up[:, :, Z1])
    reduction.after_x()
    for chunk in range(2, CHUNKS):
        take_corner(chunk)
    reduction.after_y()
    for chunk in range(2, CHUNKS):
        send_outer(chunk)
    side.wait_recv()
    out[:, Z1, Z0] = extended[:, Z1, Z0] + (sums[:, Z1, Z0] + from_left[:, Z1, :])
    reduction.gather_x()
    reduction.gather_z()
    for chunk in range(CHUNKS):
        rows = rows_of(Z0, chunk)
        outer[chunk].wait_recv()
        out[:, rows, Z0] = extended[:, rows, Z0] + (
            (sums[:, rows, Z0] + from_left[:, rows, :]) + from_up[:, rows, Z0]
        )
    reduction.finish()
    for copy in corners + outer + [middle, side]:
        copy.wait_send()


def fold(sums, extended, totals, probe):
    copies = REDUCTION_COPIES + 2 * CHUNKS + 2
    return pl.pallas_call(
        fold_kernel,
        out_shape=(
            jax.ShapeDtypeStruct((2, TILE, TILE), F32),
            jax.ShapeDtypeStruct((2, PATCH, PATCH), F32),
        ),
        in_specs=[VMEM] * 4,
        out_specs=(VMEM, VMEM),
        scratch_shapes=[
            pltpu.VMEM((2, EXT, PATCH), F32),
            pltpu.VMEM((2, PATCH, TILE), F32),
            pltpu.VMEM((2, PATCH, PATCH), F32),
            *reduction_scratch(),
            pltpu.SemaphoreType.DMA((copies,)),
            pltpu.SemaphoreType.DMA((copies,)),
        ],
        compiler_params=pltpu.CompilerParams(
            vmem_limit_bytes=22 * 2**20, collective_id=2, has_side_effects=True
        ),
        cost_estimate=pl.CostEstimate(
            flops=10**9, bytes_accessed=14 * 10**6, transcendentals=0
        ),
    )(sums, extended, totals, probe)


def publish_kernel(tile, probe, tile_out, probe_out, done):
    copies = [
        pltpu.make_async_copy(tile, tile_out, done.at[0]),
        pltpu.make_async_copy(probe, probe_out, done.at[1]),
    ]
    for copy in copies:
        copy.start()
    for copy in copies:
        copy.wait()


def publish(tile, probe):
    return pl.pallas_call(
        publish_kernel,
        out_shape=(
            jax.ShapeDtypeStruct(tile.shape, tile.dtype),
            jax.ShapeDtypeStruct(probe.shape, probe.dtype),
        ),
        in_specs=[VMEM, VMEM],
        out_specs=(HBM, HBM),
        scratch_shapes=[pltpu.SemaphoreType.DMA((2,))],
        compiler_params=pltpu.CompilerParams(vmem_limit_bytes=8 * 2**20),
    )(tile, probe)


def shards(object_field, probe, moduli, positions, counts):
    positions = positions.T
    extended, ordered, table, updates, totals = extend(
        counts,
        positions,
        pltpu.with_memory_space_constraint(probe, pltpu.HBM),
        pltpu.with_memory_space_constraint(object_field, pltpu.HBM),
        pltpu.with_memory_space_constraint(moduli, pltpu.HBM),
    )
    sums, totals = run_slots(
        counts, positions, extended, probe, ordered, table, updates, totals
    )
    extended, probe = exchange(sums, extended, totals, probe)
    sums, totals = run_slots(counts, positions, extended, probe, ordered, table)
    return publish(*fold(sums, extended, totals, probe))


def solution(mesh):
    return jax.shard_map(
        shards,
        mesh=mesh,
        in_specs=(
            P(None, "ty", "tx"),
            P(),
            P(("ty", "tx"), None, None),
            P(("ty", "tx"), None),
            P(),
        ),
        out_specs=(P(None, "ty", "tx"), P()),
        check_vma=False,
    )
```

```python
import math

import jax
import jax.numpy as jnp
from jax import lax
from jax.experimental import pallas as pl
from jax.experimental.pallas import tpu as pltpu
from jax.sharding import PartitionSpec as P

F32 = jnp.float32
BF16 = jnp.bfloat16
MESH = pl.DeviceIdType.MESH

PATCH = 256
HALF = 128
QUARTER = 64
TILE = 512
EXT = 768
CAP = 12
NEAR = 4
EARLY = 8
CHUNKS = 4
CHUNK = PATCH // CHUNKS
tiny_value = 1e-06
floor_sq = 0.0625

Z0 = slice(0, 256)
Z1 = slice(256, 512)
Z2 = slice(512, 768)


def write_tables(table):
    first = lax.broadcasted_iota(jnp.int32, (HALF, HALF), 0)
    second = lax.broadcasted_iota(jnp.int32, (HALF, HALF), 1)
    for odd in range(2):
        forms = ((first * (2 * second + odd), 1.0), (second * (2 * first + odd), -1.0))
        for k, (step, sign) in enumerate(forms):
            angle = (step % PATCH).astype(F32) * (2.0 * math.pi / PATCH)
            real = jnp.cos(angle) / 16.0
            imag = jnp.sin(angle) * (-sign / 16.0)
            form = jnp.concatenate(
                [jnp.concatenate([real, imag], 1), jnp.concatenate([-imag, real], 1)], 0
            )
            at = 4 * odd + 2 * k
            table[at], table[at + 1] = split(form)
    for part in range(4):
        for k, (point, wave) in enumerate(((second, first), (first, second))):
            step = (point % QUARTER) * (4 * (wave % QUARTER) + part)
            step = step + QUARTER * (wave // QUARTER - point // QUARTER)
            angle = ((step + 2 * PATCH) % PATCH).astype(F32) * (2.0 * math.pi / PATCH)
            high, low = split(jnp.cos(angle) / 16.0)
            table[8 + 4 * k + part] = jnp.concatenate(
                [jnp.concatenate([high, high], 1), jnp.concatenate([low, low], 1)], 0
            )


def dot(left, right):
    return jnp.dot(left, right, preferred_element_type=F32)


def split(value):
    high = value.astype(BF16)
    return high, (value - high.astype(F32)).astype(BF16)


def thirds(value):
    high = value.astype(BF16)
    rest = value - high.astype(F32)
    middle = rest.astype(BF16)
    return high, middle, (rest - middle.astype(F32)).astype(BF16)


def right_product(value, table, at):
    high, low = split(value)
    both = dot(jnp.concatenate([high, low], 0), table[at])
    return both[:PATCH] + (both[PATCH:] + dot(high, table[at + 1]))


def left_product(table, real, imag):
    high, low = split(jnp.concatenate([real, imag], 0))
    both = dot(table, jnp.concatenate([high, low], 0))
    both = both[:HALF] + both[HALF:]
    return both[:QUARTER], both[QUARTER:]


def window(row, col):
    row_at = lax.shift_right_logical(row, 3) * 8
    col_at = lax.shift_right_logical(col, 7) * 128
    sub_shift = row - row_at
    lane_shift = col - col_at
    sub = lax.broadcasted_iota(jnp.int32, (33, 8, 128), 1)
    lane = lax.broadcasted_iota(jnp.int32, (33, 8, 128), 2)
    return row_at, col_at, sub_shift, lane_shift, sub, lane


def gather(ref, plane, row, col):
    row_at, col_at, sub_shift, lane_shift, sub, lane = window(row, col)
    cols = []
    for k in range(3):
        block = ref[plane, pl.ds(row_at, 264), pl.ds(col_at + 128 * k, 128)]
        cols.append(pltpu.roll(block.reshape(33, 8, 128), (128 - lane_shift) & 127, 2))
    parts = []
    for k in range(2):
        block = jnp.where(lane < 128 - lane_shift, cols[k], cols[k + 1])
        block = pltpu.roll(block, (8 - sub_shift) & 7, 1)
        block = jnp.where(sub[:32] < 8 - sub_shift, block[:32], block[1:])
        parts.append(block.reshape(PATCH, 128))
    return jnp.concatenate(parts, 1)


def scatter_add(ref, plane, row, col, update):
    row_at, col_at, sub_shift, lane_shift, sub, lane = window(row, col)
    zeros = jnp.zeros((1, 8, 128), F32)
    parts = []
    for k in range(2):
        block = pltpu.roll(update[:, 128 * k : 128 * k + 128].reshape(32, 8, 128), sub_shift, 1)
        block = jnp.where(
            sub >= sub_shift,
            jnp.concatenate([block, zeros], 0),
            jnp.concatenate([zeros, block], 0),
        )
        parts.append(pltpu.roll(block, lane_shift, 2))
    right = lane >= lane_shift
    cols = [
        jnp.where(right, parts[0], 0.0),
        jnp.where(right, parts[1], parts[0]),
        jnp.where(right, 0.0, parts[1]),
    ]
    for k in range(3):
        place = (plane, pl.ds(row_at, 264), pl.ds(col_at + 128 * k, 128))
        ref[place] += cols[k].reshape(264, 128)


def scaled(real, imag, modulus):
    scale = modulus * lax.rsqrt(real * real + imag * imag + floor_sq) - 1.0
    return real * scale, imag * scale


def butterfly(real, imag):
    return (
        (real[0] + real[2], imag[0] + imag[2]),
        (real[0] - real[2], imag[0] - imag[2]),
        (real[1] + real[3], imag[1] + imag[3]),
        (real[1] - real[3], imag[1] - imag[3]),
    )


def visit(slot, row, col, keep, source, probe, weighted, moduli, table, totals, deliver):
    patch_real = gather(source, 0, row, col)
    patch_imag = gather(source, 1, row, col)
    kept_real, kept_imag = patch_real, patch_imag
    if keep is not None:
        kept_real, kept_imag = patch_real * keep, patch_imag * keep
    totals[2] += patch_real * kept_real + patch_imag * kept_imag
    exit_real = probe[0] * patch_real - probe[1] * patch_imag
    exit_imag = probe[0] * patch_imag + probe[1] * patch_real
    even = jnp.concatenate(
        [exit_real[:, :HALF] + exit_real[:, HALF:], exit_imag[:, :HALF] + exit_imag[:, HALF:]], 1
    )
    odd = jnp.concatenate(
        [exit_real[:, :HALF] - exit_real[:, HALF:], exit_imag[:, :HALF] - exit_imag[:, HALF:]], 1
    )
    yield
    even = right_product(even, table, 0)
    odd = right_product(odd, table, 4)
    yield
    real = jnp.concatenate([even[:, :HALF], odd[:, :HALF]], 1)
    imag = jnp.concatenate([even[:, HALF:], odd[:, HALF:]], 1)
    rows = [slice(QUARTER * k, QUARTER * (k + 1)) for k in range(4)]
    (ar, ai), (br, bi), (cr, ci), (dr, di) = butterfly(
        [real[at] for at in rows], [imag[at] for at in rows]
    )
    parts = [(ar + cr, ai + ci), (br + di, bi - dr), (ar - cr, ai - ci), (br - di, bi + dr)]
    yield
    parts = [left_product(table[8 + k], *part) for k, part in enumerate(parts)]
    yield
    parts = [scaled(*part, moduli[slot, rows[k]]) for k, part in enumerate(parts)]
    yield
    parts = [left_product(table[12 + k], *part) for k, part in enumerate(parts)]
    yield
    (ar, ai), (br, bi), (cr, ci), (dr, di) = butterfly(
        [part[0] for part in parts], [part[1] for part in parts]
    )
    real = jnp.concatenate([ar + cr, br - di, ar - cr, br + di], 0)
    imag = jnp.concatenate([ai + ci, bi + dr, ai - ci, bi - dr], 0)
    even = jnp.concatenate([real[:, :HALF], imag[:, :HALF]], 1)
    odd = jnp.concatenate([real[:, HALF:], imag[:, HALF:]], 1)
    yield
    even = right_product(even, table, 2)
    odd = right_product(odd, table, 6)
    yield
    delta_real = jnp.concatenate(
        [even[:, :HALF] + odd[:, :HALF], even[:, :HALF] - odd[:, :HALF]], 1
    )
    delta_imag = jnp.concatenate(
        [even[:, HALF:] + odd[:, HALF:], even[:, HALF:] - odd[:, HALF:]], 1
    )
    totals[0] += kept_real * delta_real + kept_imag * delta_imag
    totals[1] += kept_real * delta_imag - kept_imag * delta_real
    yield
    deliver(0, weighted[0] * delta_real + weighted[1] * delta_imag)
    deliver(1, weighted[0] * delta_imag - weighted[1] * delta_real)


def together(turns):
    while turns:
        turns = [turn for turn in turns if next(turn, "end") != "end"]


class Slots:
    def __init__(self, counts, positions):
        self.positions = positions
        self.ty = lax.axis_index("ty")
        self.tx = lax.axis_index("tx")
        self.count = counts[self.ty * lax.axis_size("tx") + self.tx]
        self.place = []
        near, far = jnp.int32(0), jnp.int32(NEAR)
        for slot in range(CAP):
            used = slot < self.count
            takes_near = used & (self.row(slot) <= TILE - PATCH) & (near < NEAR)
            takes_far = used & (self.row(slot) <= TILE - HALF) & (far < EARLY)
            place = jnp.where(takes_near, near, jnp.where(takes_far, far, -1))
            near = near + takes_near.astype(jnp.int32)
            far = far + jnp.where(takes_near, 0, takes_far.astype(jnp.int32))
            self.place.append(place)

    def row(self, slot):
        return self.positions[0, slot] - self.ty * TILE

    def col(self, slot):
        return self.positions[1, slot] - self.tx * TILE

    def at(self, place):
        found, present = jnp.int32(0), jnp.int32(0)
        for slot in range(CAP):
            chosen = self.place[slot] == place
            found = jnp.where(chosen, slot, found)
            present = jnp.where(chosen, 1, present)
        return found, present


def write_weighted(weighted, probe):
    peak = jnp.max(probe[0] * probe[0] + probe[1] * probe[1])
    weighted[...] = probe[...] * (1.0 / (peak + tiny_value))


def slots_kernel(
    first, counts, positions, extended, probe, moduli, table, updates, totals_in,
    sums, totals, weighted, queue,
):
    slots = Slots(counts, positions)
    write_weighted(weighted, probe)
    sums[...] = jnp.zeros_like(sums)

    def turn(slot):
        row, col = slots.row(slot), slots.col(slot)

        def deliver(plane, update):
            scatter_add(sums, plane, row, col, update)

        return visit(
            slot, row, col, None, extended, probe, weighted, moduli, table, totals, deliver
        )

    left = jnp.int32(0)
    if first:
        totals[...] = totals_in[...]

        def add_early(index, carry):
            slot, present = slots.at(index)

            @pl.when(present == 1)
            def _():
                for plane in range(2):
                    update = updates[index, plane]
                    scatter_add(sums, plane, slots.row(slot), slots.col(slot), update)

            return carry

        lax.fori_loop(0, EARLY, add_early, 0)
        for slot in range(CAP):
            queue[left] = slot
            late = (slot < slots.count) & (slots.place[slot] < 0)
            left = left + late.astype(jnp.int32)
        pick = lambda index: queue[index]
    else:
        totals[...] = jnp.zeros_like(totals)
        left = slots.count
        pick = lambda index: index

    def two(pair, carry):
        together([turn(pick(2 * pair)), turn(pick(2 * pair + 1))])
        return carry

    def one(index, carry):
        together([turn(pick(index))])
        return carry

    lax.fori_loop(0, left // 2, two, 0)
    lax.fori_loop(2 * (left // 2), left, one, 0)


VMEM = pl.BlockSpec(memory_space=pltpu.VMEM)
SMEM = pl.BlockSpec(memory_space=pltpu.SMEM)
HBM = pl.BlockSpec(memory_space=pltpu.HBM)


def run_slots(counts, positions, extended, probe, moduli, table, updates=None, totals=None):
    first = updates is not None

    def kernel(*refs):
        refs = list(refs)
        if not first:
            refs[6:6] = [None, None]
        slots_kernel(first, *refs)

    operands = [counts, positions, extended, probe, moduli, table]
    if first:
        operands += [updates, totals]
    return pl.pallas_call(
        kernel,
        out_shape=(
            jax.ShapeDtypeStruct((2, EXT, EXT), F32),
            jax.ShapeDtypeStruct((3, PATCH, PATCH), F32),
        ),
        in_specs=[SMEM, SMEM] + [VMEM] * (len(operands) - 2),
        out_specs=(VMEM, VMEM),
        scratch_shapes=[pltpu.VMEM((2, PATCH, PATCH), F32), pltpu.SMEM((CAP,), jnp.int32)],
        compiler_params=pltpu.CompilerParams(vmem_limit_bytes=24 * 2**20),
        cost_estimate=pl.CostEstimate(
            flops=6 * 10**9, bytes_accessed=14 * 10**6, transcendentals=0
        ),
    )(*operands)


class Place:
    def __init__(self):
        ty = lax.axis_index("ty")
        tx = lax.axis_index("tx")
        self.ty, self.tx = ty, tx
        self.y, self.x = ty // 4, ty % 4
        self.z, self.core = tx // 2, tx % 2
        self.up = ((ty + 15) % 16, tx)
        self.down = ((ty + 1) % 16, tx)
        self.left = (ty, (tx + 7) % 8)
        self.right = (ty, (tx + 1) % 8)
        self.other = (ty, self.z * 2 + 1 - self.core)

    def along_y(self, step):
        return (((self.y + step) % 4) * 4 + self.x, self.tx)

    def along_x(self, step):
        return (self.y * 4 + (self.x + step) % 4, self.tx)

    def along_z(self, step):
        return (self.ty, ((self.z + step) % 4) * 2 + self.core)


def greet(devices):
    barrier = pltpu.get_barrier_semaphore()
    for device in devices:
        pl.semaphore_signal(barrier, inc=1, device_id=device, device_id_type=MESH)
    pl.semaphore_wait(barrier, len(devices))


class Copies:
    def __init__(self, send, receive):
        self.send, self.receive, self.used = send, receive, 0

    def make(self, source, target, device):
        copy = pltpu.make_async_remote_copy(
            src_ref=source,
            dst_ref=target,
            send_sem=self.send.at[self.used],
            recv_sem=self.receive.at[self.used],
            device_id=device,
            device_id_type=MESH,
        )
        self.used += 1
        return copy

    def start(self, source, target, device):
        copy = self.make(source, target, device)
        copy.start()
        return copy


def rows_of(zone, chunk):
    return slice(zone.start + chunk * CHUNK, zone.start + (chunk + 1) * CHUNK)


def extend_kernel(
    counts, positions, probe_far, tile, moduli_far,
    extended, ordered, table, updates, totals,
    moduli, near, probe, weighted, send, receive, arrived,
):
    here = Place()
    copies = Copies(send, receive)
    moduli_copy = pltpu.make_async_copy(moduli_far, moduli, arrived.at[0])
    moduli_copy.start()
    tile_copy = pltpu.make_async_copy(tile, extended.at[:, 0:TILE, 0:TILE], arrived.at[1])
    tile_copy.start()
    near_copy = pltpu.make_async_copy(tile, near.at[:, 0:TILE, 0:TILE], arrived.at[2])
    near_copy.start()
    probe_copy = pltpu.make_async_copy(probe_far, probe, arrived.at[3])
    probe_copy.start()
    greet([here.up, here.down, here.left, here.right])
    above, middle = [], []
    for chunk in range(CHUNKS):
        above.append(
            copies.start(
                tile.at[:, rows_of(Z0, chunk), Z0], extended.at[:, rows_of(Z2, chunk), Z0], here.up
            )
        )
    side = copies.start(tile.at[:, :, Z0], near.at[:, 0:TILE, Z2], here.left)
    for half in range(2):
        rows = slice(half * HALF, (half + 1) * HALF)
        low = slice(TILE + half * HALF, TILE + (half + 1) * HALF)
        middle.append(copies.start(tile.at[:, rows, Z1], extended.at[:, low, Z1], here.up))

    first = lax.broadcasted_iota(jnp.int32, (PATCH, PATCH), 0)
    second = lax.broadcasted_iota(jnp.int32, (PATCH, PATCH), 1)
    rows_order = (second == 4 * (first % QUARTER) + first // QUARTER).astype(F32).astype(BF16)
    cols_order = (first == 2 * (second % HALF) + second // HALF).astype(F32).astype(BF16)

    def reorder(slot, carry):
        block = moduli[slot]
        block = sum(dot(rows_order, part) for part in thirds(block))
        ordered[slot] = sum(dot(part, cols_order) for part in thirds(block))
        return carry

    write_tables(table)
    probe_copy.wait()
    write_weighted(weighted, probe)
    totals[...] = jnp.zeros_like(totals)
    near[:, TILE:, :] = jnp.zeros((2, HALF + 8, EXT), F32)
    moduli_copy.wait()
    lax.fori_loop(0, CAP, reorder, 0)
    corners = []
    for chunk in range(CHUNKS):
        above[chunk].wait_recv()
        corners.append(
            copies.start(
                extended.at[:, rows_of(Z2, chunk), Z0],
                extended.at[:, rows_of(Z2, chunk), Z2],
                here.left,
            )
        )
    near_copy.wait()
    side.wait_recv()
    extended[:, 0:TILE, Z2] = near[:, 0:TILE, Z2]

    slots = Slots(counts, positions)

    def turn(index):
        slot, present = slots.at(index)
        row = jnp.clip(slots.row(slot), 0, TILE - HALF)
        col = jnp.clip(slots.col(slot), 0, TILE - 1)
        keep = present.astype(F32)

        def deliver(plane, update):
            updates[index, plane] = update

        return visit(
            slot, row, col, keep, near, probe, weighted, ordered, table, totals, deliver
        )

    def two(pair, carry):
        @pl.when(pair == NEAR // 2)
        def _():
            middle[0].wait_recv()
            for copy in corners[: CHUNKS // 2]:
                copy.wait_recv()
            near[:, TILE : TILE + HALF, :] = extended[:, TILE : TILE + HALF, :]

        together([turn(2 * pair), turn(2 * pair + 1)])
        return carry

    lax.fori_loop(0, EARLY // 2, two, 0)
    tile_copy.wait()
    middle[1].wait_recv()
    for copy in corners[CHUNKS // 2 :]:
        copy.wait_recv()
    for copy in above + middle + corners + [side]:
        copy.wait_send()


def extend(counts, positions, probe, tile, moduli):
    copies = 2 * CHUNKS + 3
    return pl.pallas_call(
        extend_kernel,
        out_shape=(
            jax.ShapeDtypeStruct((2, EXT, EXT), F32),
            jax.ShapeDtypeStruct((CAP, PATCH, PATCH), F32),
            jax.ShapeDtypeStruct((16, PATCH, PATCH), BF16),
            jax.ShapeDtypeStruct((EARLY, 2, PATCH, PATCH), F32),
            jax.ShapeDtypeStruct((3, PATCH, PATCH), F32),
        ),
        in_specs=[SMEM, SMEM, HBM, HBM, HBM],
        out_specs=(VMEM,) * 5,
        scratch_shapes=[
            pltpu.VMEM((CAP, PATCH, PATCH), F32),
            pltpu.VMEM((2, TILE + HALF + 8, EXT), F32),
            pltpu.VMEM((2, PATCH, PATCH), F32),
            pltpu.VMEM((2, PATCH, PATCH), F32),
            pltpu.SemaphoreType.DMA((copies,)),
            pltpu.SemaphoreType.DMA((copies,)),
            pltpu.SemaphoreType.DMA((4,)),
        ],
        compiler_params=pltpu.CompilerParams(
            vmem_limit_bytes=30 * 2**20, collective_id=0, has_side_effects=True
        ),
        cost_estimate=pl.CostEstimate(
            flops=10**9, bytes_accessed=14 * 10**6, transcendentals=0
        ),
    )(counts, positions, probe, tile, moduli)


def is_inner(x):
    return (x == 1) | (x == 2)


class Reduction:
    def __init__(self, here, copies, totals, probe, probe_out, landed, held):
        self.here, self.copies = here, copies
        self.totals, self.probe, self.probe_out = totals, probe, probe_out
        self.land_core, self.land_z, self.land_x, self.land_y = landed
        self.held_core, self.held_z, self.held_x = held
        self.in_flight = []
        self.sent = []

    def launch(self, source, target, device):
        self.in_flight.append(self.copies.start(source, target, device))

    def arrive(self):
        for copy in self.in_flight:
            copy.wait_recv()
        self.sent += self.in_flight
        self.in_flight = []

    def start(self):
        half = pl.ds(pl.multiple_of((1 - self.here.core) * HALF, HALF), HALF)
        self.launch(self.totals.at[:, half, :], self.land_core, self.here.other)

    def after_core(self):
        self.arrive()
        half = pl.ds(pl.multiple_of(self.here.core * HALF, HALF), HALF)
        self.held_core[...] = self.totals[:, half, :] + self.land_core[...]
        for step in (2, 1, 3):
            part = pl.ds(pl.multiple_of(((self.here.z + step) % 4) * 32, 32), 32)
            self.launch(
                self.held_core.at[:, part, :], self.land_z.at[step - 1], self.here.along_z(step)
            )

    def after_z(self):
        self.arrive()
        part = pl.ds(pl.multiple_of(self.here.z * 32, 32), 32)
        self.held_z[...] = (self.held_core[:, part, :] + self.land_z[0]) + (
            self.land_z[1] + self.land_z[2]
        )
        self.to_inner = []
        for step in (2, 1, 3):
            target = (self.here.x + step) % 4
            copy = self.copies.make(
                self.held_z.at[:, self.inner_rows(0, target), :],
                self.land_x.at[step - 1],
                self.here.along_x(step),
            )
            self.to_inner.append((copy, is_inner(target)))
            pl.when(is_inner(target))(copy.start)

    def inner_rows(self, start, x):
        rows = start + (x // 2) * 16
        return pl.ds(pl.multiple_of(rows, 16), 16)

    def after_x(self):
        self.across = [
            self.copies.make(
                self.held_x, self.land_y.at[self.here.y], self.here.along_y(step)
            )
            for step in (2, 1, 3)
        ]

        @pl.when(is_inner(self.here.x))
        def _():
            for copy, _ in self.to_inner:
                copy.wait_recv()
            part = self.inner_rows(0, self.here.x)
            self.held_x[...] = (self.held_z[:, part, :] + self.land_x[0]) + (
                self.land_x[1] + self.land_x[2]
            )
            for copy in self.across:
                copy.start()
            self.land_y[self.here.y] = self.held_x[...]

    def share(self, rows):
        start = self.here.core * HALF
        if rows < 128:
            start = start + self.here.z * 32
        return pl.ds(pl.multiple_of(start, rows), rows)

    def spread(self, rows, device):
        part = self.probe_out.at[:, self.share(rows), :]
        self.launch(part, part, device)

    def after_y(self):
        part = self.inner_rows(self.here.core * HALF + self.here.z * 32, self.here.x)
        updated = self.probe_out.at[:, part, :]
        self.from_inner = [
            self.copies.make(updated, updated, self.here.along_x(step)) for step in (2, 1, 3)
        ]

        @pl.when(is_inner(self.here.x))
        def _():
            for copy in self.across:
                copy.wait_recv()
            total = (self.land_y[0] + self.land_y[1]) + (self.land_y[2] + self.land_y[3])
            self.probe_out[:, part, :] = self.probe[:, part, :] + total[0:2] / (
                total[2:3] + tiny_value
            )
            for copy in self.from_inner:
                copy.start()

    def gather_x(self):
        for copy, step in zip(self.from_inner, (2, 1, 3)):
            sender = (self.here.x + 4 - step) % 4
            pl.when(is_inner(sender))(copy.wait_recv)
        for step in (2, 1, 3):
            self.spread(32, self.here.along_z(step))

    def gather_z(self):
        self.arrive()
        self.spread(128, self.here.other)

    def finish(self):
        self.arrive()
        for copy in self.sent:
            copy.wait_send()
        for copy, started in self.to_inner:
            pl.when(started)(copy.wait_send)

        @pl.when(is_inner(self.here.x))
        def _():
            for copy in self.across + self.from_inner:
                copy.wait_send()


REDUCTION_COPIES = 1 + 3 + 3 + 3 + 3 + 3 + 1


def everyone(here):
    devices = [here.up, here.down, here.left, here.right, here.other]
    for step in range(1, 4):
        devices += [here.along_y(step), here.along_x(step), here.along_z(step)]
    return devices


def exchange_kernel(
    sums, extended, totals, probe, out, probe_out,
    from_side, from_up, from_down, from_right, top, bottom,
    land_core, land_z, land_x, land_y, held_core, held_z, held_x,
    send, receive,
):
    here = Place()
    copies = Copies(send, receive)
    reduction = Reduction(
        here, copies, totals, probe, probe_out,
        (land_core, land_z, land_x, land_y), (held_core, held_z, held_x),
    )
    greet(everyone(here))
    corners, outer, middle, last = [], [], [], []

    def shared(chunk):
        return (Z2, Z0, here.right, here.left) if chunk % 2 == 0 else (Z0, Z2, here.left, here.right)

    def send_corner(chunk):
        given, _, owner, _ = shared(chunk)
        pair = []
        for zone in (Z2, Z0):
            rows = rows_of(zone, chunk)
            pair.append(copies.start(sums.at[:, rows, given], from_side.at[:, rows, :], owner))
        corners.append(pair)

    def take_corner(chunk):
        rows, low = rows_of(Z0, chunk), rows_of(Z2, chunk)
        _, kept, _, _ = shared(chunk)
        for copy in corners[chunk]:
            copy.wait_recv()
        bottom[:, rows, :] = sums[:, low, kept] + from_side[:, low, :]
        top[:, rows, :] = sums[:, rows, kept] + from_side[:, rows, :]

    def send_outer(chunk):
        rows = rows_of(Z0, chunk)
        down = copies.start(bottom.at[:, rows, :], from_up.at[:, rows, Z0], here.down)
        up = copies.start(top.at[:, rows, :], from_down.at[:, rows, Z0], here.up)
        outer.append((down, up))

    def take_outer(chunk):
        rows, low = rows_of(Z0, chunk), rows_of(Z2, chunk)
        given, kept, _, partner = shared(chunk)
        down, up = outer[chunk]
        down.wait_recv()
        out[:, rows, kept] = extended[:, rows, kept] + (top[:, rows, :] + from_up[:, rows, Z0])
        last.append(copies.start(out.at[:, rows, kept], out.at[:, rows, given], partner))
        up.wait_recv()
        out[:, low, kept] = extended[:, low, kept] + (bottom[:, rows, :] + from_down[:, rows, Z0])
        last.append(copies.start(out.at[:, low, kept], out.at[:, low, given], partner))

    def send_middle(chunk):
        rows, low = rows_of(Z0, chunk), rows_of(Z2, chunk)
        down = copies.start(sums.at[:, low, Z1], from_up.at[:, rows, Z1], here.down)
        up = copies.start(sums.at[:, rows, Z1], from_down.at[:, rows, Z1], here.up)
        middle.append((down, up))

    def take_middle(chunk):
        rows, low = rows_of(Z0, chunk), rows_of(Z2, chunk)
        down, up = middle[chunk]
        down.wait_recv()
        out[:, rows, Z1] = extended[:, rows, Z1] + (sums[:, rows, Z1] + from_up[:, rows, Z1])
        up.wait_recv()
        out[:, low, Z1] = extended[:, low, Z1] + (sums[:, low, Z1] + from_down[:, rows, Z1])

    reduction.start()
    send_corner(0)
    send_corner(1)
    for chunk in range(3):
        send_middle(chunk)
    reduction.after_core()
    for chunk in range(2, CHUNKS):
        send_corner(chunk)
    side_left = copies.start(sums.at[:, Z1, Z0], from_right, here.left)
    side_right = copies.start(sums.at[:, Z1, Z2], from_side.at[:, Z1, :], here.right)
    out[:, Z1, Z1] = extended[:, Z1, Z1] + sums[:, Z1, Z1]
    take_corner(0)
    send_outer(0)
    reduction.after_z()
    take_corner(1)
    send_outer(1)
    reduction.after_x()
    take_outer(0)
    take_corner(2)
    send_outer(2)
    take_corner(3)
    reduction.after_y()
    send_outer(3)
    send_middle(3)
    take_outer(1)
    side_left.wait_recv()
    out[:, Z1, Z2] = extended[:, Z1, Z2] + (sums[:, Z1, Z2] + from_right[...])
    reduction.gather_x()
    for chunk in range(3):
        take_middle(chunk)
    take_outer(2)
    side_right.wait_recv()
    out[:, Z1, Z0] = extended[:, Z1, Z0] + (sums[:, Z1, Z0] + from_side[:, Z1, :])
    reduction.gather_z()
    take_outer(3)
    take_middle(3)
    reduction.finish()
    for pair in corners + outer + middle:
        for copy in pair:
            copy.wait_send()
    for copy in [side_left, side_right]:
        copy.wait_send()
    for copy in last:
        copy.wait()


def reduction_scratch():
    return [
        pltpu.VMEM((3, 128, PATCH), F32),
        pltpu.VMEM((3, 3, 32, PATCH), F32),
        pltpu.VMEM((3, 3, 16, PATCH), F32),
        pltpu.VMEM((4, 3, 16, PATCH), F32),
        pltpu.VMEM((3, 128, PATCH), F32),
        pltpu.VMEM((3, 32, PATCH), F32),
        pltpu.VMEM((3, 16, PATCH), F32),
    ]


def exchange(sums, extended, totals, probe):
    copies = REDUCTION_COPIES + 8 * CHUNKS + 2
    return pl.pallas_call(
        exchange_kernel,
        out_shape=(
            jax.ShapeDtypeStruct((2, EXT, EXT), F32),
            jax.ShapeDtypeStruct((2, PATCH, PATCH), F32),
        ),
        in_specs=[VMEM] * 4,
        out_specs=(VMEM, VMEM),
        scratch_shapes=[
            pltpu.VMEM((2, EXT, PATCH), F32),
            pltpu.VMEM((2, PATCH, TILE), F32),
            pltpu.VMEM((2, PATCH, TILE), F32),
            pltpu.VMEM((2, PATCH, PATCH), F32),
            pltpu.VMEM((2, PATCH, PATCH), F32),
            pltpu.VMEM((2, PATCH, PATCH), F32),
            *reduction_scratch(),
            pltpu.SemaphoreType.DMA((copies,)),
            pltpu.SemaphoreType.DMA((copies,)),
        ],
        compiler_params=pltpu.CompilerParams(
            vmem_limit_bytes=28 * 2**20, collective_id=1, has_side_effects=True
        ),
        cost_estimate=pl.CostEstimate(
            flops=10**9, bytes_accessed=14 * 10**6, transcendentals=0
        ),
    )(sums, extended, totals, probe)


def fold_kernel(
    sums, extended, totals, probe, out, probe_out,
    from_left, from_up, bottom,
    land_core, land_z, land_x, land_y, held_core, held_z, held_x,
    send, receive,
):
    here = Place()
    copies = Copies(send, receive)
    reduction = Reduction(
        here, copies, totals, probe, probe_out,
        (land_core, land_z, land_x, land_y), (held_core, held_z, held_x),
    )
    greet(everyone(here))
    corners, outer = [], []

    def send_corner(chunk):
        rows = rows_of(Z2, chunk)
        corners.append(copies.start(sums.at[:, rows, Z2], from_left.at[:, rows, :], here.right))

    def take_corner(chunk):
        rows, low = rows_of(Z0, chunk), rows_of(Z2, chunk)
        corners[chunk].wait_recv()
        bottom[:, rows, :] = sums[:, low, Z0] + from_left[:, low, :]

    def send_outer(chunk):
        rows = rows_of(Z0, chunk)
        outer.append(copies.start(bottom.at[:, rows, :], from_up.at[:, rows, Z0], here.down))

    reduction.start()
    send_corner(0)
    middle = copies.start(sums.at[:, Z2, Z1], from_up.at[:, :, Z1], here.down)
    reduction.after_core()
    for chunk in range(1, CHUNKS):
        send_corner(chunk)
    side = copies.start(sums.at[:, 0:TILE, Z2], from_left.at[:, 0:TILE, :], here.right)
    out[:, Z1, Z1] = extended[:, Z1, Z1] + sums[:, Z1, Z1]
    reduction.after_z()
    for chunk in range(2):
        take_corner(chunk)
        send_outer(chunk)
    middle.wait_recv()
    out[:, Z0, Z1] = extended[:, Z0, Z1] + (sums[:, Z0, Z1] + from_up[:, :, Z1])
    reduction.after_x()
    for chunk in range(2, CHUNKS):
        take_corner(chunk)
    reduction.after_y()
    for chunk in range(2, CHUNKS):
        send_outer(chunk)
    side.wait_recv()
    out[:, Z1, Z0] = extended[:, Z1, Z0] + (sums[:, Z1, Z0] + from_left[:, Z1, :])
    reduction.gather_x()
    reduction.gather_z()
    for chunk in range(CHUNKS):
        rows = rows_of(Z0, chunk)
        outer[chunk].wait_recv()
        out[:, rows, Z0] = extended[:, rows, Z0] + (
            (sums[:, rows, Z0] + from_left[:, rows, :]) + from_up[:, rows, Z0]
        )
    reduction.finish()
    for copy in corners + outer + [middle, side]:
        copy.wait_send()


def fold(sums, extended, totals, probe):
    copies = REDUCTION_COPIES + 2 * CHUNKS + 2
    return pl.pallas_call(
        fold_kernel,
        out_shape=(
            jax.ShapeDtypeStruct((2, TILE, TILE), F32),
            jax.ShapeDtypeStruct((2, PATCH, PATCH), F32),
        ),
        in_specs=[VMEM] * 4,
        out_specs=(VMEM, VMEM),
        scratch_shapes=[
            pltpu.VMEM((2, EXT, PATCH), F32),
            pltpu.VMEM((2, PATCH, TILE), F32),
            pltpu.VMEM((2, PATCH, PATCH), F32),
            *reduction_scratch(),
            pltpu.SemaphoreType.DMA((copies,)),
            pltpu.SemaphoreType.DMA((copies,)),
        ],
        compiler_params=pltpu.CompilerParams(
            vmem_limit_bytes=22 * 2**20, collective_id=2, has_side_effects=True
        ),
        cost_estimate=pl.CostEstimate(
            flops=10**9, bytes_accessed=14 * 10**6, transcendentals=0
        ),
    )(sums, extended, totals, probe)


def publish_kernel(tile, probe, tile_out, probe_out, done):
    copies = [
        pltpu.make_async_copy(tile, tile_out, done.at[0]),
        pltpu.make_async_copy(probe, probe_out, done.at[1]),
    ]
    for copy in copies:
        copy.start()
    for copy in copies:
        copy.wait()


def publish(tile, probe):
    return pl.pallas_call(
        publish_kernel,
        out_shape=(
            jax.ShapeDtypeStruct(tile.shape, tile.dtype),
            jax.ShapeDtypeStruct(probe.shape, probe.dtype),
        ),
        in_specs=[VMEM, VMEM],
        out_specs=(HBM, HBM),
        scratch_shapes=[pltpu.SemaphoreType.DMA((2,))],
        compiler_params=pltpu.CompilerParams(vmem_limit_bytes=8 * 2**20),
    )(tile, probe)


def shards(object_field, probe, moduli, positions, counts):
    positions = positions.T
    extended, ordered, table, updates, totals = extend(
        counts,
        positions,
        pltpu.with_memory_space_constraint(probe, pltpu.HBM),
        pltpu.with_memory_space_constraint(object_field, pltpu.HBM),
        pltpu.with_memory_space_constraint(moduli, pltpu.HBM),
    )
    sums, totals = run_slots(
        counts, positions, extended, probe, ordered, table, updates, totals
    )
    extended, probe = exchange(sums, extended, totals, probe)
    sums, totals = run_slots(counts, positions, extended, probe, ordered, table)
    return publish(*fold(sums, extended, totals, probe))


def solution(mesh):
    return jax.shard_map(
        shards,
        mesh=mesh,
        in_specs=(
            P(None, "ty", "tx"),
            P(),
            P(("ty", "tx"), None, None),
            P(("ty", "tx"), None),
            P(),
        ),
        out_specs=(P(None, "ty", "tx"), P()),
        check_vma=False,
    )
```

```python
import math

import jax
import jax.numpy as jnp
from jax import lax
from jax.experimental import pallas as pl
from jax.experimental.pallas import tpu as pltpu
from jax.sharding import PartitionSpec as P

F32 = jnp.float32
BF16 = jnp.bfloat16
MESH = pl.DeviceIdType.MESH

PATCH = 256
HALF = 128
QUARTER = 64
TILE = 512
EXT = 768
CAP = 12
NEAR = 4
EARLY = 8
CHUNKS = 4
CHUNK = PATCH // CHUNKS
tiny_value = 1e-06
floor_sq = 0.0625

Z0 = slice(0, 256)
Z1 = slice(256, 512)
Z2 = slice(512, 768)


def write_tables(table):
    first = lax.broadcasted_iota(jnp.int32, (HALF, HALF), 0)
    second = lax.broadcasted_iota(jnp.int32, (HALF, HALF), 1)
    for odd in range(2):
        forms = ((first * (2 * second + odd), 1.0), (second * (2 * first + odd), -1.0))
        for k, (step, sign) in enumerate(forms):
            angle = (step % PATCH).astype(F32) * (2.0 * math.pi / PATCH)
            real = jnp.cos(angle) / 16.0
            imag = jnp.sin(angle) * (-sign / 16.0)
            form = jnp.concatenate(
                [jnp.concatenate([real, imag], 1), jnp.concatenate([-imag, real], 1)], 0
            )
            at = 4 * odd + 2 * k
            table[at], table[at + 1] = split(form)
    for part in range(4):
        for k, (point, wave) in enumerate(((second, first), (first, second))):
            step = (point % QUARTER) * (4 * (wave % QUARTER) + part)
            step = step + QUARTER * (wave // QUARTER - point // QUARTER)
            angle = ((step + 2 * PATCH) % PATCH).astype(F32) * (2.0 * math.pi / PATCH)
            high, low = split(jnp.cos(angle) / 16.0)
            table[8 + 4 * k + part] = jnp.concatenate(
                [jnp.concatenate([high, high], 1), jnp.concatenate([low, low], 1)], 0
            )


def dot(left, right):
    return jnp.dot(left, right, preferred_element_type=F32)


def split(value):
    high = value.astype(BF16)
    return high, (value - high.astype(F32)).astype(BF16)


def thirds(value):
    high = value.astype(BF16)
    rest = value - high.astype(F32)
    middle = rest.astype(BF16)
    return high, middle, (rest - middle.astype(F32)).astype(BF16)


def right_product(value, table, at):
    high, low = split(value)
    both = dot(jnp.concatenate([high, low], 0), table[at])
    return both[:PATCH] + (both[PATCH:] + dot(high, table[at + 1]))


def left_product(table, real, imag):
    high, low = split(jnp.concatenate([real, imag], 0))
    both = dot(table, jnp.concatenate([high, low], 0))
    both = both[:HALF] + both[HALF:]
    return both[:QUARTER], both[QUARTER:]


def window(row, col):
    row_at = lax.shift_right_logical(row, 3) * 8
    col_at = lax.shift_right_logical(col, 7) * 128
    sub_shift = row - row_at
    lane_shift = col - col_at
    sub = lax.broadcasted_iota(jnp.int32, (33, 8, 128), 1)
    lane = lax.broadcasted_iota(jnp.int32, (33, 8, 128), 2)
    return row_at, col_at, sub_shift, lane_shift, sub, lane


def gather(ref, plane, row, col):
    row_at, col_at, sub_shift, lane_shift, sub, lane = window(row, col)
    cols = []
    for k in range(3):
        block = ref[plane, pl.ds(row_at, 264), pl.ds(col_at + 128 * k, 128)]
        cols.append(pltpu.roll(block.reshape(33, 8, 128), (128 - lane_shift) & 127, 2))
    parts = []
    for k in range(2):
        block = jnp.where(lane < 128 - lane_shift, cols[k], cols[k + 1])
        block = pltpu.roll(block, (8 - sub_shift) & 7, 1)
        block = jnp.where(sub[:32] < 8 - sub_shift, block[:32], block[1:])
        parts.append(block.reshape(PATCH, 128))
    return jnp.concatenate(parts, 1)


def scatter_add(ref, plane, row, col, update):
    row_at, col_at, sub_shift, lane_shift, sub, lane = window(row, col)
    zeros = jnp.zeros((1, 8, 128), F32)
    parts = []
    for k in range(2):
        block = pltpu.roll(update[:, 128 * k : 128 * k + 128].reshape(32, 8, 128), sub_shift, 1)
        block = jnp.where(
            sub >= sub_shift,
            jnp.concatenate([block, zeros], 0),
            jnp.concatenate([zeros, block], 0),
        )
        parts.append(pltpu.roll(block, lane_shift, 2))
    right = lane >= lane_shift
    cols = [
        jnp.where(right, parts[0], 0.0),
        jnp.where(right, parts[1], parts[0]),
        jnp.where(right, 0.0, parts[1]),
    ]
    for k in range(3):
        place = (plane, pl.ds(row_at, 264), pl.ds(col_at + 128 * k, 128))
        ref[place] += cols[k].reshape(264, 128)


def scaled(real, imag, modulus):
    scale = modulus * lax.rsqrt(real * real + imag * imag + floor_sq) - 1.0
    return real * scale, imag * scale


def butterfly(real, imag):
    return (
        (real[0] + real[2], imag[0] + imag[2]),
        (real[0] - real[2], imag[0] - imag[2]),
        (real[1] + real[3], imag[1] + imag[3]),
        (real[1] - real[3], imag[1] - imag[3]),
    )


def visit(slot, row, col, keep, source, probe, weighted, moduli, table, totals, deliver):
    patch_real = gather(source, 0, row, col)
    patch_imag = gather(source, 1, row, col)
    kept_real, kept_imag = patch_real, patch_imag
    if keep is not None:
        kept_real, kept_imag = patch_real * keep, patch_imag * keep
    totals[2] += patch_real * kept_real + patch_imag * kept_imag
    exit_real = probe[0] * patch_real - probe[1] * patch_imag
    exit_imag = probe[0] * patch_imag + probe[1] * patch_real
    even = jnp.concatenate(
        [exit_real[:, :HALF] + exit_real[:, HALF:], exit_imag[:, :HALF] + exit_imag[:, HALF:]], 1
    )
    odd = jnp.concatenate(
        [exit_real[:, :HALF] - exit_real[:, HALF:], exit_imag[:, :HALF] - exit_imag[:, HALF:]], 1
    )
    yield
    even = right_product(even, table, 0)
    odd = right_product(odd, table, 4)
    yield
    real = jnp.concatenate([even[:, :HALF], odd[:, :HALF]], 1)
    imag = jnp.concatenate([even[:, HALF:], odd[:, HALF:]], 1)
    rows = [slice(QUARTER * k, QUARTER * (k + 1)) for k in range(4)]
    (ar, ai), (br, bi), (cr, ci), (dr, di) = butterfly(
        [real[at] for at in rows], [imag[at] for at in rows]
    )
    parts = [(ar + cr, ai + ci), (br + di, bi - dr), (ar - cr, ai - ci), (br - di, bi + dr)]
    yield
    parts = [left_product(table[8 + k], *part) for k, part in enumerate(parts)]
    yield
    parts = [scaled(*part, moduli[slot, rows[k]]) for k, part in enumerate(parts)]
    yield
    parts = [left_product(table[12 + k], *part) for k, part in enumerate(parts)]
    yield
    (ar, ai), (br, bi), (cr, ci), (dr, di) = butterfly(
        [part[0] for part in parts], [part[1] for part in parts]
    )
    real = jnp.concatenate([ar + cr, br - di, ar - cr, br + di], 0)
    imag = jnp.concatenate([ai + ci, bi + dr, ai - ci, bi - dr], 0)
    even = jnp.concatenate([real[:, :HALF], imag[:, :HALF]], 1)
    odd = jnp.concatenate([real[:, HALF:], imag[:, HALF:]], 1)
    yield
    even = right_product(even, table, 2)
    odd = right_product(odd, table, 6)
    yield
    delta_real = jnp.concatenate(
        [even[:, :HALF] + odd[:, :HALF], even[:, :HALF] - odd[:, :HALF]], 1
    )
    delta_imag = jnp.concatenate(
        [even[:, HALF:] + odd[:, HALF:], even[:, HALF:] - odd[:, HALF:]], 1
    )
    totals[0] += kept_real * delta_real + kept_imag * delta_imag
    totals[1] += kept_real * delta_imag - kept_imag * delta_real
    yield
    deliver(0, weighted[0] * delta_real + weighted[1] * delta_imag)
    deliver(1, weighted[0] * delta_imag - weighted[1] * delta_real)


def together(turns):
    while turns:
        turns = [turn for turn in turns if next(turn, "end") != "end"]


class Slots:
    def __init__(self, counts, positions):
        self.positions = positions
        self.ty = lax.axis_index("ty")
        self.tx = lax.axis_index("tx")
        self.count = counts[self.ty * lax.axis_size("tx") + self.tx]
        self.place = []
        near, far = jnp.int32(0), jnp.int32(NEAR)
        for slot in range(CAP):
            used = slot < self.count
            takes_near = used & (self.row(slot) <= TILE - PATCH) & (near < NEAR)
            takes_far = used & (self.row(slot) <= TILE - HALF) & (far < EARLY)
            place = jnp.where(takes_near, near, jnp.where(takes_far, far, -1))
            near = near + takes_near.astype(jnp.int32)
            far = far + jnp.where(takes_near, 0, takes_far.astype(jnp.int32))
            self.place.append(place)

    def row(self, slot):
        return self.positions[0, slot] - self.ty * TILE

    def col(self, slot):
        return self.positions[1, slot] - self.tx * TILE

    def at(self, place):
        found, present = jnp.int32(0), jnp.int32(0)
        for slot in range(CAP):
            chosen = self.place[slot] == place
            found = jnp.where(chosen, slot, found)
            present = jnp.where(chosen, 1, present)
        return found, present


def write_weighted(weighted, probe):
    peak = jnp.max(probe[0] * probe[0] + probe[1] * probe[1])
    weighted[...] = probe[...] * (1.0 / (peak + tiny_value))


def slots_kernel(
    first, counts, positions, extended, probe, moduli, table, updates, totals_in,
    sums, totals, weighted, queue,
):
    slots = Slots(counts, positions)
    write_weighted(weighted, probe)
    sums[...] = jnp.zeros_like(sums)

    def turn(slot):
        row, col = slots.row(slot), slots.col(slot)

        def deliver(plane, update):
            scatter_add(sums, plane, row, col, update)

        return visit(
            slot, row, col, None, extended, probe, weighted, moduli, table, totals, deliver
        )

    left = jnp.int32(0)
    if first:
        totals[...] = totals_in[...]

        def add_early(index, carry):
            slot, present = slots.at(index)

            @pl.when(present == 1)
            def _():
                for plane in range(2):
                    update = updates[index, plane]
                    scatter_add(sums, plane, slots.row(slot), slots.col(slot), update)

            return carry

        lax.fori_loop(0, EARLY, add_early, 0)
        for slot in range(CAP):
            queue[left] = slot
            late = (slot < slots.count) & (slots.place[slot] < 0)
            left = left + late.astype(jnp.int32)
        pick = lambda index: queue[index]
    else:
        totals[...] = jnp.zeros_like(totals)
        left = slots.count
        pick = lambda index: index

    def two(pair, carry):
        together([turn(pick(2 * pair)), turn(pick(2 * pair + 1))])
        return carry

    def one(index, carry):
        together([turn(pick(index))])
        return carry

    lax.fori_loop(0, left // 2, two, 0)
    lax.fori_loop(2 * (left // 2), left, one, 0)


VMEM = pl.BlockSpec(memory_space=pltpu.VMEM)
SMEM = pl.BlockSpec(memory_space=pltpu.SMEM)
HBM = pl.BlockSpec(memory_space=pltpu.HBM)


def run_slots(counts, positions, extended, probe, moduli, table, updates=None, totals=None):
    first = updates is not None

    def kernel(*refs):
        refs = list(refs)
        if not first:
            refs[6:6] = [None, None]
        slots_kernel(first, *refs)

    operands = [counts, positions, extended, probe, moduli, table]
    if first:
        operands += [updates, totals]
    return pl.pallas_call(
        kernel,
        out_shape=(
            jax.ShapeDtypeStruct((2, EXT, EXT), F32),
            jax.ShapeDtypeStruct((3, PATCH, PATCH), F32),
        ),
        in_specs=[SMEM, SMEM] + [VMEM] * (len(operands) - 2),
        out_specs=(VMEM, VMEM),
        scratch_shapes=[pltpu.VMEM((2, PATCH, PATCH), F32), pltpu.SMEM((CAP,), jnp.int32)],
        compiler_params=pltpu.CompilerParams(vmem_limit_bytes=24 * 2**20),
        cost_estimate=pl.CostEstimate(
            flops=6 * 10**9, bytes_accessed=14 * 10**6, transcendentals=0
        ),
    )(*operands)


class Place:
    def __init__(self):
        ty = lax.axis_index("ty")
        tx = lax.axis_index("tx")
        self.ty, self.tx = ty, tx
        self.y, self.x = ty // 4, ty % 4
        self.z, self.core = tx // 2, tx % 2
        self.up = ((ty + 15) % 16, tx)
        self.down = ((ty + 1) % 16, tx)
        self.left = (ty, (tx + 7) % 8)
        self.right = (ty, (tx + 1) % 8)
        self.other = (ty, self.z * 2 + 1 - self.core)

    def along_y(self, step):
        return (((self.y + step) % 4) * 4 + self.x, self.tx)

    def along_x(self, step):
        return (self.y * 4 + (self.x + step) % 4, self.tx)

    def along_z(self, step):
        return (self.ty, ((self.z + step) % 4) * 2 + self.core)


def greet(devices):
    barrier = pltpu.get_barrier_semaphore()
    for device in devices:
        pl.semaphore_signal(barrier, inc=1, device_id=device, device_id_type=MESH)
    pl.semaphore_wait(barrier, len(devices))


class Copies:
    def __init__(self, send, receive):
        self.send, self.receive, self.used = send, receive, 0

    def make(self, source, target, device):
        copy = pltpu.make_async_remote_copy(
            src_ref=source,
            dst_ref=target,
            send_sem=self.send.at[self.used],
            recv_sem=self.receive.at[self.used],
            device_id=device,
            device_id_type=MESH,
        )
        self.used += 1
        return copy

    def start(self, source, target, device):
        copy = self.make(source, target, device)
        copy.start()
        return copy


def rows_of(zone, chunk):
    return slice(zone.start + chunk * CHUNK, zone.start + (chunk + 1) * CHUNK)


def extend_kernel(
    counts, positions, probe_far, tile, moduli_far,
    extended, ordered, table, updates, totals,
    moduli, near, probe, weighted, send, receive, arrived,
):
    here = Place()
    copies = Copies(send, receive)
    moduli_copy = pltpu.make_async_copy(moduli_far, moduli, arrived.at[0])
    moduli_copy.start()
    tile_copy = pltpu.make_async_copy(tile, extended.at[:, 0:TILE, 0:TILE], arrived.at[1])
    tile_copy.start()
    near_copy = pltpu.make_async_copy(tile, near.at[:, 0:TILE, 0:TILE], arrived.at[2])
    near_copy.start()
    probe_copy = pltpu.make_async_copy(probe_far, probe, arrived.at[3])
    probe_copy.start()
    greet([here.up, here.down, here.left, here.right])
    above, middle = [], []
    for chunk in range(CHUNKS):
        above.append(
            copies.start(
                tile.at[:, rows_of(Z0, chunk), Z0], extended.at[:, rows_of(Z2, chunk), Z0], here.up
            )
        )
    side = copies.start(tile.at[:, :, Z0], near.at[:, 0:TILE, Z2], here.left)
    for half in range(2):
        rows = slice(half * HALF, (half + 1) * HALF)
        low = slice(TILE + half * HALF, TILE + (half + 1) * HALF)
        middle.append(copies.start(tile.at[:, rows, Z1], extended.at[:, low, Z1], here.up))

    first = lax.broadcasted_iota(jnp.int32, (PATCH, PATCH), 0)
    second = lax.broadcasted_iota(jnp.int32, (PATCH, PATCH), 1)
    rows_order = (second == 4 * (first % QUARTER) + first // QUARTER).astype(F32).astype(BF16)
    cols_order = (first == 2 * (second % HALF) + second // HALF).astype(F32).astype(BF16)

    def reorder(slot, carry):
        block = moduli[slot]
        block = sum(dot(rows_order, part) for part in thirds(block))
        ordered[slot] = sum(dot(part, cols_order) for part in thirds(block))
        return carry

    write_tables(table)
    probe_copy.wait()
    write_weighted(weighted, probe)
    totals[...] = jnp.zeros_like(totals)
    near[:, TILE:, :] = jnp.zeros((2, HALF + 8, EXT), F32)
    moduli_copy.wait()
    lax.fori_loop(0, CAP, reorder, 0)
    corners = []
    for chunk in range(CHUNKS):
        above[chunk].wait_recv()
        corners.append(
            copies.start(
                extended.at[:, rows_of(Z2, chunk), Z0],
                extended.at[:, rows_of(Z2, chunk), Z2],
                here.left,
            )
        )
    near_copy.wait()
    side.wait_recv()
    extended[:, 0:TILE, Z2] = near[:, 0:TILE, Z2]

    slots = Slots(counts, positions)

    def turn(index):
        slot, present = slots.at(index)
        row = jnp.clip(slots.row(slot), 0, TILE - HALF)
        col = jnp.clip(slots.col(slot), 0, TILE - 1)
        keep = present.astype(F32)

        def deliver(plane, update):
            updates[index, plane] = update

        return visit(
            slot, row, col, keep, near, probe, weighted, ordered, table, totals, deliver
        )

    def two(pair, carry):
        @pl.when(pair == NEAR // 2)
        def _():
            middle[0].wait_recv()
            for copy in corners[: CHUNKS // 2]:
                copy.wait_recv()
            near[:, TILE : TILE + HALF, :] = extended[:, TILE : TILE + HALF, :]

        together([turn(2 * pair), turn(2 * pair + 1)])
        return carry

    lax.fori_loop(0, EARLY // 2, two, 0)
    tile_copy.wait()
    middle[1].wait_recv()
    for copy in corners[CHUNKS // 2 :]:
        copy.wait_recv()
    for copy in above + middle + corners + [side]:
        copy.wait_send()


def extend(counts, positions, probe, tile, moduli):
    copies = 2 * CHUNKS + 3
    return pl.pallas_call(
        extend_kernel,
        out_shape=(
            jax.ShapeDtypeStruct((2, EXT, EXT), F32),
            jax.ShapeDtypeStruct((CAP, PATCH, PATCH), F32),
            jax.ShapeDtypeStruct((16, PATCH, PATCH), BF16),
            jax.ShapeDtypeStruct((EARLY, 2, PATCH, PATCH), F32),
            jax.ShapeDtypeStruct((3, PATCH, PATCH), F32),
        ),
        in_specs=[SMEM, SMEM, HBM, HBM, HBM],
        out_specs=(VMEM,) * 5,
        scratch_shapes=[
            pltpu.VMEM((CAP, PATCH, PATCH), F32),
            pltpu.VMEM((2, TILE + HALF + 8, EXT), F32),
            pltpu.VMEM((2, PATCH, PATCH), F32),
            pltpu.VMEM((2, PATCH, PATCH), F32),
            pltpu.SemaphoreType.DMA((copies,)),
            pltpu.SemaphoreType.DMA((copies,)),
            pltpu.SemaphoreType.DMA((4,)),
        ],
        compiler_params=pltpu.CompilerParams(
            vmem_limit_bytes=30 * 2**20, collective_id=0, has_side_effects=True
        ),
        cost_estimate=pl.CostEstimate(
            flops=10**9, bytes_accessed=14 * 10**6, transcendentals=0
        ),
    )(counts, positions, probe, tile, moduli)


def is_inner(x):
    return (x == 1) | (x == 2)


class Reduction:
    def __init__(self, here, copies, totals, probe, probe_out, landed, held, pieces):
        self.pieces = pieces
        self.here, self.copies = here, copies
        self.totals, self.probe, self.probe_out = totals, probe, probe_out
        self.land_core, self.land_z, self.land_x, self.land_y = landed
        self.held_core, self.held_z, self.held_x = held
        self.in_flight = []
        self.sent = []

    def launch(self, source, target, device):
        self.in_flight.append(self.copies.start(source, target, device))

    def arrive(self):
        for copy in self.in_flight:
            copy.wait_recv()
        self.sent += self.in_flight
        self.in_flight = []

    def start(self):
        half = pl.ds(pl.multiple_of((1 - self.here.core) * HALF, HALF), HALF)
        self.launch(self.totals.at[:, half, :], self.land_core, self.here.other)

    def after_core(self):
        self.arrive()
        half = pl.ds(pl.multiple_of(self.here.core * HALF, HALF), HALF)
        self.held_core[...] = self.totals[:, half, :] + self.land_core[...]
        for step in (2, 1, 3):
            part = pl.ds(pl.multiple_of(((self.here.z + step) % 4) * 32, 32), 32)
            self.launch(
                self.held_core.at[:, part, :], self.land_z.at[step - 1], self.here.along_z(step)
            )

    def after_z(self):
        self.arrive()
        part = pl.ds(pl.multiple_of(self.here.z * 32, 32), 32)
        self.held_z[...] = (self.held_core[:, part, :] + self.land_z[0]) + (
            self.land_z[1] + self.land_z[2]
        )
        self.to_inner = []
        for step in (2, 1, 3):
            target = (self.here.x + step) % 4
            copy = self.copies.make(
                self.held_z.at[:, self.inner_rows(0, target), :],
                self.land_x.at[step - 1],
                self.here.along_x(step),
            )
            self.to_inner.append((copy, is_inner(target)))
            pl.when(is_inner(target))(copy.start)

    def inner_rows(self, start, x):
        rows = start + (x // 2) * 16
        return pl.ds(pl.multiple_of(rows, 16), 16)

    def after_x(self):
        self.across = [
            self.copies.make(
                self.held_x, self.land_y.at[self.here.y], self.here.along_y(step)
            )
            for step in (2, 1, 3)
        ]

        @pl.when(is_inner(self.here.x))
        def _():
            for copy, _ in self.to_inner:
                copy.wait_recv()
            part = self.inner_rows(0, self.here.x)
            self.held_x[...] = (self.held_z[:, part, :] + self.land_x[0]) + (
                self.land_x[1] + self.land_x[2]
            )
            for copy in self.across:
                copy.start()
            self.land_y[self.here.y] = self.held_x[...]

    def share(self, rows):
        start = self.here.core * HALF
        if rows < 128:
            start = start + self.here.z * 32
        return pl.ds(pl.multiple_of(start, rows), rows)

    def spread(self, rows, device):
        part = self.probe_out.at[:, self.share(rows), :]
        self.launch(part, part, device)

    def after_y(self):
        part = self.inner_rows(self.here.core * HALF + self.here.z * 32, self.here.x)
        updated = self.probe_out.at[:, part, :]
        self.from_inner = [
            self.copies.make(updated, updated, self.here.along_x(step)) for step in (2, 1, 3)
        ]

        @pl.when(is_inner(self.here.x))
        def _():
            for copy in self.across:
                copy.wait_recv()
            total = (self.land_y[0] + self.land_y[1]) + (self.land_y[2] + self.land_y[3])
            self.probe_out[:, part, :] = self.probe[:, part, :] + total[0:2] / (
                total[2:3] + tiny_value
            )
            for copy in self.from_inner:
                copy.start()

    def gather_x(self):
        for copy, step in zip(self.from_inner, (2, 1, 3)):
            sender = (self.here.x + 4 - step) % 4
            pl.when(is_inner(sender))(copy.wait_recv)
        for step in (2, 1, 3):
            self.spread(32, self.here.along_z(step))

    def gather_z(self):
        if not self.pieces:
            self.arrive()
            self.spread(128, self.here.other)
            return
        arriving, self.in_flight = self.in_flight, []
        self.spread(32, self.here.other)
        for copy, step in zip(arriving, (2, 1, 3)):
            copy.wait_recv()
            z = (self.here.z + 4 - step) % 4
            rows = pl.ds(pl.multiple_of(self.here.core * HALF + z * 32, 32), 32)
            part = self.probe_out.at[:, rows, :]
            self.launch(part, part, self.here.other)
        self.sent += arriving

    def finish(self):
        self.arrive()
        for copy in self.sent:
            copy.wait_send()
        for copy, started in self.to_inner:
            pl.when(started)(copy.wait_send)

        @pl.when(is_inner(self.here.x))
        def _():
            for copy in self.across + self.from_inner:
                copy.wait_send()


REDUCTION_COPIES = 1 + 3 + 3 + 3 + 3 + 3 + 4


def everyone(here):
    devices = [here.up, here.down, here.left, here.right, here.other]
    for step in range(1, 4):
        devices += [here.along_y(step), here.along_x(step), here.along_z(step)]
    return devices


def exchange_kernel(
    sums, extended, totals, probe, out, probe_out,
    from_side, from_up, from_down, from_right, top, bottom,
    land_core, land_z, land_x, land_y, held_core, held_z, held_x,
    send, receive,
):
    here = Place()
    copies = Copies(send, receive)
    reduction = Reduction(
        here, copies, totals, probe, probe_out,
        (land_core, land_z, land_x, land_y), (held_core, held_z, held_x), False,
    )
    greet(everyone(here))
    corners, outer, middle, last = [], [], [], []

    def shared(chunk):
        return (Z2, Z0, here.right, here.left) if chunk % 2 == 0 else (Z0, Z2, here.left, here.right)

    def send_corner(chunk):
        given, _, owner, _ = shared(chunk)
        pair = []
        for zone in (Z2, Z0):
            rows = rows_of(zone, chunk)
            pair.append(copies.start(sums.at[:, rows, given], from_side.at[:, rows, :], owner))
        corners.append(pair)

    def take_corner(chunk):
        rows, low = rows_of(Z0, chunk), rows_of(Z2, chunk)
        _, kept, _, _ = shared(chunk)
        for copy in corners[chunk]:
            copy.wait_recv()
        bottom[:, rows, :] = sums[:, low, kept] + from_side[:, low, :]
        top[:, rows, :] = sums[:, rows, kept] + from_side[:, rows, :]

    def send_outer(chunk):
        rows = rows_of(Z0, chunk)
        down = copies.start(bottom.at[:, rows, :], from_up.at[:, rows, Z0], here.down)
        up = copies.start(top.at[:, rows, :], from_down.at[:, rows, Z0], here.up)
        outer.append((down, up))

    def take_outer(chunk):
        rows, low = rows_of(Z0, chunk), rows_of(Z2, chunk)
        given, kept, _, partner = shared(chunk)
        down, up = outer[chunk]
        down.wait_recv()
        out[:, rows, kept] = extended[:, rows, kept] + (top[:, rows, :] + from_up[:, rows, Z0])
        last.append(copies.start(out.at[:, rows, kept], out.at[:, rows, given], partner))
        up.wait_recv()
        out[:, low, kept] = extended[:, low, kept] + (bottom[:, rows, :] + from_down[:, rows, Z0])
        last.append(copies.start(out.at[:, low, kept], out.at[:, low, given], partner))

    def send_middle(chunk):
        rows, low = rows_of(Z0, chunk), rows_of(Z2, chunk)
        down = copies.start(sums.at[:, low, Z1], from_up.at[:, rows, Z1], here.down)
        up = copies.start(sums.at[:, rows, Z1], from_down.at[:, rows, Z1], here.up)
        middle.append((down, up))

    def take_middle(chunk):
        rows, low = rows_of(Z0, chunk), rows_of(Z2, chunk)
        down, up = middle[chunk]
        down.wait_recv()
        out[:, rows, Z1] = extended[:, rows, Z1] + (sums[:, rows, Z1] + from_up[:, rows, Z1])
        up.wait_recv()
        out[:, low, Z1] = extended[:, low, Z1] + (sums[:, low, Z1] + from_down[:, rows, Z1])

    reduction.start()
    send_corner(0)
    send_corner(1)
    for chunk in range(3):
        send_middle(chunk)
    reduction.after_core()
    for chunk in range(2, CHUNKS):
        send_corner(chunk)
    side_left = copies.start(sums.at[:, Z1, Z0], from_right, here.left)
    side_right = copies.start(sums.at[:, Z1, Z2], from_side.at[:, Z1, :], here.right)
    out[:, Z1, Z1] = extended[:, Z1, Z1] + sums[:, Z1, Z1]
    take_corner(0)
    send_outer(0)
    reduction.after_z()
    take_corner(1)
    send_outer(1)
    reduction.after_x()
    take_outer(0)
    take_corner(2)
    send_outer(2)
    take_corner(3)
    reduction.after_y()
    send_outer(3)
    send_middle(3)
    take_outer(1)
    side_left.wait_recv()
    out[:, Z1, Z2] = extended[:, Z1, Z2] + (sums[:, Z1, Z2] + from_right[...])
    reduction.gather_x()
    for chunk in range(3):
        take_middle(chunk)
    take_outer(2)
    side_right.wait_recv()
    out[:, Z1, Z0] = extended[:, Z1, Z0] + (sums[:, Z1, Z0] + from_side[:, Z1, :])
    reduction.gather_z()
    take_outer(3)
    take_middle(3)
    reduction.finish()
    for pair in corners + outer + middle:
        for copy in pair:
            copy.wait_send()
    for copy in [side_left, side_right]:
        copy.wait_send()
    for copy in last:
        copy.wait()


def reduction_scratch():
    return [
        pltpu.VMEM((3, 128, PATCH), F32),
        pltpu.VMEM((3, 3, 32, PATCH), F32),
        pltpu.VMEM((3, 3, 16, PATCH), F32),
        pltpu.VMEM((4, 3, 16, PATCH), F32),
        pltpu.VMEM((3, 128, PATCH), F32),
        pltpu.VMEM((3, 32, PATCH), F32),
        pltpu.VMEM((3, 16, PATCH), F32),
    ]


def exchange(sums, extended, totals, probe):
    copies = REDUCTION_COPIES + 8 * CHUNKS + 2
    return pl.pallas_call(
        exchange_kernel,
        out_shape=(
            jax.ShapeDtypeStruct((2, EXT, EXT), F32),
            jax.ShapeDtypeStruct((2, PATCH, PATCH), F32),
        ),
        in_specs=[VMEM] * 4,
        out_specs=(VMEM, VMEM),
        scratch_shapes=[
            pltpu.VMEM((2, EXT, PATCH), F32),
            pltpu.VMEM((2, PATCH, TILE), F32),
            pltpu.VMEM((2, PATCH, TILE), F32),
            pltpu.VMEM((2, PATCH, PATCH), F32),
            pltpu.VMEM((2, PATCH, PATCH), F32),
            pltpu.VMEM((2, PATCH, PATCH), F32),
            *reduction_scratch(),
            pltpu.SemaphoreType.DMA((copies,)),
            pltpu.SemaphoreType.DMA((copies,)),
        ],
        compiler_params=pltpu.CompilerParams(
            vmem_limit_bytes=28 * 2**20, collective_id=1, has_side_effects=True
        ),
        cost_estimate=pl.CostEstimate(
            flops=10**9, bytes_accessed=14 * 10**6, transcendentals=0
        ),
    )(sums, extended, totals, probe)


def fold_kernel(
    sums, extended, totals, probe, out, probe_out,
    from_left, from_up, bottom,
    land_core, land_z, land_x, land_y, held_core, held_z, held_x,
    send, receive,
):
    here = Place()
    copies = Copies(send, receive)
    reduction = Reduction(
        here, copies, totals, probe, probe_out,
        (land_core, land_z, land_x, land_y), (held_core, held_z, held_x), True,
    )
    greet(everyone(here))
    corners, outer = [], []

    def send_corner(chunk):
        rows = rows_of(Z2, chunk)
        corners.append(copies.start(sums.at[:, rows, Z2], from_left.at[:, rows, :], here.right))

    def take_corner(chunk):
        rows, low = rows_of(Z0, chunk), rows_of(Z2, chunk)
        corners[chunk].wait_recv()
        bottom[:, rows, :] = sums[:, low, Z0] + from_left[:, low, :]

    def send_outer(chunk):
        rows = rows_of(Z0, chunk)
        outer.append(copies.start(bottom.at[:, rows, :], from_up.at[:, rows, Z0], here.down))

    reduction.start()
    send_corner(0)
    middle = copies.start(sums.at[:, Z2, Z1], from_up.at[:, :, Z1], here.down)
    reduction.after_core()
    for chunk in range(1, CHUNKS):
        send_corner(chunk)
    side = copies.start(sums.at[:, 0:TILE, Z2], from_left.at[:, 0:TILE, :], here.right)
    out[:, Z1, Z1] = extended[:, Z1, Z1] + sums[:, Z1, Z1]
    reduction.after_z()
    for chunk in range(2):
        take_corner(chunk)
        send_outer(chunk)
    middle.wait_recv()
    out[:, Z0, Z1] = extended[:, Z0, Z1] + (sums[:, Z0, Z1] + from_up[:, :, Z1])
    reduction.after_x()
    for chunk in range(2, CHUNKS):
        take_corner(chunk)
    reduction.after_y()
    for chunk in range(2, CHUNKS):
        send_outer(chunk)
    side.wait_recv()
    out[:, Z1, Z0] = extended[:, Z1, Z0] + (sums[:, Z1, Z0] + from_left[:, Z1, :])
    reduction.gather_x()
    reduction.gather_z()
    for chunk in range(CHUNKS):
        rows = rows_of(Z0, chunk)
        outer[chunk].wait_recv()
        out[:, rows, Z0] = extended[:, rows, Z0] + (
            (sums[:, rows, Z0] + from_left[:, rows, :]) + from_up[:, rows, Z0]
        )
    reduction.finish()
    for copy in corners + outer + [middle, side]:
        copy.wait_send()


def fold(sums, extended, totals, probe):
    copies = REDUCTION_COPIES + 2 * CHUNKS + 2
    return pl.pallas_call(
        fold_kernel,
        out_shape=(
            jax.ShapeDtypeStruct((2, TILE, TILE), F32),
            jax.ShapeDtypeStruct((2, PATCH, PATCH), F32),
        ),
        in_specs=[VMEM] * 4,
        out_specs=(VMEM, VMEM),
        scratch_shapes=[
            pltpu.VMEM((2, EXT, PATCH), F32),
            pltpu.VMEM((2, PATCH, TILE), F32),
            pltpu.VMEM((2, PATCH, PATCH), F32),
            *reduction_scratch(),
            pltpu.SemaphoreType.DMA((copies,)),
            pltpu.SemaphoreType.DMA((copies,)),
        ],
        compiler_params=pltpu.CompilerParams(
            vmem_limit_bytes=22 * 2**20, collective_id=2, has_side_effects=True
        ),
        cost_estimate=pl.CostEstimate(
            flops=10**9, bytes_accessed=14 * 10**6, transcendentals=0
        ),
    )(sums, extended, totals, probe)


def publish_kernel(tile, probe, tile_out, probe_out, done):
    copies = [
        pltpu.make_async_copy(tile, tile_out, done.at[0]),
        pltpu.make_async_copy(probe, probe_out, done.at[1]),
    ]
    for copy in copies:
        copy.start()
    for copy in copies:
        copy.wait()


def publish(tile, probe):
    return pl.pallas_call(
        publish_kernel,
        out_shape=(
            jax.ShapeDtypeStruct(tile.shape, tile.dtype),
            jax.ShapeDtypeStruct(probe.shape, probe.dtype),
        ),
        in_specs=[VMEM, VMEM],
        out_specs=(HBM, HBM),
        scratch_shapes=[pltpu.SemaphoreType.DMA((2,))],
        compiler_params=pltpu.CompilerParams(vmem_limit_bytes=8 * 2**20),
    )(tile, probe)


def shards(object_field, probe, moduli, positions, counts):
    positions = positions.T
    extended, ordered, table, updates, totals = extend(
        counts,
        positions,
        pltpu.with_memory_space_constraint(probe, pltpu.HBM),
        pltpu.with_memory_space_constraint(object_field, pltpu.HBM),
        pltpu.with_memory_space_constraint(moduli, pltpu.HBM),
    )
    sums, totals = run_slots(
        counts, positions, extended, probe, ordered, table, updates, totals
    )
    extended, probe = exchange(sums, extended, totals, probe)
    sums, totals = run_slots(counts, positions, extended, probe, ordered, table)
    return publish(*fold(sums, extended, totals, probe))


def solution(mesh):
    return jax.shard_map(
        shards,
        mesh=mesh,
        in_specs=(
            P(None, "ty", "tx"),
            P(),
            P(("ty", "tx"), None, None),
            P(("ty", "tx"), None),
            P(),
        ),
        out_specs=(P(None, "ty", "tx"), P()),
        check_vma=False,
    )
```
